32 devices in a mesh: rows: 8 (over z, x), pre: 4 (over y, core).
Axes of the slice: x: 2, y: 2, z: 4, core: 2. Of those that a mesh axis runs over, the one named last changes fastest.
Arguments:
- tokens: bfloat16 [32, 1024, 1024], P(('rows', 'pre')), may hold values from -6 to 6
- seg_ids: int32 [32, 1024], P(('rows', 'pre')), may hold values from 0 to 7, never falling along the last dimension, each value on 1 to 256 neighbouring positions
- valid: int32 [32, 1024], P(('rows', 'pre')), may hold values from 0 to 1, as said below
- out_grad: bfloat16 [32, 1024, 1024], P(('rows', 'pre')), may hold values from -6 to 6
- ln1_gain: bfloat16 [1024], replicated, may hold values from 0.25 to 1.75
- ln1_bias: bfloat16 [1024], replicated, may hold values from -1.25 to 1.25
- qkv_weight: bfloat16 [1024, 3072], P(('rows', 'pre')), may hold values from -0.1875 to 0.1875
- qkv_bias: bfloat16 [3072], replicated, may hold values from -1.75 to 1.75
- proj_weight: bfloat16 [1024, 1024], P(('rows', 'pre')), may hold values from -0.5 to 0.5
- proj_bias: bfloat16 [1024], replicated, may hold values from -1.25 to 1.25
- ln2_gain: bfloat16 [1024], replicated, may hold values from 0.25 to 1.75
- ln2_bias: bfloat16 [1024], replicated, may hold values from -1.25 to 1.25
- fc_weight: bfloat16 [1024, 4096], P(('rows', 'pre')), may hold values from -0.1875 to 0.1875
- fc_bias: bfloat16 [4096], replicated, may hold values from -3 to 3
- out_weight: bfloat16 [4096, 1024], P(('rows', 'pre')), may hold values from -0.09375 to 0.09375
- out_bias: bfloat16 [1024], replicated, may hold values from -1.75 to 1.75
- prefix_emb: bfloat16 [10, 1024], replicated, may hold values from -6 to 6
- rep_weight1: bfloat16 [1024, 800], replicated, may hold values from -0.1875 to 0.1875
- rep_bias1: bfloat16 [800], replicated, may hold values from -3 to 3
- rep_weight2: bfloat16 [800, 2048], P(None, 'pre'), may hold values from -0.4375 to 0.4375
- rep_bias2: bfloat16 [2048], P('pre'), may hold values from -3 to 3
Outputs:
- output: bfloat16 [32, 1024, 1024], P(('rows', 'pre'))
- in_grad: bfloat16 [32, 1024, 1024], P(('rows', 'pre'))
- emb_grad: float32 [10, 1024], replicated
- rep_weight1_grad: float32 [1024, 800], replicated
- rep_bias1_grad: float32 [800], replicated
- rep_weight2_grad: float32 [800, 2048], P(None, 'pre')
- rep_bias2_grad: float32 [2048], P('pre')
The draws below stay inside these ranges and needn't reach their ends.
Inputs may be any that keep to these rules, and one draw needn't show every extreme that they name: `seg_ids`: ids never fall along a row; each id covers 1 to 256 positions. `valid`: in each row, 1 on a leading run of 512 positions or more and 0 on the rest; every row ends in at least one 0.
All inputs are finite; a program needn't handle non-finite values.
Results may differ from the reference program's by a relative error of at most 0.019.
Values may be sent and summed in bfloat16 or wider, within the bound.
No kernel may reach another device: no remote copies, remote signals or barrier semaphores. Data moves between devices by JAX's collectives and lax.ppermute only.
A program may use at most 320 MiB of HBM per device.

```python
import math
import jax
import jax.numpy as jnp
import numpy as np
from jax import lax

D = 1024
H = 16
HD = 64
FF = 4096
MID = 800
P_SIZE = 10
LEN = 1024
SEQS = 32


def draw_valid(key, part):
    key = jax.random.fold_in(key, 7)
    row_lengths = jax.random.randint(key, (SEQS, 1), LEN // 2, LEN)
    positions = jnp.arange(LEN)[None, :]
    return (positions < row_lengths).astype(jnp.int32)


def block_levels(key, shape, cuts, low, largest):
    level = 1.0
    for axis_at, parts in cuts:
        steps = jax.random.uniform(jax.random.fold_in(jax.random.fold_in(key, 6), axis_at), (parts,), jnp.float32, low / len(cuts), largest / len(cuts))
        level = level * jnp.repeat(jnp.exp(steps), shape[axis_at] // parts).reshape((-1,) + (1,) * (len(shape) - 1 - axis_at))
    return level


def split_up(count, total, limit, lean):
    weights = [(1 << 20) // math.isqrt(standing ** lean) + 1 for standing in range(2, count + 1)]
    spare, holding = total - limit - (count - 1), [1] * (count - 1)
    while spare > 0:
        free = [i for i in range(count - 1) if holding[i] < limit]
        pool, left = sum([weights[i] for i in free]), spare
        for i in free:
            extra = min(limit - holding[i], max(1, left * weights[i] // pool), spare)
            holding[i] = holding[i] + extra
            spare = spare - extra
    return np.array([limit] + holding)


def uneven_parts(rng, amount, total, limit, slope):
    if amount == 2:
        one = jax.random.randint(rng, (), max(1, total - limit), min(limit, total - 1) + 1)
        return jnp.stack([one, total - one])
    lengths = jnp.asarray(split_up(amount, total, limit, slope), jnp.int32)
    pairs = (amount - 1) // 2
    source_of, taker = lengths[1:1 + 2 * pairs:2], lengths[2:2 + 2 * pairs:2]
    slack = jnp.minimum(source_of - 1, limit - taker)
    passed = jax.random.randint(jax.random.fold_in(rng, 1), (pairs,), 0, 1 << 20) % (slack + 1)
    lengths = lengths.at[1:1 + 2 * pairs:2].set(source_of - passed).at[2:2 + 2 * pairs:2].set(taker + passed)
    return lengths[jax.random.permutation(jax.random.fold_in(rng, 2), amount)]


def scatter_about(stream_key, extent, scale, limit, pieces=(), kind=jnp.bfloat16):
    factor_of = block_levels(stream_key, extent, pieces, -0.22, 0.18) if pieces else 1.0
    result = jax.random.normal(stream_key, extent, jnp.float32) * scale * factor_of
    return jnp.minimum(jnp.maximum(result, -limit), limit).astype(kind)


def setup_inputs(seed: int = 0) -> dict:
    streams_of = jax.random.split(jax.random.key(seed), 22)
    tokens = scatter_about(streams_of[0], (SEQS, LEN, D), 1.0, 6.0, ((0, 32),))
    seg_ids = jax.vmap(lambda own: jnp.searchsorted(jnp.cumsum(uneven_parts(own, 8, LEN, LEN // 4, 2)), jnp.arange(LEN), side="right"))(jax.random.split(streams_of[1], SEQS)).reshape((SEQS, LEN)).astype(jnp.int32)
    valid = draw_valid(jax.random.fold_in(streams_of[21], 71), 0)
    out_grad = scatter_about(streams_of[3], (SEQS, LEN, D), 1.0, 6.0, ((0, 32),))
    ln1_gain = jnp.clip(1.0 + 0.15 * jax.random.normal(streams_of[4], (D,), jnp.float32), 0.25, 1.75).astype(jnp.bfloat16)
    ln1_bias = scatter_about(streams_of[5], (D,), 0.2, 1.25)
    qkv_weight = scatter_about(streams_of[6], (D, 3 * D), D ** -0.5, 0.1875, ((0, 32),))
    qkv_bias = scatter_about(streams_of[7], (3 * D,), 0.3, 1.75)
    proj_weight = scatter_about(streams_of[8], (D, D), (D // 8) ** -0.5, 0.5, ((0, 32),))
    proj_bias = scatter_about(streams_of[9], (D,), 0.2, 1.25)
    ln2_gain = jnp.clip(1.0 + 0.15 * jax.random.normal(streams_of[10], (D,), jnp.float32), 0.25, 1.75).astype(jnp.bfloat16)
    ln2_bias = scatter_about(streams_of[11], (D,), 0.2, 1.25)
    fc_weight = scatter_about(streams_of[12], (D, FF), D ** -0.5, 0.1875, ((0, 32),))
    fc_bias = scatter_about(streams_of[13], (FF,), 0.5, 3.0)
    out_weight = scatter_about(streams_of[14], (FF, D), FF ** -0.5, 0.09375, ((0, 32),))
    out_bias = scatter_about(streams_of[15], (D,), 0.3, 1.75)
    prefix_emb = scatter_about(streams_of[16], (P_SIZE, D), 1.0, 6.0)
    rep_weight1 = scatter_about(streams_of[17], (D, MID), D ** -0.5, 0.1875)
    rep_bias1 = scatter_about(streams_of[18], (MID,), 0.5, 3.0)
    rep_weight2 = scatter_about(streams_of[19], (MID, 2 * D), (MID // 4) ** -0.5, 0.4375, ((1, 4),))
    rep_bias2 = scatter_about(streams_of[20], (2 * D,), 0.5, 3.0, ((0, 4),))
    return {"tokens": tokens, "seg_ids": seg_ids, "valid": valid, "out_grad": out_grad, "ln1_gain": ln1_gain, "ln1_bias": ln1_bias, "qkv_weight": qkv_weight, "qkv_bias": qkv_bias, "proj_weight": proj_weight, "proj_bias": proj_bias, "ln2_gain": ln2_gain, "ln2_bias": ln2_bias, "fc_weight": fc_weight, "fc_bias": fc_bias, "out_weight": out_weight, "out_bias": out_bias, "prefix_emb": prefix_emb, "rep_weight1": rep_weight1, "rep_bias1": rep_bias1, "rep_weight2": rep_weight2, "rep_bias2": rep_bias2}


@jax.custom_vjp
def low(v):
    return lax.optimization_barrier(v.astype(jnp.bfloat16)).astype(jnp.float32)

@jax.custom_vjp
def low_back(v):
    return v

def low_keep(v):
    return (low(v), None)

def low_pass(kept, grad):
    return (grad,)

def back_keep(v):
    return (v, None)

def back_low(kept, grad):
    return (low(grad),)
low.defvjp(low_keep, low_pass)
low_back.defvjp(back_keep, back_low)
NEG = -1e+30
EPS = 1e-05

def widen(array):
    return array.astype(jnp.float32)

def mat(left, right):
    return jnp.dot(left, right, precision=lax.Precision.HIGHEST)

def norm_rows(values, gain, shift):
    center = values - lax.optimization_barrier(jnp.mean(values, axis=-1, keepdims=True))
    spread = lax.optimization_barrier(jnp.mean(center * center, axis=-1, keepdims=True))
    return center * lax.rsqrt(spread + EPS) * gain + shift

def attend(queries, keys, values, pkeys, pvalues, seg_row, valid_row):
    length = queries.shape[0]
    scale = float(HD) ** (-0.5)
    hp = lax.Precision.HIGHEST
    q_heads = queries.reshape(length, H, HD)
    k_heads = keys.reshape(length, H, HD)
    v_heads = values.reshape(length, H, HD)
    pk_heads = pkeys.reshape(-1, H, HD)
    pv_heads = pvalues.reshape(-1, H, HD)
    positions = jnp.arange(length)
    allowed = (seg_row[:, None] == seg_row[None, :]) & (positions[None, :] <= positions[:, None]) & (valid_row[None, :] > 0)
    scores = low_back(jnp.einsum('qhd,khd->hqk', q_heads, k_heads, precision=hp) * scale)
    scores = jnp.where(allowed[None], scores, NEG)
    prefix_scores = low_back(jnp.einsum('qhd,phd->hqp', q_heads, pk_heads, precision=hp) * scale)
    highest = jnp.maximum(lax.optimization_barrier(jnp.max(scores, axis=-1)), lax.optimization_barrier(jnp.max(prefix_scores, axis=-1)))[..., None]
    exp_scores = jnp.exp(scores - highest)
    exp_prefix = jnp.exp(prefix_scores - highest)
    row_total = lax.optimization_barrier(jnp.sum(exp_scores, axis=-1, keepdims=True)) + lax.optimization_barrier(jnp.sum(exp_prefix, axis=-1, keepdims=True))
    attn_probs = low(exp_scores / row_total)
    prefix_probs = low(exp_prefix / row_total)
    attn_mix = jnp.einsum('hqk,khd->qhd', attn_probs, v_heads, precision=hp) + jnp.einsum('hqp,phd->qhd', prefix_probs, pv_heads, precision=hp)
    return attn_mix.reshape(length, H * HD)

def layer(inputs, seg_row, valid_row, pkeys, pvalues, weights):
    g_one, c_one, w_qkv, b_qkv, w_proj, b_proj, g_two, c_two, w_fc, b_fc, w_out, b_out = weights
    normed1 = low(norm_rows(inputs, g_one, c_one))
    qkv = low_back(low(mat(normed1, w_qkv) + b_qkv))
    attn = low_back(low(attend(qkv[:, :D], qkv[:, D:2 * D], qkv[:, 2 * D:], pkeys, pvalues, seg_row, valid_row)))
    middle = inputs + low_back(mat(attn, w_proj) + b_proj)
    normed2 = low(norm_rows(middle, g_two, c_two))
    pre_act = low_back(mat(normed2, w_fc) + b_fc)
    act = low(jax.nn.gelu(pre_act, approximate=True))
    return middle + low_back(mat(act, w_out) + b_out)

def reference(tokens, seg_ids, valid, out_grad, ln1_gain, ln1_bias, qkv_weight, qkv_bias, proj_weight, proj_bias, ln2_gain, ln2_bias, fc_weight, fc_bias, out_weight, out_bias, prefix_emb, rep_weight1, rep_bias1, rep_weight2, rep_bias2):
    weights = tuple((widen(item) for item in (ln1_gain, ln1_bias, qkv_weight, qkv_bias, proj_weight, proj_bias, ln2_gain, ln2_bias, fc_weight, fc_bias, out_weight, out_bias)))

    def forward(token_rows, embedding, w_first, b_first, w_second, b_second):
        pre_hidden = low_back(mat(embedding, w_first) + b_first)
        hidden_low = low(jnp.tanh(pre_hidden))
        prefix_kv = low_back(low(mat(hidden_low, w_second) + b_second))
        pkeys = prefix_kv[:, :D]
        pvalues = prefix_kv[:, D:]

        def one_row(item):
            return layer(item[0], item[1], item[2], pkeys, pvalues, weights)
        return lax.map(jax.checkpoint(one_row), (token_rows, seg_ids, valid))
    output, pull_back = jax.vjp(forward, widen(tokens), widen(prefix_emb), widen(rep_weight1), widen(rep_bias1), widen(rep_weight2), widen(rep_bias2))
    grads = pull_back(widen(out_grad))
    return (output.astype(jnp.bfloat16), grads[0].astype(jnp.bfloat16), grads[1], grads[2], grads[3], grads[4], grads[5])
```

```python
import functools

import jax
import jax.numpy as jnp
from jax import lax
from jax.experimental import pallas as pl
from jax.experimental.pallas import tpu as pltpu
from jax.sharding import PartitionSpec as P

f32 = jnp.float32
bf16 = jnp.bfloat16
ALL = ("rows", "pre")
NEG = -1e30
EPS = 1e-05
HD = 64
SPAN = 256
BQ = SPAN
PW = 16
LANES = 256
HEADS = LANES // HD
GROUPS = 2
CHUNKS = 4
BM = 256

NN = (((1,), (0,)), ((), ()))
NT = (((1,), (1,)), ((), ()))
TN = (((0,), (0,)), ((), ()))


def dot(a, b, dims=NN):
    return lax.dot_general(a, b, dims, preferred_element_type=f32)


def params():
    return pltpu.CompilerParams(vmem_limit_bytes=56 << 20)


def cost(flops, moved):
    return pl.CostEstimate(flops=int(flops), bytes_accessed=int(moved), transcendentals=0)


class Weight:
    def __init__(self, arrays, block, table, rows):
        self.arrays, self.block, self.table, self.rows = arrays, block, table, rows
        self.cols = arrays[0].shape[1]

    def specs(self):
        return [pl.BlockSpec(memory_space=pltpu.SMEM)] + [
            pl.BlockSpec(memory_space=pl.ANY) for _ in self.arrays
        ]

    def args(self):
        return [self.table] + list(self.arrays)

    def count(self):
        return 1 + len(self.arrays)

    def scratch(self):
        return [pltpu.VMEM((self.rows, self.cols), bf16), pltpu.SemaphoreType.DMA]


def start_load(refs, block, whole, sem):
    table, arrays = refs[0], refs[1:]
    at = 0
    for ref in arrays:
        for k in range(ref.shape[0] // block):
            first = pl.multiple_of(table[at], block)
            pltpu.make_async_copy(
                ref.at[pl.ds(k * block, block)], whole.at[pl.ds(first, block)], sem
            ).start()
            at += 1


def wait_load(whole, sem):
    pltpu.make_async_copy(whole, whole, sem).wait()


def split(refs, *counts):
    out, at = [], 0
    for n in counts:
        out.append(refs[at : at + n])
        at += n
    return out


def norm(values):
    center = values - jnp.mean(values, axis=-1, keepdims=True)
    rate = lax.rsqrt(jnp.mean(center * center, axis=-1, keepdims=True) + EPS)
    return center * rate, rate


def norm_back(values, gain, grad):
    n, rate = norm(values)
    w = grad * gain
    return rate * (
        w - jnp.mean(w, axis=-1, keepdims=True) - n * jnp.mean(w * n, axis=-1, keepdims=True)
    )


def rows_spec(cols, at=0):
    return pl.BlockSpec((BM, cols), lambda i: (i, at))


def whole_spec(shape):
    return pl.BlockSpec(shape, lambda i: (0,) * len(shape))


def project_kernel(w, *refs):
    x_ref, b_ref, wr, (o_ref, whole, sem) = *refs[:2], refs[2 : 2 + w.count()], refs[2 + w.count() :]

    @pl.when(pl.program_id(0) == 0)
    def _():
        start_load(wr, w.block, whole, sem)
        wait_load(whole, sem)

    o_ref[...] = (dot(x_ref[...], whole[...]) + b_ref[...]).astype(bf16)


def project(x, w, bias):
    length = x.shape[0]
    return pl.pallas_call(
        functools.partial(project_kernel, w),
        grid=(length // BM,),
        in_specs=[rows_spec(w.rows), whole_spec((1, w.cols))] + w.specs(),
        out_specs=rows_spec(w.cols),
        out_shape=jax.ShapeDtypeStruct((length, w.cols), bf16),
        scratch_shapes=w.scratch(),
        compiler_params=params(),
        cost_estimate=cost(2 * length * w.rows * w.cols, 2 * w.rows * w.cols + 4 * length * w.cols),
        name="project",
    )(x, bias, *w.args())


def middle_kernel(w, *refs):
    head = refs[: GROUPS + 4]
    parts, (x_ref, b_ref, g_ref, s_ref) = head[:GROUPS], head[GROUPS:]
    wr = refs[GROUPS + 4 : GROUPS + 4 + w.count()]
    mid_ref, n_ref, whole, sem = refs[GROUPS + 4 + w.count() :]

    @pl.when(pl.program_id(0) == 0)
    def _():
        start_load(wr, w.block, whole, sem)
        wait_load(whole, sem)

    attn = jnp.concatenate([p[...] for p in parts], 1)
    mid = x_ref[...].astype(f32) + (dot(attn, whole[...]) + b_ref[...])
    mid_ref[...] = mid
    n_ref[...] = (norm(mid)[0] * g_ref[...] + s_ref[...]).astype(bf16)


def middle_block(parts, x, w, bias, gain, shift):
    length, model = x.shape
    vec = whole_spec((1, model))
    return pl.pallas_call(
        functools.partial(middle_kernel, w),
        grid=(length // BM,),
        in_specs=[rows_spec(p.shape[1]) for p in parts] + [rows_spec(model), vec, vec, vec] + w.specs(),
        out_specs=[rows_spec(model)] * 2,
        out_shape=[
            jax.ShapeDtypeStruct((length, model), f32),
            jax.ShapeDtypeStruct((length, model), bf16),
        ],
        scratch_shapes=w.scratch(),
        compiler_params=params(),
        cost_estimate=cost(2 * length * w.rows * w.cols, 12 * length * model),
        name="middle_block",
    )(*parts, x, bias, gain, shift, *w.args())


def gelu_both(v):
    c, a = 0.7978845608, 0.044715
    sq = v * v
    t = jnp.tanh(v * (c + (c * a) * sq))
    half = 0.5 + 0.5 * t
    act = v * half
    slope = half + (0.5 * v) * (1.0 - t * t) * (c + (3.0 * c * a) * sq)
    return act, slope


def expand_kernel(w, *refs):
    x_ref, b_ref, wr = refs[0], refs[1], refs[2 : 2 + w.count()]
    act_ref, slope_ref, whole, sem = refs[2 + w.count() :]

    @pl.when(pl.program_id(0) == 0)
    def _():
        start_load(wr, w.block, whole, sem)
        wait_load(whole, sem)

    step = 512
    for j in range(0, w.cols, step):
        at = pl.ds(j, step)
        act, slope = gelu_both(dot(x_ref[...], whole[:, at]) + b_ref[:, at])
        act_ref[:, at] = act.astype(bf16)
        slope_ref[:, at] = slope.astype(bf16)


def expand(x, w, bias):
    length = x.shape[0]
    return pl.pallas_call(
        functools.partial(expand_kernel, w),
        grid=(length // BM,),
        in_specs=[rows_spec(w.rows), whole_spec((1, w.cols))] + w.specs(),
        out_specs=[rows_spec(w.cols)] * 2,
        out_shape=[jax.ShapeDtypeStruct((length, w.cols), bf16)] * 2,
        scratch_shapes=w.scratch(),
        compiler_params=params(),
        cost_estimate=cost(2 * length * w.rows * w.cols, 2 * w.rows * w.cols + 4 * length * w.cols),
        name="expand",
    )(x, bias, *w.args())


def contract_kernel(w_in, w_out, w_proj, chunk, first, last, *refs):
    refs = list(refs)
    og_ref, act_ref, slope_ref, mid_ref = refs[:4]
    refs = refs[4:]
    if first:
        ob_ref = refs.pop(0)
    else:
        out_in, gn_in = refs.pop(0), refs.pop(0)
    if last:
        g_ref = refs.pop(0)
    wi, refs = refs[: w_in.count()], refs[w_in.count() :]
    wo, refs = refs[: w_out.count()], refs[w_out.count() :]
    if last:
        wp, refs = refs[: w_proj.count()], refs[w_proj.count() :]
        out_ref, gm_ref, ga_ref = refs[:3]
        refs = refs[3:]
    else:
        out_ref, gn_ref = refs[:2]
        refs = refs[2:]
    fc, fc_sem, ow, ow_sem = refs[:4]
    width = w_out.rows

    @pl.when(pl.program_id(0) == 0)
    def _():
        start_load(wo, w_out.block, ow, ow_sem)
        table, arrays = wi[0], wi[1:]
        at = 0
        for ref in arrays:
            for k in range(ref.shape[0] // w_in.block):
                row = pl.multiple_of(table[at], w_in.block)
                pltpu.make_async_copy(
                    ref.at[pl.ds(k * w_in.block, w_in.block), pl.ds(chunk * width, width)],
                    fc.at[pl.ds(row, w_in.block)],
                    fc_sem,
                ).start()
                at += 1
        if last:
            start_load(wp, w_proj.block, refs[4], refs[5])
            wait_load(refs[4], refs[5])
        wait_load(ow, ow_sem)
        wait_load(fc, fc_sem)

    og = og_ref[...]
    grad_act = dot(og, ow[...], NT)
    grad_pre = (grad_act * slope_ref[...].astype(f32)).astype(bf16)
    gn = dot(grad_pre, fc[...], NT)
    out = dot(act_ref[...], ow[...])
    if first:
        out = out + (mid_ref[...] + ob_ref[...])
    else:
        out = out + out_in[...]
        gn = gn + gn_in[...]
    out_ref[...] = out.astype(out_ref.dtype)
    if last:
        gm = og.astype(f32) + norm_back(mid_ref[...], g_ref[...], gn)
        gm_ref[...] = gm
        ga_ref[...] = dot(gm.astype(bf16), refs[4][...], NT).astype(bf16)
    else:
        gn_ref[...] = gn


def contract(chunk, og, act, slope, mid, out_bias, gain, so_far, w_in, w_out, w_proj):
    length, model = og.shape
    first, last = chunk == 0, chunk == CHUNKS - 1
    width = w_out.rows
    vec = whole_spec((1, model))
    full = rows_spec(model)
    specs = [full, rows_spec(width, chunk), rows_spec(width, chunk), full]
    args = [og, act, slope, mid]
    if first:
        specs, args = specs + [vec], args + [out_bias]
    else:
        specs, args = specs + [full, full], args + list(so_far)
    if last:
        specs, args = specs + [vec], args + [gain]
    specs, args = specs + w_in.specs() + w_out.specs(), args + w_in.args() + w_out.args()
    scratch = [pltpu.VMEM((w_in.rows, width), bf16), pltpu.SemaphoreType.DMA] + w_out.scratch()
    if last:
        specs, args = specs + w_proj.specs(), args + w_proj.args()
        scratch = scratch + w_proj.scratch()
        outs = [bf16, f32, bf16]
    else:
        outs = [f32, f32]
    return pl.pallas_call(
        functools.partial(contract_kernel, w_in, w_out, w_proj, chunk, first, last),
        grid=(length // BM,),
        in_specs=specs,
        out_specs=[full] * len(outs),
        out_shape=[jax.ShapeDtypeStruct((length, model), t) for t in outs],
        scratch_shapes=scratch,
        compiler_params=params(),
        cost_estimate=cost(6 * length * width * model, 24 * length * model),
        name="contract",
    )(*args)


def finish_kernel(ws, *refs):
    n = 3 * GROUPS
    parts, refs = refs[:n], refs[n:]
    (x_ref, gm_ref, g_ref), refs = refs[:3], refs[3:]
    wr = []
    for w in ws:
        wr.append(refs[: w.count()])
        refs = refs[w.count() :]
    o_ref, scratch = refs[0], refs[1:]

    @pl.when(pl.program_id(0) == 0)
    def _():
        for i, w in enumerate(ws):
            start_load(wr[i], w.block, scratch[2 * i], scratch[2 * i + 1])
        for i in range(len(ws)):
            wait_load(scratch[2 * i], scratch[2 * i + 1])

    gn = 0.0
    for i in range(GROUPS):
        part = jnp.concatenate([r[...] for r in parts[3 * i : 3 * i + 3]], 1)
        gn = gn + dot(part, scratch[2 * i][...], NT)
    o_ref[...] = (gm_ref[...] + norm_back(x_ref[...].astype(f32), g_ref[...], gn)).astype(bf16)


def finish(parts, x, gm, gain, ws):
    length, model = x.shape
    full = rows_spec(model)
    return pl.pallas_call(
        functools.partial(finish_kernel, ws),
        grid=(length // BM,),
        in_specs=[rows_spec(p.shape[1]) for p in parts]
        + [full, full, whole_spec((1, model))]
        + sum([w.specs() for w in ws], []),
        out_specs=full,
        out_shape=jax.ShapeDtypeStruct((length, model), bf16),
        scratch_shapes=sum([w.scratch() for w in ws], []),
        compiler_params=params(),
        cost_estimate=cost(6 * length * model * model, 16 * length * model),
        name="finish",
    )(*parts, x, gm, gain, *sum([w.args() for w in ws], []))


def spans(length):
    out, at = [], 0
    for first in range(0, length, BQ):
        key = max(0, first - SPAN)
        keys = PW + first + BQ - key
        out.append((first, key, keys, at))
        at += keys
    return out, at


def mask_bias(seg, valid, prefix):
    length = seg.shape[0]
    place = jnp.arange(length)
    parts = []
    for first, key, keys, _ in spans(length)[0]:
        ks, qs = slice(key, key + keys - PW), slice(first, first + BQ)
        seen = (
            (seg[ks][:, None] == seg[qs][None, :])
            & (place[ks][:, None] <= place[qs][None, :])
            & (valid[ks][:, None] > 0)
        )
        pad = jnp.broadcast_to(jnp.arange(PW)[:, None] < prefix, (PW, BQ))
        parts += [pad, seen]
    return jnp.where(jnp.concatenate(parts, 0), 0.0, NEG).astype(f32)


def of_head(shape, head):
    lane = lax.broadcasted_iota(jnp.int32, shape, 1)
    return (lane >= HD * head) & (lane < HD * (head + 1))


def stack_heads(q):
    return jnp.concatenate([jnp.where(of_head(q.shape, h), q, jnp.zeros_like(q)) for h in range(HEADS)], 0)


def pick_heads(o):
    out = o[:BQ]
    for h in range(1, HEADS):
        out = jnp.where(of_head(out.shape, h), o[h * BQ : (h + 1) * BQ], out)
    return out


def attend_kernel(length, q_ref, k_ref, v_ref, pk_ref, pv_ref, bias_ref, o_ref, p_ref):
    plan = spans(length)[0]

    def score(i):
        first, key, keys, _ = plan[i]
        q = q_ref[pl.ds(first, BQ), :] * jnp.asarray(HD**-0.5, bf16)
        ks = jnp.concatenate([pk_ref[...], k_ref[pl.ds(key, keys - PW), :]], 0)
        return dot(ks, stack_heads(q), NT)

    def soft(i, s):
        _, _, keys, at = plan[i]
        s = s + jnp.concatenate([bias_ref[pl.ds(at, keys), :]] * HEADS, 1)
        e = jnp.exp(s - jnp.max(s, axis=0, keepdims=True))
        probs = (e * (1.0 / jnp.sum(e, axis=0, keepdims=True))).astype(bf16)
        p_ref[0, pl.ds(at, keys), :] = probs
        return probs

    def mix(i, probs):
        first, key, keys, _ = plan[i]
        vs = jnp.concatenate([pv_ref[...], v_ref[pl.ds(key, keys - PW), :]], 0)
        o_ref[pl.ds(first, BQ), :] = pick_heads(dot(probs, vs, TN)).astype(bf16)

    n = len(plan)
    s, held = score(0), None
    for i in range(n):
        later = score(i + 1) if i + 1 < n else None
        probs = soft(i, s)
        if held is not None:
            mix(i - 1, held)
        s, held = later, probs
    mix(n - 1, held)


def attend(qkv, pk, pv, bias):
    length = qkv.shape[0]
    steps = qkv.shape[1] // 3 // LANES
    total = spans(length)[1]

    def col(at):
        return pl.BlockSpec((length, LANES), lambda i: (0, at * steps + i))

    small = pl.BlockSpec((PW, LANES), lambda i: (0, i))
    return pl.pallas_call(
        functools.partial(attend_kernel, length),
        grid=(steps,),
        in_specs=[col(0), col(1), col(2), small, small, whole_spec((total, BQ))],
        out_specs=[col(0), pl.BlockSpec((1, total, HEADS * BQ), lambda i: (i, 0, 0))],
        out_shape=[
            jax.ShapeDtypeStruct((length, steps * LANES), bf16),
            jax.ShapeDtypeStruct((steps, total, HEADS * BQ), bf16),
        ],
        compiler_params=params(),
        cost_estimate=cost(steps * 5e9, steps * 6e6),
        name="attend",
    )(qkv, qkv, qkv, pk, pv, bias)


def attend_back_kernel(
    length, q_ref, k_ref, v_ref, pk_ref, pv_ref, p_ref, do_ref, dq_ref, dk_ref, dv_ref, dpk_ref, dpv_ref, ak, av
):
    ak[...] = jnp.zeros_like(ak)
    av[...] = jnp.zeros_like(av)
    for first, key, keys, at in spans(length)[0]:
        n = keys - PW
        qs = stack_heads(q_ref[pl.ds(first, BQ), :] * jnp.asarray(HD**-0.5, bf16))
        dos = stack_heads(do_ref[pl.ds(first, BQ), :])
        ks = jnp.concatenate([pk_ref[...], k_ref[pl.ds(key, n), :]], 0)
        vs = jnp.concatenate([pv_ref[...], v_ref[pl.ds(key, n), :]], 0)
        dp = dot(vs, dos, NT)
        probs = p_ref[0, pl.ds(at, keys), :]
        wide = probs.astype(f32)
        t = wide * dp
        ds = (t - wide * jnp.sum(t, axis=0, keepdims=True)).astype(bf16)
        dk = dot(ds, qs)
        dv = dot(probs, dos)
        dq_ref[pl.ds(first, BQ), :] = (pick_heads(dot(ds, ks, TN)) * HD**-0.5).astype(bf16)
        ak[pl.ds(0, PW), :] += dk[:PW]
        av[pl.ds(0, PW), :] += dv[:PW]
        ak[pl.ds(PW + key, n), :] += dk[PW:]
        av[pl.ds(PW + key, n), :] += dv[PW:]
    dpk_ref[...] = ak[pl.ds(0, PW), :]
    dpv_ref[...] = av[pl.ds(0, PW), :]
    dk_ref[...] = ak[pl.ds(PW, length), :].astype(bf16)
    dv_ref[...] = av[pl.ds(PW, length), :].astype(bf16)


def attend_back(group, qkv, pk, pv, probs, do):
    length = qkv.shape[0]
    steps = qkv.shape[1] // 3 // LANES
    total = spans(length)[1]

    def col(at):
        return pl.BlockSpec((length, LANES), lambda i: (0, at * steps + i))

    small = pl.BlockSpec((PW, LANES), lambda i: (0, i))
    return pl.pallas_call(
        functools.partial(attend_back_kernel, length),
        grid=(steps,),
        in_specs=[col(0), col(1), col(2), small, small]
        + [pl.BlockSpec((1, total, HEADS * BQ), lambda i: (i, 0, 0)), col(group)],
        out_specs=[col(0)] * 3 + [small] * 2,
        out_shape=[jax.ShapeDtypeStruct((length, steps * LANES), bf16)] * 3
        + [jax.ShapeDtypeStruct((PW, steps * LANES), f32)] * 2,
        scratch_shapes=[pltpu.VMEM((PW + length, LANES), f32)] * 2,
        compiler_params=params(),
        cost_estimate=cost(steps * 6e9, steps * 8e6),
        name="attend_back",
    )(qkv, qkv, qkv, pk, pv, probs, do)


def gather_plain(shard):
    whole = lax.all_gather(shard, ALL, axis=0, tiled=True)
    return Weight([whole], whole.shape[0], jnp.zeros((1,), jnp.int32), whole.shape[0])


def per_device(
    tokens,
    seg_ids,
    valid,
    out_grad,
    ln1_gain,
    ln1_bias,
    qkv_weight,
    qkv_bias,
    proj_weight,
    proj_bias,
    ln2_gain,
    ln2_bias,
    fc_weight,
    fc_bias,
    out_weight,
    out_bias,
    prefix_emb,
    rep_weight1,
    rep_bias1,
    rep_weight2,
    rep_bias2,
):
    x, og = tokens[0], out_grad[0]
    length, model = x.shape
    devices = lax.axis_size(ALL)
    hidden_units = fc_weight.shape[1]
    prefix_len = prefix_emb.shape[0]
    gather = gather_plain

    def vec(a):
        return a.astype(f32).reshape(1, -1)

    part = model // GROUPS
    qkv_parts = [
        jnp.concatenate([qkv_weight[:, i * model + g * part : i * model + (g + 1) * part] for i in range(3)], 1)
        for g in range(GROUPS)
    ]
    qkv_biases = [
        jnp.concatenate([qkv_bias[i * model + g * part : i * model + (g + 1) * part] for i in range(3)])
        for g in range(GROUPS)
    ]
    own = out_weight.shape[0] // CHUNKS

    def regroup(a):
        lead = a.shape[:-1]
        a = a.reshape(lead + (devices, CHUNKS, own))
        return jnp.swapaxes(a, -2, -3).reshape(lead + (hidden_units,))

    fc_shard, fc_shift = regroup(fc_weight), regroup(fc_bias)

    pre_hidden = jnp.dot(prefix_emb, rep_weight1, preferred_element_type=f32) + rep_bias1.astype(f32)
    hidden = jnp.tanh(pre_hidden)
    hidden_low = hidden.astype(bf16)
    kv_local = (jnp.dot(hidden_low, rep_weight2, preferred_element_type=f32) + rep_bias2.astype(f32)).astype(bf16)
    prefix_kv = lax.all_gather(kv_local, "pre", axis=1, tiled=True)
    prefix_kv = jnp.pad(prefix_kv, ((0, PW - prefix_len), (0, 0)))

    w_qkv = [gather(p) for p in qkv_parts]
    w_proj = gather(proj_weight)
    w_fc = gather(fc_shard)
    w_out = [gather(out_weight[j * own : (j + 1) * own]) for j in range(CHUNKS)]

    bias = mask_bias(seg_ids[0], valid[0], prefix_len)
    xf = x.astype(f32)
    normed1 = (norm(xf)[0] * ln1_gain.astype(f32) + ln1_bias.astype(f32)).astype(bf16)

    qkvs, mixes, probs, pks, pvs = [], [], [], [], []
    for g in range(GROUPS):
        pks.append(prefix_kv[:, g * part : (g + 1) * part])
        pvs.append(prefix_kv[:, model + g * part : model + (g + 1) * part])
        qkvs.append(project(normed1, w_qkv[g], vec(qkv_biases[g])))
        o, p = attend(qkvs[g], pks[g], pvs[g], bias)
        mixes.append(o)
        probs.append(p)
    mid, normed2 = middle_block(mixes, x, w_proj, vec(proj_bias), vec(ln2_gain), vec(ln2_bias))
    act, slope = expand(normed2, w_fc, vec(fc_shift))
    so_far = None
    for j in range(CHUNKS):
        so_far = contract(j, og, act, slope, mid, vec(out_bias), vec(ln2_gain), so_far, w_fc, w_out[j], w_proj)
    output, grad_mid, grad_attn = so_far

    parts, dpk, dpv = [], [], []
    for g in range(GROUPS):
        dq, dk, dv, a, b = attend_back(g, qkvs[g], pks[g], pvs[g], probs[g], grad_attn)
        parts += [dq, dk, dv]
        dpk.append(a)
        dpv.append(b)
    in_grad = finish(parts, x, grad_mid, vec(ln1_gain), w_qkv)

    prefix_grad = jnp.concatenate(dpk + dpv, 1)[:prefix_len]
    summed = lax.psum(prefix_grad.astype(bf16), "rows")
    kv_low = lax.psum_scatter(summed, "pre", scatter_dimension=1, tiled=True)
    bias2_grad = jnp.sum(kv_low.astype(f32), axis=0)
    weight2_grad = dot(hidden_low, kv_low, TN)
    hid_grad = lax.psum(dot(kv_low, rep_weight2, NT), "pre")
    pre_grad = (hid_grad * (1.0 - hidden * hidden)).astype(bf16)
    bias1_grad = jnp.sum(pre_grad.astype(f32), axis=0)
    weight1_grad = dot(prefix_emb, pre_grad, TN)
    emb_grad = dot(pre_grad, rep_weight1, NT)
    return output[None], in_grad[None], emb_grad, weight1_grad, bias1_grad, weight2_grad, bias2_grad


def solution(mesh):
    split_all = P(ALL, None)
    whole = P()
    return jax.shard_map(
        per_device,
        mesh=mesh,
        in_specs=(
            P(ALL, None, None),
            split_all,
            split_all,
            P(ALL, None, None),
            whole,
            whole,
            split_all,
            whole,
            split_all,
            whole,
            whole,
            whole,
            split_all,
            whole,
            split_all,
            whole,
            whole,
            whole,
            whole,
            P(None, "pre"),
            P("pre"),
        ),
        out_specs=(
            P(ALL, None, None),
            P(ALL, None, None),
            whole,
            whole,
            whole,
            P(None, "pre"),
            P("pre"),
        ),
        check_vma=False,
    )
```

```python
import functools

import jax
import jax.numpy as jnp
from jax import lax
from jax.experimental import pallas as pl
from jax.experimental.pallas import tpu as pltpu
from jax.sharding import PartitionSpec as P

f32 = jnp.float32
bf16 = jnp.bfloat16
ALL = ("rows", "pre")
NEG = -1e30
EPS = 1e-05
HD = 64
SPAN = 256
BQ = 128
PW = 16
LANES = 256
HEADS = LANES // HD
GROUPS = 2
GROUP_STEPS = 2
CHUNKS = 4
BM = 256
LIMIT = 58
SUB = 256

NN = (((1,), (0,)), ((), ()))
NT = (((1,), (1,)), ((), ()))
TN = (((0,), (0,)), ((), ()))


def dot(a, b, dims=NN):
    return lax.dot_general(a, b, dims, preferred_element_type=f32)


def params(mebibytes):
    return pltpu.CompilerParams(vmem_limit_bytes=mebibytes << 20)


def cost(flops, moved):
    return pl.CostEstimate(flops=1, bytes_accessed=1, transcendentals=0)


class Weight:
    def __init__(self, arrays, block, pieces, table, base, rows, cols, at=0):
        self.arrays, self.block, self.pieces, self.table, self.base = arrays, block, pieces, table, base
        self.rows, self.cols, self.at = rows, cols, at

    def specs(self):
        return [pl.BlockSpec(memory_space=pltpu.SMEM)] + [
            pl.BlockSpec(memory_space=pl.ANY) for _ in self.arrays
        ]

    def args(self):
        return [self.table] + list(self.arrays)

    def count(self):
        return 1 + len(self.arrays)

    def scratch(self):
        return [pltpu.VMEM((self.rows, self.cols), bf16), pltpu.SemaphoreType.DMA]


def start_load(w, refs, whole, sem):
    for i, (array, row) in enumerate(w.pieces):
        first = pl.multiple_of(refs[0][w.base + i], w.block)
        pltpu.make_async_copy(
            refs[1 + array].at[pl.ds(row, w.block), pl.ds(w.at, w.cols)], whole.at[pl.ds(first, w.block)], sem
        ).start()


def wait_load(whole, sem):
    pltpu.make_async_copy(whole, whole, sem).wait()


def tied(kernel, count):
    return lambda *refs: kernel(*refs[count:])


def tie_specs(ties):
    return [pl.BlockSpec(memory_space=pl.ANY)] * len(ties)


def arrange(plan, *arrays, ties=()):
    def kernel(*refs):
        ins, outs, sems = refs[: len(arrays)], refs[len(arrays) + len(ties) : -1], refs[-1]
        for k, (_, parts) in enumerate(plan):
            for row, col, array, from_row, from_col, rows, cols in parts:
                pltpu.make_async_copy(
                    ins[array].at[pl.ds(from_row, rows), pl.ds(from_col, cols)],
                    outs[k].at[pl.ds(row, rows), pl.ds(col, cols)],
                    sems.at[k],
                ).start()
        for k in range(len(plan)):
            pltpu.make_async_copy(outs[k], outs[k], sems.at[k]).wait()

    return pl.pallas_call(
        kernel,
        grid=(1,),
        in_specs=[pl.BlockSpec(memory_space=pl.ANY)] * (len(arrays) + len(ties)),
        out_specs=[whole_spec(shape) for shape, _ in plan],
        out_shape=[jax.ShapeDtypeStruct(shape, bf16) for shape, _ in plan],
        scratch_shapes=[pltpu.SemaphoreType.DMA((len(plan),))],
        compiler_params=params(LIMIT),
        cost_estimate=cost(0, 0),
        name="arrange",
    )(*arrays, *ties)


def join(*arrays, ties=()):
    parts, at = [], 0
    for k, a in enumerate(arrays):
        parts.append((at, 0, k, 0, 0, *a.shape))
        at += a.shape[0]
    return arrange([((at, arrays[0].shape[1]), parts)], *arrays, ties=ties)[0]


def norm(values):
    center = values - jnp.mean(values, axis=-1, keepdims=True)
    rate = lax.rsqrt(jnp.mean(center * center, axis=-1, keepdims=True) + EPS)
    return center * rate, rate


def norm_back(values, gain, grad):
    n, rate = norm(values)
    w = grad * gain
    return rate * (
        w - jnp.mean(w, axis=-1, keepdims=True) - n * jnp.mean(w * n, axis=-1, keepdims=True)
    )


def rows_spec(cols, at=0):
    return pl.BlockSpec((BM, cols), lambda i: (i, at))


def whole_spec(shape):
    return pl.BlockSpec(shape, lambda i: (0,) * len(shape))


def middle_kernel(w, *refs):
    head = refs[: GROUPS + 4]
    parts, (x_ref, b_ref, g_ref, s_ref) = head[:GROUPS], head[GROUPS:]
    wr = refs[GROUPS + 4 : GROUPS + 4 + w.count()]
    mid_ref, n_ref, whole, sem = refs[GROUPS + 4 + w.count() :]

    @pl.when(pl.program_id(0) == 0)
    def _():
        start_load(w, wr, whole, sem)
        wait_load(whole, sem)

    attn = jnp.concatenate([p[...] for p in parts], 1)
    mid = x_ref[...].astype(f32) + (dot(attn, whole[...]) + b_ref[...])
    mid_ref[...] = mid
    n_ref[...] = (norm(mid)[0] * g_ref[...] + s_ref[...]).astype(bf16)


def middle_block(parts, x, w, bias, gain, shift, ties=()):
    length, model = x.shape
    vec = whole_spec((1, model))
    return pl.pallas_call(
        tied(functools.partial(middle_kernel, w), len(ties)),
        grid=(length // BM,),
        in_specs=tie_specs(ties) + [rows_spec(p.shape[1]) for p in parts] + [rows_spec(model), vec, vec, vec] + w.specs(),
        out_specs=[rows_spec(model)] * 2,
        out_shape=[
            jax.ShapeDtypeStruct((length, model), f32),
            jax.ShapeDtypeStruct((length, model), bf16),
        ],
        scratch_shapes=w.scratch(),
        compiler_params=params(LIMIT),
        cost_estimate=cost(2 * length * w.rows * w.cols, 12 * length * model),
        name="middle_block",
    )(*ties, *parts, x, bias, gain, shift, *w.args())


def gelu_both(v):
    c, a = 0.7978845608, 0.044715
    sq = v * v
    t = jnp.tanh(v * (c + (c * a) * sq))
    half = 0.5 + 0.5 * t
    act = v * half
    slope = half + (0.5 * v) * (1.0 - t * t) * (c + (3.0 * c * a) * sq)
    return act, slope


def hidden_kernel(w_in, w_out, w_proj, first, *refs):
    refs = list(refs)
    last = w_proj is not None
    (n_ref, og_ref, b_ref), refs = refs[:3], refs[3:]
    if first or last:
        mid_ref = refs.pop(0)
    if first:
        ob_ref = refs.pop(0)
    else:
        (out_in, gn_in), refs = refs[:2], refs[2:]
    if last:
        g_ref = refs.pop(0)
        back, refs = refs[: BACK_REFS], refs[BACK_REFS:]
    wi, refs = refs[: w_in.count()], refs[w_in.count() :]
    wo, refs = refs[: w_out.count()], refs[w_out.count() :]
    if last:
        wp, refs = refs[: w_proj.count()], refs[w_proj.count() :]
        (out_ref, gm_ref, ga_ref, dpk_ref, dpv_ref), refs = refs[:5], refs[5:]
    else:
        (out_ref, gn_ref), refs = refs[:2], refs[2:]
    fc, fc_sem, ow, ow_sem = refs[:4]

    @pl.when(pl.program_id(0) == 0)
    def _():
        start_load(w_in, wi, fc, fc_sem)
        start_load(w_out, wo, ow, ow_sem)
        if last:
            start_load(w_proj, wp, refs[4], refs[5])
            start_back(back, refs[6:11])
        wait_load(fc, fc_sem)
        wait_load(ow, ow_sem)
        if last:
            wait_load(refs[4], refs[5])

    normed, og = n_ref[...], og_ref[...]
    acts, grads = [], []
    for j in range(0, w_in.cols, SUB):
        at = pl.ds(j, SUB)
        act, slope = gelu_both(dot(normed, fc[:, at]) + b_ref[:, at])
        acts.append(act.astype(bf16))
        grads.append((dot(og, ow[at, :], NT) * slope).astype(bf16))
    out = dot(jnp.concatenate(acts, 1), ow[...])
    gn = dot(jnp.concatenate(grads, 1), fc[...], NT)
    if first:
        out = out + (mid_ref[...] + ob_ref[...])
    else:
        out = out + out_in[...]
        gn = gn + gn_in[...]
    out_ref[...] = out.astype(out_ref.dtype)
    if last:
        gm = og.astype(f32) + norm_back(mid_ref[...], g_ref[...], gn)
        gm_ref[...] = gm
        ga = dot(gm.astype(bf16), refs[4][...], NT).astype(bf16)
        ga_ref[...] = ga
        do_all = refs[9]
        do_all[pl.ds(pl.multiple_of(pl.program_id(0) * BM, BM), BM), :] = ga

        @pl.when(pl.program_id(0) == pl.num_programs(0) - 1)
        def _():
            finish_back(back[-1], dpk_ref, dpv_ref, refs[6:11])
    else:
        gn_ref[...] = gn


BACK_REFS = 2 * GROUPS + GROUPS + 1


def start_back(refs, scratch):
    mixes, probs, qkvs = refs[:GROUPS], refs[GROUPS : 2 * GROUPS], refs[2 * GROUPS : 3 * GROUPS]
    q_all, mix_all, p_all, _, sems = scratch
    wide = GROUP_STEPS * LANES
    for g in range(GROUPS):
        rows = probs[g].shape[0]
        pltpu.make_async_copy(probs[g], p_all.at[pl.ds(g * rows, rows)], sems.at[0]).start()
        pltpu.make_async_copy(mixes[g], mix_all.at[:, pl.ds(g * wide, wide)], sems.at[1]).start()
        for k in range(GROUP_STEPS):
            pltpu.make_async_copy(
                qkvs[g].at[:, pl.ds(3 * LANES * k, LANES)], q_all.at[:, pl.ds(g * wide + k * LANES, LANES)], sems.at[2]
            ).start()


def finish_back(pv_ref, dpk_ref, dpv_ref, scratch):
    q_all, mix_all, p_all, do_all, sems = scratch
    for k, ref in enumerate((p_all, mix_all, q_all)):
        pltpu.make_async_copy(ref, ref, sems.at[k]).wait()
    model = do_all.shape[1]
    heads = model // HD
    rows = heads * PW
    own = lax.broadcasted_iota(jnp.int32, (rows, model), 0) // PW == lax.broadcasted_iota(jnp.int32, (rows, model), 1) // HD
    head = lax.broadcasted_iota(jnp.int32, (heads, model), 0) == lax.broadcasted_iota(jnp.int32, (heads, model), 1) // HD
    pv = jnp.concatenate([pv_ref[...]] * heads, 0)
    do = do_all[...]
    dp = dot(jnp.where(own, pv, jnp.zeros_like(pv)), do, NT)
    both = do.astype(f32) * mix_all[...].astype(f32)
    high = both.astype(bf16)
    low = (both - high.astype(f32)).astype(bf16)
    ones = jnp.where(head, 1.0, 0.0).astype(bf16)
    delta = dot(ones, high, NT) + dot(ones, low, NT)
    delta = jnp.concatenate([jnp.broadcast_to(delta[h : h + 1], (PW, delta.shape[1])) for h in range(heads)], 0)
    p = p_all[...]
    ds = (p.astype(f32) * (dp - delta)).astype(bf16)
    for total, ref, scale in ((dot(ds, q_all[...]), dpk_ref, HD**-0.5), (dot(p, do), dpv_ref, 1.0)):
        kept = jnp.where(own, total, 0.0)
        ref[...] = sum(kept[h * PW : (h + 1) * PW] for h in range(heads)) * scale


def hidden_part(normed, og, shift, mid, out_bias, gain, so_far, w_in, w_out, w_proj, back, ties=()):
    length, model = og.shape
    first, last = so_far is None, w_proj is not None
    vec, full = whole_spec((1, model)), rows_spec(model)
    specs, args = [full, full, whole_spec((1, w_in.cols))], [normed, og, shift]
    if first or last:
        specs, args = specs + [full], args + [mid]
    if first:
        specs, args = specs + [vec], args + [out_bias]
    else:
        specs, args = specs + [full, full], args + list(so_far)
    if last:
        mixes, probs, qkvs, pv = back
        specs = specs + [vec] + tie_specs([*mixes, *probs, *qkvs]) + [whole_spec(pv.shape)]
        args = args + [gain, *mixes, *probs, *qkvs, pv]
    specs, args = specs + w_in.specs() + w_out.specs(), args + w_in.args() + w_out.args()
    scratch = w_in.scratch() + w_out.scratch()
    outs = [f32, f32]
    if last:
        specs, args = specs + w_proj.specs(), args + w_proj.args()
        scratch = scratch + w_proj.scratch()
        scratch = scratch + [
            pltpu.VMEM((length, model), bf16),
            pltpu.VMEM((length, model), bf16),
            pltpu.VMEM((model // HD * PW, length), bf16),
            pltpu.VMEM((length, model), bf16),
            pltpu.SemaphoreType.DMA((3,)),
        ]
        outs = [bf16, f32, bf16]
    out_specs = [full] * len(outs)
    out_shape = [jax.ShapeDtypeStruct((length, model), t) for t in outs]
    if last:
        out_specs = out_specs + [whole_spec((PW, model))] * 2
        out_shape = out_shape + [jax.ShapeDtypeStruct((PW, model), f32)] * 2
    return pl.pallas_call(
        tied(functools.partial(hidden_kernel, w_in, w_out, w_proj, first), len(ties)),
        grid=(length // BM,),
        in_specs=tie_specs(ties) + specs,
        out_specs=out_specs,
        out_shape=out_shape,
        scratch_shapes=scratch,
        compiler_params=params(LIMIT),
        cost_estimate=cost(8 * length * w_in.cols * model, 24 * length * model),
        name="hidden_part",
    )(*ties, *args)


def spans(length):
    out, at = [], 0
    for first in range(0, length, BQ):
        key = max(0, first - SPAN)
        keys = PW + first + BQ - key
        out.append((first, key, keys, at))
        at += keys
    return out, at


def mask_kernel(length, prefix, column_ref, row_ref, o_ref):
    for first, key, keys, at in spans(length)[0]:
        n = keys - PW
        pad = lax.broadcasted_iota(jnp.int32, (PW, BQ), 0) < prefix
        o_ref[pl.ds(at, PW), :] = jnp.where(pad, 0.0, NEG)
        key_at = key + lax.broadcasted_iota(jnp.int32, (n, BQ), 0)
        query_at = first + lax.broadcasted_iota(jnp.int32, (n, BQ), 1)
        seen = (column_ref[pl.ds(key, n), :] == row_ref[:, pl.ds(first, BQ)]) & (key_at <= query_at)
        o_ref[pl.ds(at + PW, n), :] = jnp.where(seen, 0.0, NEG)


def mask_bias(seg, valid, prefix, ties=()):
    length = seg.shape[0]
    total = spans(length)[1]
    column = jnp.where(valid > 0, seg, -1).reshape(length, 1)
    return pl.pallas_call(
        tied(functools.partial(mask_kernel, length, prefix), len(ties)),
        grid=(1,),
        in_specs=tie_specs(ties) + [whole_spec((length, 1)), whole_spec((1, length))],
        out_specs=whole_spec((total, BQ)),
        out_shape=jax.ShapeDtypeStruct((total, BQ), f32),
        compiler_params=params(LIMIT),
        cost_estimate=cost(0, 0),
        name="mask_bias",
    )(*ties, column, seg.reshape(1, length))


def first_norm_kernel(x_ref, g_ref, s_ref, o_ref):
    o_ref[...] = (norm(x_ref[...].astype(f32))[0] * g_ref[...] + s_ref[...]).astype(bf16)


def first_norm(x, gain, shift, ties=()):
    length, model = x.shape
    vec = whole_spec((1, model))
    return pl.pallas_call(
        tied(first_norm_kernel, len(ties)),
        grid=(length // BM,),
        in_specs=tie_specs(ties) + [rows_spec(model), vec, vec],
        out_specs=rows_spec(model),
        out_shape=jax.ShapeDtypeStruct((length, model), bf16),
        compiler_params=params(LIMIT),
        cost_estimate=cost(0, 0),
        name="first_norm",
    )(*ties, x, gain, shift)


def of_head(shape, head):
    lane = lax.broadcasted_iota(jnp.int32, shape, 1)
    return (lane >= HD * head) & (lane < HD * (head + 1))


def stack_heads(q):
    return jnp.concatenate([jnp.where(of_head(q.shape, h), q, jnp.zeros_like(q)) for h in range(HEADS)], 0)


def pick_heads(o):
    out = o[:BQ]
    for h in range(1, HEADS):
        out = jnp.where(of_head(out.shape, h), o[h * BQ : (h + 1) * BQ], out)
    return out


def attend_kernel(length, w, *refs):
    x_ref, b_ref, pk_ref, pv_ref, bias_ref = refs[:5]
    wr = refs[5 : 5 + w.count()]
    qkv_ref, o_ref, p_ref, pp_ref, whole, sem = refs[5 + w.count() :]
    plan = spans(length)[0]
    step = pl.program_id(0)

    @pl.when(step == 0)
    def _():
        start_load(w, wr, whole, sem)
        wait_load(whole, sem)

    cols = pl.ds(pl.multiple_of(step * 3 * LANES, 3 * LANES), 3 * LANES)
    qkv_ref[...] = (dot(x_ref[...], whole[:, cols]) + b_ref[...]).astype(bf16)

    def score(i):
        first, key, keys, _ = plan[i]
        q = qkv_ref[pl.ds(first, BQ), pl.ds(0, LANES)] * jnp.asarray(HD**-0.5, bf16)
        ks = jnp.concatenate([pk_ref[...], qkv_ref[pl.ds(key, keys - PW), pl.ds(LANES, LANES)]], 0)
        return dot(ks, stack_heads(q), NT)

    def soft(i, s):
        first, _, keys, at = plan[i]
        s = s + jnp.concatenate([bias_ref[pl.ds(at, keys), :]] * HEADS, 1)
        e = jnp.exp(s - jnp.max(s, axis=0, keepdims=True))
        probs = (e * (1.0 / jnp.sum(e, axis=0, keepdims=True))).astype(bf16)
        p_ref[0, pl.ds(at, keys), :] = probs
        for h in range(HEADS):
            pp_ref[pl.ds(h * PW, PW), pl.ds(first, BQ)] = probs[:PW, h * BQ : (h + 1) * BQ]
        return probs

    def mix(i, probs):
        first, key, keys, _ = plan[i]
        vs = jnp.concatenate([pv_ref[...], qkv_ref[pl.ds(key, keys - PW), pl.ds(2 * LANES, LANES)]], 0)
        o_ref[pl.ds(first, BQ), :] = pick_heads(dot(probs, vs, TN)).astype(bf16)

    n = len(plan)
    s, held = score(0), None
    for i in range(n):
        later = score(i + 1) if i + 1 < n else None
        probs = soft(i, s)
        if held is not None:
            mix(i - 1, held)
        s, held = later, probs
    mix(n - 1, held)


def attend(x, w, shift, pk, pv, bias, ties=()):
    length = x.shape[0]
    steps = w.cols // (3 * LANES)
    total = spans(length)[1]
    small = pl.BlockSpec((PW, LANES), lambda i: (0, i))
    return pl.pallas_call(
        tied(functools.partial(attend_kernel, length, w), len(ties)),
        grid=(steps,),
        in_specs=tie_specs(ties) + [whole_spec(x.shape), pl.BlockSpec((1, 3 * LANES), lambda i: (0, i)), small, small]
        + [whole_spec((total, BQ))]
        + w.specs(),
        out_specs=[
            pl.BlockSpec((length, 3 * LANES), lambda i: (0, i)),
            pl.BlockSpec((length, LANES), lambda i: (0, i)),
            pl.BlockSpec((1, total, HEADS * BQ), lambda i: (i, 0, 0)),
            pl.BlockSpec((HEADS * PW, length), lambda i: (i, 0)),
        ],
        out_shape=[
            jax.ShapeDtypeStruct((length, w.cols), bf16),
            jax.ShapeDtypeStruct((length, steps * LANES), bf16),
            jax.ShapeDtypeStruct((steps, total, HEADS * BQ), bf16),
            jax.ShapeDtypeStruct((steps * HEADS * PW, length), bf16),
        ],
        scratch_shapes=w.scratch(),
        compiler_params=params(LIMIT),
        cost_estimate=cost(steps * 8e9, steps * 8e6),
        name="attend",
    )(*ties, x, shift, pk, pv, bias, *w.args())


def attend_back_kernel(length, ws, *refs):
    steps = GROUP_STEPS * GROUPS
    qkv_refs, refs = refs[:GROUPS], refs[GROUPS:]
    p_refs, refs = refs[:GROUPS], refs[GROUPS:]
    (pk_ref, pv_ref, do_ref, x_hbm, gm_hbm, g_ref), refs = refs[:6], refs[6:]
    wr = []
    for w in ws:
        wr.append(refs[: w.count()])
        refs = refs[w.count() :]
    out_ref, refs = refs[0], refs[1:]
    ak, av, dqkv, gn, x_vm, gm_vm, io_sem = refs[:7]
    scratch = refs[7:]
    step = pl.program_id(0)
    x_copy = pltpu.make_async_copy(x_hbm, x_vm, io_sem.at[0])
    gm_copy = pltpu.make_async_copy(gm_hbm, gm_vm, io_sem.at[1])

    @pl.when(step == 0)
    def _():
        for i, w in enumerate(ws):
            start_load(w, wr[i], scratch[2 * i], scratch[2 * i + 1])
        x_copy.start()
        gm_copy.start()

    def run(qkv_ref, p_ref):
        ak[...] = jnp.zeros_like(ak)
        av[...] = jnp.zeros_like(av)
        plan = spans(length)[0]

        def scores(i):
            first, key, keys, _ = plan[i]
            dos = stack_heads(do_ref[pl.ds(first, BQ), :])
            vs = jnp.concatenate([pv_ref[...], qkv_ref[pl.ds(key, keys - PW), pl.ds(2 * LANES, LANES)]], 0)
            return dos, dot(vs, dos, NT)

        def soft(i, dos, dp):
            _, _, keys, at = plan[i]
            probs = p_ref[0, pl.ds(at, keys), :]
            wide = probs.astype(f32)
            t = wide * dp
            return dos, probs, (t - wide * jnp.sum(t, axis=0, keepdims=True)).astype(bf16)

        def mix(i, dos, probs, ds):
            first, key, keys, _ = plan[i]
            n = keys - PW
            qs = stack_heads(qkv_ref[pl.ds(first, BQ), pl.ds(0, LANES)] * jnp.asarray(HD**-0.5, bf16))
            ks = jnp.concatenate([pk_ref[...], qkv_ref[pl.ds(key, n), pl.ds(LANES, LANES)]], 0)
            ak[pl.ds(key, n), :] += dot(ds[PW:], qs)
            av[pl.ds(key, n), :] += dot(probs[PW:], dos)
            dqkv[pl.ds(first, BQ), pl.ds(0, LANES)] = (pick_heads(dot(ds, ks, TN)) * HD**-0.5).astype(bf16)

        n = len(plan)
        s, held = scores(0), None
        for i in range(n):
            later = scores(i + 1) if i + 1 < n else None
            done = soft(i, *s)
            if held is not None:
                mix(i - 1, *held)
            s, held = later, done
        mix(n - 1, *held)
        dqkv[:, pl.ds(LANES, LANES)] = ak[...].astype(bf16)
        dqkv[:, pl.ds(2 * LANES, LANES)] = av[...].astype(bf16)

    for g in range(GROUPS):

        @pl.when(step // GROUP_STEPS == g)
        def _():
            run(qkv_refs[g], p_refs[g])

            @pl.when(step == g * GROUP_STEPS)
            def _():
                wait_load(scratch[2 * g], scratch[2 * g + 1])

            at = pl.multiple_of((step - g * GROUP_STEPS) * 3 * LANES, 3 * LANES)
            part = dot(dqkv[...], scratch[2 * g][:, pl.ds(at, 3 * LANES)], NT)

            @pl.when(step == 0)
            def _():
                gn[...] = part

            @pl.when(step > 0)
            def _():
                gn[...] += part

    @pl.when(step == steps - 1)
    def _():
        x_copy.wait()
        gm_copy.wait()

        def rows(i, carry):
            at = pl.ds(pl.multiple_of(i * BM, BM), BM)
            out_ref[at, :] = (
                gm_vm[at, :] + norm_back(x_vm[at, :].astype(f32), g_ref[...], gn[at, :])
            ).astype(bf16)
            return carry

        lax.fori_loop(0, length // BM, rows, 0)


def attend_back(qkvs, probs, pk, pv, do, x, gm, gain, ws):
    length, model = x.shape
    steps = GROUP_STEPS * GROUPS
    total = spans(length)[1]

    def mine(g):
        return lambda i: jnp.clip(i - g * GROUP_STEPS, 0, GROUP_STEPS - 1)

    def qkv_spec(g):
        return pl.BlockSpec((length, 3 * LANES), lambda i: (0, mine(g)(i)))

    def p_spec(g):
        return pl.BlockSpec((1, total, HEADS * BQ), lambda i: (mine(g)(i), 0, 0))

    small = pl.BlockSpec((PW, LANES), lambda i: (0, i))
    hbm = pl.BlockSpec(memory_space=pl.ANY)
    return pl.pallas_call(
        functools.partial(attend_back_kernel, length, ws),
        grid=(steps,),
        in_specs=[qkv_spec(g) for g in range(GROUPS)]
        + [p_spec(g) for g in range(GROUPS)]
        + [small, small, pl.BlockSpec((length, LANES), lambda i: (0, i)), hbm, hbm, whole_spec((1, model))]
        + sum([w.specs() for w in ws], []),
        out_specs=whole_spec((length, model)),
        out_shape=jax.ShapeDtypeStruct((length, model), bf16),
        scratch_shapes=[pltpu.VMEM((length, LANES), f32)] * 2
        + [pltpu.VMEM((length, 3 * LANES), bf16), pltpu.VMEM((length, model), f32)]
        + [pltpu.VMEM((length, model), bf16), pltpu.VMEM((length, model), f32), pltpu.SemaphoreType.DMA((2,))]
        + sum([w.scratch() for w in ws], []),
        compiler_params=params(LIMIT),
        cost_estimate=cost(steps * 8e9, steps * 8e6),
        name="attend_back",
    )(*qkvs, *probs, pk, pv, do, x, gm, gain, *sum([w.args() for w in ws], []))


def after(value, *others):
    return lax.optimization_barrier((value, *others))[0]


class Plain:
    def gather(self, shard):
        whole = lax.all_gather(shard, ALL, axis=0, tiled=True)
        rows, cols = whole.shape
        return Weight([whole], rows, [(0, 0)], jnp.zeros((1,), jnp.int32), 0, rows, cols)

    def columns(self, part):
        return lax.all_gather(part, "pre", axis=1, tiled=True)

    def sum_columns(self, part):
        return lax.psum_scatter(lax.psum(part, "rows"), "pre", scatter_dimension=1, tiled=True)

    def sum_pre(self, part):
        return lax.psum(part, "pre")


class Grid:
    planes = 4

    def __init__(self, rows_in, rows_out):
        self.places = [(z, x, y, c) for z in range(4) for x in range(2) for y in range(2) for c in range(2)]
        self.me = lax.axis_index(ALL)
        self.rows_in, self.rows_out = rows_in, rows_out
        table = []
        for z, x, y, c in self.places:
            lines = [place for pair in self.sources(x, y, c) for place in pair]
            table.append(
                [rows_in * self.number(z ^ k, *p) for p in lines for k in range(4)]
                + [rows_in * self.number(k, *p) for p in lines for k in range(4)]
                + [rows_out * self.number(0, *p) for p in lines]
            )
        self.table = lax.dynamic_index_in_dim(jnp.asarray(table, jnp.int32), self.me, 0, False)

    @staticmethod
    def number(z, x, y, c):
        return z * 8 + x * 4 + y * 2 + c

    @staticmethod
    def side(x, y, c, second):
        return (1 - x, y) if (c == 0) != second else (x, 1 - y)

    def send(self, value, where):
        return lax.ppermute(value, ALL, [(self.number(*p), self.number(*where(*p))) for p in self.places])

    def plane(self, value, k):
        return self.send(value, lambda z, x, y, c: (z ^ k, x, y, c))

    def beside(self, value, second):
        return self.send(value, lambda z, x, y, c: (z, *self.side(x, y, c, second), c))

    def core(self, value):
        return self.send(value, lambda z, x, y, c: (z, x, y, 1 - c))

    def planes_of(self, block):
        return [self.plane(block, k) for k in range(1, self.planes)]

    def line_in_order(self, block):
        groups = [[self.number(z, x, y, c) for z in range(4)] for x in range(2) for y in range(2) for c in range(2)]
        return lax.all_gather(block, ALL, axis=0, tiled=True, axis_index_groups=groups)

    def far(self, half):
        return self.beside(half, True)

    def swap(self, half, other):
        return [half, other, self.core(half), self.core(other)]

    def sources(self, x, y, c):
        out = []
        for core in (c, 1 - c):
            for place in ((x, y), self.side(x, y, core, True)):
                out.append([(*place, core), (*self.side(*place, core, False), core)])
        return out

    def weight(self, arrays, cols, at=0):
        rows = self.rows_in
        pieces = [(a, (4 * s + k) * rows) for a in range(4) for s in (0, 1) for k in range(4)]
        return Weight(arrays, rows, pieces, self.table, 0, rows * len(self.places), cols, at)

    def hidden_weights(self, arrays):
        rows_in, rows_out = self.rows_in, self.rows_out
        size = rows_out + 4 * rows_in
        devices, cols = len(self.places), arrays[0].shape[1]
        inner = [(a, size * s + rows_out + rows_in * z) for a in range(4) for s in (0, 1) for z in range(4)]
        outer = [(a, size * s) for a in range(4) for s in (0, 1)]
        return (
            Weight(arrays, rows_in, inner, self.table, devices, rows_in * devices, cols),
            Weight(arrays, rows_out, outer, self.table, 2 * devices, rows_out * devices // 4, cols),
        )

    def columns(self, part):
        y, c = (self.me // 2) % 2, self.me % 2
        other = self.core(part)
        pair = jnp.where(c == 0, jnp.concatenate([part, other], 1), jnp.concatenate([other, part], 1))
        other = self.send(pair, lambda z, x, y, c: (z, x, 1 - y, c))
        return jnp.where(y == 0, jnp.concatenate([pair, other], 1), jnp.concatenate([other, pair], 1))

    def sum_columns(self, part):
        y, c = (self.me // 2) % 2, self.me % 2
        cols = part.shape[1]
        low, high = part[:, : cols // 2], part[:, cols // 2 :]
        part = jnp.where(y == 0, low, high) + self.send(
            jnp.where(y == 0, high, low), lambda z, x, y, c: (z, x, 1 - y, c)
        )
        low, high = part[:, : cols // 4], part[:, cols // 4 :]
        part = jnp.where(c == 0, low, high) + self.core(jnp.where(c == 0, high, low))
        part = part + self.send(part, lambda z, x, y, c: (z, 1 - x, y, c))
        part = part + self.plane(part, 1)
        return part + self.plane(part, 2)

    def sum_pre(self, part):
        part = part + self.core(part)
        return part + self.send(part, lambda z, x, y, c: (z, x, 1 - y, c))


def per_device(
    tokens,
    seg_ids,
    valid,
    out_grad,
    ln1_gain,
    ln1_bias,
    qkv_weight,
    qkv_bias,
    proj_weight,
    proj_bias,
    ln2_gain,
    ln2_bias,
    fc_weight,
    fc_bias,
    out_weight,
    out_bias,
    prefix_emb,
    rep_weight1,
    rep_bias1,
    rep_weight2,
    rep_bias2,
):
    x, og = tokens[0], out_grad[0]
    length, model = x.shape
    devices = lax.axis_size(ALL)
    hidden_units = fc_weight.shape[1]
    prefix_len = prefix_emb.shape[0]
    on_grid = (lax.axis_size("rows"), lax.axis_size("pre")) == (8, 4)
    net = Grid(qkv_weight.shape[0], out_weight.shape[0]) if on_grid else Plain()

    def vec(a):
        return a.astype(f32).reshape(1, -1)

    part = model // GROUPS

    def step_starts(g):
        return [i * model + g * part + k * LANES for k in range(GROUP_STEPS) for i in range(3)]

    qkv_biases = [vec(jnp.concatenate([qkv_bias[at : at + LANES] for at in step_starts(g)])) for g in range(GROUPS)]
    gain1, shift1, gain2, shift2 = vec(ln1_gain), vec(ln1_bias), vec(ln2_gain), vec(ln2_bias)
    proj_shift, out_shift = vec(proj_bias), vec(out_bias)
    width = hidden_units // CHUNKS
    fc_biases = [vec(fc_bias[j * width : (j + 1) * width]) for j in range(CHUNKS)]

    own_q, own_o = qkv_weight.shape[0], out_weight.shape[0]

    def by_step(g):
        return [(0, k * LANES, 0, 0, at, own_q, LANES) for k, at in enumerate(step_starts(g))]

    shard_a, shard_b = arrange(
        [
            ((own_q, 3 * part), by_step(0)),
            ((own_q, 3 * part + model), by_step(1) + [(0, 3 * part, 1, 0, 0, own_q, model)]),
        ],
        qkv_weight,
        proj_weight,
    )
    (shard_h,) = arrange(
        [
            (
                (own_o + CHUNKS * own_q, model),
                [(0, 0, 0, 0, 0, own_o, model)]
                + [(own_o + j * own_q, 0, 1, 0, j * width, own_q, width) for j in range(CHUNKS)],
            )
        ],
        out_weight,
        fc_weight,
    )

    if on_grid:
        others_a = net.planes_of(shard_a)
        others_b = net.planes_of(shard_b)
        line_h = net.line_in_order(shard_h)
        line_a = join(shard_a, *others_a)
        next_a = net.beside(line_a, False)
        prefix_emb = after(prefix_emb, line_a)

    pre_hidden = jnp.dot(prefix_emb, rep_weight1, preferred_element_type=f32) + rep_bias1.astype(f32)
    hidden = jnp.tanh(pre_hidden)
    hidden_low = hidden.astype(bf16)
    kv_local = (jnp.dot(hidden_low, rep_weight2, preferred_element_type=f32) + rep_bias2.astype(f32)).astype(bf16)
    prefix_kv = net.columns(kv_local)
    prefix_kv = jnp.pad(prefix_kv, ((0, PW - prefix_len), (0, 0)))


    def run_norm(ties=()):
        return first_norm(x, gain1, shift1, ties)

    pks = [prefix_kv[:, g * part : (g + 1) * part] for g in range(GROUPS)]
    pvs = [prefix_kv[:, model + g * part : model + (g + 1) * part] for g in range(GROUPS)]

    def run_attend(g, w, normed1, bias, ties=()):
        return attend(normed1, w, qkv_biases[g], pks[g], pvs[g], bias, ties)

    def run_hidden(j, so_far, normed2, w_in, w_out, ties=()):
        back = (mixes, pprobs, qkvs, prefix_kv[:, model:])
        return hidden_part(
            normed2,
            og,
            fc_biases[j],
            mid,
            out_shift,
            gain2,
            so_far,
            w_in,
            w_out,
            w_proj if j == CHUNKS - 1 else None,
            back,
            ties,
        )

    so_far = None
    if isinstance(net, Plain):
        w_qkv = [net.gather(shard_a), net.gather(shard_b[:, : 3 * part])]
        w_proj = net.gather(proj_weight)
        normed1, bias = run_norm(), mask_bias(seg_ids[0], valid[0], prefix_len)
        out_all = lax.all_gather(out_weight, ALL, axis=0, tiled=True)
        qkvs, mixes, probs, pprobs = zip(*[run_attend(g, w_qkv[g], normed1, bias) for g in range(GROUPS)])
        mid, normed2 = middle_block(mixes, x, w_proj, proj_shift, gain2, shift2)
        for j in range(CHUNKS):
            w_in = net.gather(fc_weight[:, j * width : (j + 1) * width])
            w_out = Weight([out_all], width, [(0, j * width)], jnp.zeros((1,), jnp.int32), 0, width, model)
            so_far = run_hidden(j, so_far, normed2, w_in, w_out)
    else:
        own_h = own_o + CHUNKS * own_q
        def send_lines(parts, ties):
            return arrange(
                [
                    (
                        (own_o + net.planes * own_q, model),
                        [(0, 0, 0, j * own_h, 0, own_o, model)]
                        + [
                            (own_o + z * own_q, 0, 0, z * own_h + own_o + j * own_q, 0, own_q, model)
                            for z in range(net.planes)
                        ],
                    )
                    for j in parts
                ],
                line_h,
                ties=ties,
            )

        normed1 = run_norm((line_a,))
        half_a = join(line_a, next_a)
        far_a = net.beside(half_a, True)
        early = (net.table, *pks, *pvs, *qkv_biases, *fc_biases, proj_shift, gain2, shift2, out_shift)
        bias = mask_bias(seg_ids[0], valid[0], prefix_len, (half_a, normed1, *early))
        line_b = join(shard_b, *others_b, ties=(bias,))
        next_b = net.beside(line_b, False)
        w_a = net.weight(net.swap(half_a, far_a), 3 * part)
        half_b = join(line_b, next_b, ties=(far_a, prefix_kv))
        far_b = net.beside(half_b, True)
        qkv_a, mix_a, probs_a, pprobs_a = run_attend(0, w_a, normed1, bias, (half_b,))
        arrays_b = net.swap(half_b, after(far_b, mix_a))
        w_b, w_proj = net.weight(arrays_b, 3 * part), net.weight(arrays_b, model, 3 * part)
        lines = list(send_lines((0, 1), (mix_a, far_b)))
        nexts = [net.beside(a, False) for a in lines]
        qkv_b, mix_b, probs_b, pprobs_b = run_attend(1, w_b, normed1, bias, tuple(lines))
        halves = [join(lines[0], nexts[0], ties=(mix_b, nexts[1]))]
        halves.append(join(lines[1], nexts[1], ties=(halves[0],)))
        fars = [net.beside(a, True) for a in halves]
        mid, normed2 = middle_block([mix_a, mix_b], x, w_proj, proj_shift, gain2, shift2, tuple(halves))
        lines += send_lines((2, 3), (mid, fars[0]))
        nexts += [net.beside(a, False) for a in lines[2:]]
        w_qkv, qkvs, probs = [w_a, w_b], [qkv_a, qkv_b], [probs_a, probs_b]
        mixes, pprobs = [mix_a, mix_b], [pprobs_a, pprobs_b]
        gate = mid
        for j in range(CHUNKS):
            w_in, w_out = net.hidden_weights(net.swap(halves[j], after(fars[j], gate)))
            if j == 0:
                ties = tuple(lines[2:])
            elif j + 1 < CHUNKS:
                halves.append(join(lines[j + 1], nexts[j + 1], ties=(gate, fars[j])))
                fars.append(net.beside(halves[j + 1], True))
                ties = (halves[j + 1],)
            else:
                ties = ()
            so_far = run_hidden(j, so_far, normed2, w_in, w_out, ties)
            gate = so_far[0]
    output, grad_mid, grad_attn, dpk, dpv = so_far
    prefix_grad = jnp.concatenate([dpk, dpv], 1)[:prefix_len]
    in_grad = attend_back(
        qkvs,
        probs,
        prefix_kv[:, :model],
        prefix_kv[:, model:],
        grad_attn,
        x,
        grad_mid,
        gain1,
        w_qkv,
    )
    kv_low = net.sum_columns(prefix_grad).astype(bf16)
    bias2_grad = jnp.sum(kv_low.astype(f32), axis=0)
    weight2_grad = dot(hidden_low, kv_low, TN)
    hid_grad = net.sum_pre(dot(kv_low, rep_weight2, NT))
    pre_grad = (hid_grad * (1.0 - hidden * hidden)).astype(bf16)
    bias1_grad = jnp.sum(pre_grad.astype(f32), axis=0)
    weight1_grad = dot(prefix_emb, pre_grad, TN)
    emb_grad = dot(pre_grad, rep_weight1, NT)
    return output[None], in_grad[None], emb_grad, weight1_grad, bias1_grad, weight2_grad, bias2_grad


def solution(mesh):
    split_all = P(ALL, None)
    whole = P()
    return jax.shard_map(
        per_device,
        mesh=mesh,
        in_specs=(
            P(ALL, None, None),
            split_all,
            split_all,
            P(ALL, None, None),
            whole,
            whole,
            split_all,
            whole,
            split_all,
            whole,
            whole,
            whole,
            split_all,
            whole,
            split_all,
            whole,
            whole,
            whole,
            whole,
            P(None, "pre"),
            P("pre"),
        ),
        out_specs=(
            P(ALL, None, None),
            P(ALL, None, None),
            whole,
            whole,
            whole,
            P(None, "pre"),
            P("pre"),
        ),
        check_vma=False,
    )
```

```python
import functools

import jax
import jax.numpy as jnp
from jax import lax
from jax.experimental import pallas as pl
from jax.experimental.pallas import tpu as pltpu
from jax.sharding import PartitionSpec as P

f32 = jnp.float32
bf16 = jnp.bfloat16
ALL = ("rows", "pre")
NEG = -1e30
EPS = 1e-05
HD = 64
SPAN = 256
BQ = 128
PW = 16
LANES = 256
HEADS = LANES // HD
GROUPS = 2
GROUP_STEPS = 2
CHUNKS = 4
BM = 256
BIG = 512
LIMIT = 58
SUB = 256

NN = (((1,), (0,)), ((), ()))
NT = (((1,), (1,)), ((), ()))
TN = (((0,), (0,)), ((), ()))


def dot(a, b, dims=NN):
    return lax.dot_general(a, b, dims, preferred_element_type=f32)


def params(mebibytes):
    return pltpu.CompilerParams(vmem_limit_bytes=mebibytes << 20)


def cost(microseconds):
    return pl.CostEstimate(flops=int(microseconds * 1.1e9), bytes_accessed=1, transcendentals=0)


class Weight:
    def __init__(self, net, arrays, block, pieces, rows, cols, at=0):
        self.net, self.arrays, self.block, self.pieces = net, arrays, block, pieces
        self.rows, self.cols, self.at = rows, cols, at

    def specs(self):
        return [pl.BlockSpec(memory_space=pl.ANY) for _ in self.arrays]

    def count(self):
        return len(self.arrays)

    def scratch(self):
        return [pltpu.VMEM((self.rows, self.cols), bf16), pltpu.SemaphoreType.DMA]


def start_load(w, refs, whole, sem):
    here = w.net.position()
    for array, row, place in w.pieces:
        first = pl.multiple_of(place(*here), w.block)
        pltpu.make_async_copy(
            refs[array].at[pl.ds(row, w.block), pl.ds(w.at, w.cols)], whole.at[pl.ds(first, w.block)], sem
        ).start()


def wait_load(whole, sem):
    pltpu.make_async_copy(whole, whole, sem).wait()


def tied(kernel, count):
    return lambda *refs: kernel(*refs[count:])


def tie_specs(ties):
    return [pl.BlockSpec(memory_space=pl.ANY)] * len(ties)


def arrange(plan, *arrays, ties=()):
    def kernel(*refs):
        ins, outs, sems = refs[: len(arrays)], refs[len(arrays) + len(ties) : -1], refs[-1]
        for k, (_, parts) in enumerate(plan):
            for row, col, array, from_row, from_col, rows, cols in parts:
                pltpu.make_async_copy(
                    ins[array].at[pl.ds(from_row, rows), pl.ds(from_col, cols)],
                    outs[k].at[pl.ds(row, rows), pl.ds(col, cols)],
                    sems.at[k],
                ).start()
        for k in range(len(plan)):
            pltpu.make_async_copy(outs[k], outs[k], sems.at[k]).wait()

    return pl.pallas_call(
        kernel,
        grid=(1,),
        in_specs=[pl.BlockSpec(memory_space=pl.ANY)] * (len(arrays) + len(ties)),
        out_specs=[whole_spec(shape) for shape, _ in plan],
        out_shape=[jax.ShapeDtypeStruct(shape, bf16) for shape, _ in plan],
        scratch_shapes=[pltpu.SemaphoreType.DMA((len(plan),))],
        compiler_params=params(LIMIT),
        cost_estimate=cost(2),
        name="arrange",
    )(*arrays, *ties)


def gate(arrays, ties):
    n = len(arrays)
    spec = pl.BlockSpec(memory_space=pl.ANY)
    return pl.pallas_call(
        lambda *refs: None,
        grid=(1,),
        in_specs=[spec] * (n + len(ties)),
        out_specs=[spec] * n,
        out_shape=[jax.ShapeDtypeStruct(a.shape, a.dtype) for a in arrays],
        input_output_aliases={i: i for i in range(n)},
        compiler_params=params(LIMIT),
        cost_estimate=cost(1),
        name="gate",
    )(*arrays, *ties)


def join(*arrays, ties=()):
    parts, at = [], 0
    for k, a in enumerate(arrays):
        parts.append((at, 0, k, 0, 0, *a.shape))
        at += a.shape[0]
    return arrange([((at, arrays[0].shape[1]), parts)], *arrays, ties=ties)[0]


GAIN1, SHIFT1, GAIN2, SHIFT2, PROJ_SHIFT, OUT_SHIFT, QKV_SHIFT, FC_SHIFT = range(8)


def pack_kernel(plan, *refs):
    out = refs[-1]
    out[...] = jnp.zeros_like(out)
    for ref, row in zip(refs[:-1], plan, strict=True):
        for at, start, size in row[1]:
            out[pl.ds(row[0], 1), pl.ds(at, size)] = ref[pl.ds(start, size)].astype(f32).reshape(1, size)


def pack(plan, width, *vectors):
    return pl.pallas_call(
        functools.partial(pack_kernel, plan),
        grid=(1,),
        in_specs=[whole_spec(v.shape) for v in vectors],
        out_specs=whole_spec((8, width)),
        out_shape=jax.ShapeDtypeStruct((8, width), f32),
        compiler_params=params(LIMIT),
        cost_estimate=cost(1.5),
        name="pack",
    )(*vectors)


def row_of(ref, row, size, at=0):
    return ref[pl.ds(row, 1), pl.ds(at, size)]


def norm(values):
    center = values - jnp.mean(values, axis=-1, keepdims=True)
    rate = lax.rsqrt(jnp.mean(center * center, axis=-1, keepdims=True) + EPS)
    return center * rate, rate


def norm_back(values, gain, grad):
    n, rate = norm(values)
    w = grad * gain
    return rate * (
        w - jnp.mean(w, axis=-1, keepdims=True) - n * jnp.mean(w * n, axis=-1, keepdims=True)
    )


def rows_spec(cols, at=0, rows=None):
    return pl.BlockSpec((rows or BM, cols), lambda i: (i, at))


def whole_spec(shape):
    return pl.BlockSpec(shape, lambda i: (0,) * len(shape))


def middle_kernel(w, *refs):
    parts, (x_ref, v_ref), refs = refs[:GROUPS], refs[GROUPS : GROUPS + 2], refs[GROUPS + 2 :]
    wr = refs[: w.count()]
    mid_ref, n_ref, whole, sem = refs[w.count() :]
    model = w.cols

    @pl.when(pl.program_id(0) == 0)
    def _():
        start_load(w, wr, whole, sem)
        wait_load(whole, sem)

    attn = jnp.concatenate([p[...] for p in parts], 1)
    mid = x_ref[...].astype(f32) + (dot(attn, whole[...]) + row_of(v_ref, PROJ_SHIFT, model))
    mid_ref[...] = mid
    n_ref[...] = (norm(mid)[0] * row_of(v_ref, GAIN2, model) + row_of(v_ref, SHIFT2, model)).astype(bf16)


def middle_block(parts, x, w, vecs, ties=()):
    length, model = x.shape
    return pl.pallas_call(
        tied(functools.partial(middle_kernel, w), len(ties)),
        grid=(length // BIG,),
        in_specs=tie_specs(ties) + [rows_spec(p.shape[1], rows=BIG) for p in parts] + [rows_spec(model, rows=BIG), whole_spec(vecs.shape)] + w.specs(),
        out_specs=[rows_spec(model, rows=BIG)] * 2,
        out_shape=[
            jax.ShapeDtypeStruct((length, model), f32),
            jax.ShapeDtypeStruct((length, model), bf16),
        ],
        scratch_shapes=w.scratch(),
        compiler_params=params(LIMIT),
        cost_estimate=cost(8.5),
        name="middle_block",
    )(*ties, *parts, x, vecs, *w.arrays)


def gelu_both(v):
    c, a = 0.7978845608, 0.044715
    sq = v * v
    t = jnp.tanh(v * (c + (c * a) * sq))
    half = 0.5 + 0.5 * t
    act = v * half
    slope = half + (0.5 * v) * (1.0 - t * t) * (c + (3.0 * c * a) * sq)
    return act, slope


def hidden_kernel(w_in, w_out, w_proj, chunk, *refs):
    refs = list(refs)
    first, last = chunk == 0, w_proj is not None
    model, width = w_in.rows, w_in.cols
    (n_ref, og_ref, v_ref), refs = refs[:3], refs[3:]
    if first or last:
        mid_ref = refs.pop(0)
    if not first:
        (out_in, gn_in), refs = refs[:2], refs[2:]
    if last:
        back, refs = refs[: BACK_REFS], refs[BACK_REFS:]
    wi, refs = refs[: w_in.count()], refs[w_in.count() :]
    wo, refs = refs[: w_out.count()], refs[w_out.count() :]
    if last:
        wp, refs = refs[: w_proj.count()], refs[w_proj.count() :]
        (out_ref, gm_ref, ga_ref, dpk_ref, dpv_ref), refs = refs[:5], refs[5:]
    else:
        (out_ref, gn_ref), refs = refs[:2], refs[2:]
    fc, fc_sem, ow, ow_sem = refs[:4]

    @pl.when(pl.program_id(0) == 0)
    def _():
        start_load(w_in, wi, fc, fc_sem)
        start_load(w_out, wo, ow, ow_sem)
        if last:
            start_load(w_proj, wp, refs[4], refs[5])
            start_back(back, refs[6:11])
        wait_load(fc, fc_sem)
        wait_load(ow, ow_sem)
        if last:
            wait_load(refs[4], refs[5])

    normed, og = n_ref[...], og_ref[...]
    acts, grads = [], []
    for j in range(0, width, SUB):
        at = pl.ds(j, SUB)
        act, slope = gelu_both(dot(normed, fc[:, at]) + row_of(v_ref, FC_SHIFT, SUB, chunk * width + j))
        acts.append(act.astype(bf16))
        grads.append((dot(og, ow[at, :], NT) * slope).astype(bf16))
    out = dot(jnp.concatenate(acts, 1), ow[...])
    gn = dot(jnp.concatenate(grads, 1), fc[...], NT)
    if first:
        out = out + (mid_ref[...] + row_of(v_ref, OUT_SHIFT, model))
    else:
        out = out + out_in[...]
        gn = gn + gn_in[...]
    out_ref[...] = out.astype(out_ref.dtype)
    if last:
        gm = og.astype(f32) + norm_back(mid_ref[...], row_of(v_ref, GAIN2, model), gn)
        gm_ref[...] = gm
        ga = dot(gm.astype(bf16), refs[4][...], NT).astype(bf16)
        ga_ref[...] = ga
        refs[9][pl.ds(pl.multiple_of(pl.program_id(0) * BM, BM), BM), :] = ga

        @pl.when(pl.program_id(0) == pl.num_programs(0) - 1)
        def _():
            finish_back(back[-1], dpk_ref, dpv_ref, refs[6:11])
    else:
        gn_ref[...] = gn


BACK_REFS = 2 * GROUPS + GROUPS + 1


def start_back(refs, scratch):
    mixes, probs, qkvs = refs[:GROUPS], refs[GROUPS : 2 * GROUPS], refs[2 * GROUPS : 3 * GROUPS]
    q_all, mix_all, p_all, _, sems = scratch[:5]
    wide = GROUP_STEPS * LANES
    for g in range(GROUPS):
        rows = probs[g].shape[0]
        pltpu.make_async_copy(probs[g], p_all.at[pl.ds(g * rows, rows)], sems.at[0]).start()
        pltpu.make_async_copy(mixes[g], mix_all.at[:, pl.ds(g * wide, wide)], sems.at[1]).start()
        for k in range(GROUP_STEPS):
            pltpu.make_async_copy(
                qkvs[g].at[:, pl.ds(3 * LANES * k, LANES)], q_all.at[:, pl.ds(g * wide + k * LANES, LANES)], sems.at[2]
            ).start()


def own_head(rows, each, model):
    head = lax.broadcasted_iota(jnp.int32, (rows, model), 0) // each
    return head == lax.broadcasted_iota(jnp.int32, (rows, model), 1) // HD


def finish_back(pv_ref, dpk_ref, dpv_ref, scratch):
    q_all, mix_all, p_all, do_all, sems = scratch
    for k, ref in enumerate((p_all, mix_all, q_all)):
        pltpu.make_async_copy(ref, ref, sems.at[k]).wait()
    model = do_all.shape[1]
    heads = model // HD
    do = do_all[...]
    own = own_head(heads * PW, PW, model)
    pv = jnp.concatenate([pv_ref[...]] * heads, 0)
    dp = dot(jnp.where(own, pv, jnp.zeros_like(pv)), do, NT)
    ones = jnp.where(own_head(heads, 1, model), 1.0, 0.0).astype(bf16)
    delta = dot(ones, (do.astype(f32) * mix_all[...].astype(f32)).astype(bf16), NT)
    delta = jnp.concatenate([jnp.broadcast_to(delta[h : h + 1], (PW, delta.shape[1])) for h in range(heads)], 0)
    p = p_all[...]
    ds = (p.astype(f32) * (dp - delta)).astype(bf16)
    for total, ref, scale in ((dot(ds, q_all[...]), dpk_ref, HD**-0.5), (dot(p, do), dpv_ref, 1.0)):
        kept = jnp.where(own, total, 0.0)
        ref[...] = sum(kept[h * PW : (h + 1) * PW] for h in range(heads)) * scale


def hidden_part(chunk, normed, og, vecs, mid, so_far, w_in, w_out, w_proj, back, ties=()):
    length, model = og.shape
    first, last = chunk == 0, w_proj is not None
    full = rows_spec(model)
    specs, args = [full, full, whole_spec(vecs.shape)], [normed, og, vecs]
    if first or last:
        specs, args = specs + [full], args + [mid]
    if not first:
        specs, args = specs + [full, full], args + list(so_far)
    if last:
        mixes, probs, qkvs, prefix_kv = back
        specs = specs + tie_specs([*mixes, *probs, *qkvs]) + [pl.BlockSpec((PW, model), lambda i: (0, 1))]
        args = args + [*mixes, *probs, *qkvs, prefix_kv]
    specs, args = specs + w_in.specs() + w_out.specs(), args + list(w_in.arrays) + list(w_out.arrays)
    scratch = w_in.scratch() + w_out.scratch()
    outs = [f32, f32]
    if last:
        specs, args = specs + w_proj.specs(), args + list(w_proj.arrays)
        scratch = scratch + w_proj.scratch()
        scratch = scratch + [
            pltpu.VMEM((length, model), bf16),
            pltpu.VMEM((length, model), bf16),
            pltpu.VMEM((model // HD * PW, length), bf16),
            pltpu.VMEM((length, model), bf16),
            pltpu.SemaphoreType.DMA((3,)),
        ]
        outs = [bf16, f32, bf16]
    out_specs = [full] * len(outs)
    out_shape = [jax.ShapeDtypeStruct((length, model), t) for t in outs]
    if last:
        out_specs = out_specs + [whole_spec((PW, model))] * 2
        out_shape = out_shape + [jax.ShapeDtypeStruct((PW, model), f32)] * 2
    return pl.pallas_call(
        tied(functools.partial(hidden_kernel, w_in, w_out, w_proj, chunk), len(ties)),
        grid=(length // BM,),
        in_specs=tie_specs(ties) + specs,
        out_specs=out_specs,
        out_shape=out_shape,
        scratch_shapes=scratch,
        compiler_params=params(LIMIT),
        cost_estimate=cost(25 if last else 15),
        name="hidden_part",
    )(*ties, *args)


def spans(length):
    out, at = [], 0
    for first in range(0, length, BQ):
        key = max(0, first - SPAN)
        keys = PW + first + BQ - key
        out.append((first, key, keys, at))
        at += keys
    return out, at


def mask_kernel(length, prefix, seg_ref, valid_ref, o_ref):
    keyed = jnp.where(valid_ref[...] > 0, seg_ref[...], -1).astype(f32)
    columns = [jnp.broadcast_to(keyed[:, i : i + BQ], (BQ, BQ)).T for i in range(0, length, BQ)]
    column = jnp.concatenate(columns, 0)
    for first, key, keys, at in spans(length)[0]:
        n = keys - PW
        pad = lax.broadcasted_iota(jnp.int32, (PW, BQ), 0) < prefix
        o_ref[pl.ds(at, PW), :] = jnp.where(pad, 0.0, NEG)
        key_at = key + lax.broadcasted_iota(jnp.int32, (n, BQ), 0)
        query_at = first + lax.broadcasted_iota(jnp.int32, (n, BQ), 1)
        seen = (column[key : key + n] == seg_ref[:, pl.ds(first, BQ)].astype(f32)) & (key_at <= query_at)
        o_ref[pl.ds(at + PW, n), :] = jnp.where(seen, 0.0, NEG)


def mask_bias(seg, valid, prefix, ties=()):
    length = seg.shape[1]
    total = spans(length)[1]
    return pl.pallas_call(
        tied(functools.partial(mask_kernel, length, prefix), len(ties)),
        grid=(1,),
        in_specs=tie_specs(ties) + [whole_spec((1, length))] * 2,
        out_specs=whole_spec((total, BQ)),
        out_shape=jax.ShapeDtypeStruct((total, BQ), f32),
        compiler_params=params(LIMIT),
        cost_estimate=cost(2),
        name="mask_bias",
    )(*ties, seg, valid)


def first_norm_kernel(x_ref, v_ref, o_ref):
    model = x_ref.shape[1]
    normed = norm(x_ref[...].astype(f32))[0]
    o_ref[...] = (normed * row_of(v_ref, GAIN1, model) + row_of(v_ref, SHIFT1, model)).astype(bf16)


def first_norm(x, vecs, ties=()):
    length, model = x.shape
    return pl.pallas_call(
        tied(first_norm_kernel, len(ties)),
        grid=(length // BM,),
        in_specs=tie_specs(ties) + [rows_spec(model), whole_spec(vecs.shape)],
        out_specs=rows_spec(model),
        out_shape=jax.ShapeDtypeStruct((length, model), bf16),
        compiler_params=params(LIMIT),
        cost_estimate=cost(4.5),
        name="first_norm",
    )(*ties, x, vecs)


def of_head(shape, head):
    lane = lax.broadcasted_iota(jnp.int32, shape, 1)
    return (lane >= HD * head) & (lane < HD * (head + 1))


def stack_heads(q):
    return jnp.concatenate([jnp.where(of_head(q.shape, h), q, jnp.zeros_like(q)) for h in range(HEADS)], 0)


def pick_heads(o):
    out = o[:BQ]
    for h in range(1, HEADS):
        out = jnp.where(of_head(out.shape, h), o[h * BQ : (h + 1) * BQ], out)
    return out


def attend_kernel(length, group, w, collect, *refs):
    (x_ref, v_ref, bias_ref), refs = refs[:3], refs[3:]
    if not collect:
        kv_ref, refs = refs[0], refs[1:]
    wr, refs = refs[: w.count()], refs[w.count() :]
    (qkv_ref, o_ref, p_ref, pp_ref), refs = refs[:4], refs[4:]
    if collect:
        kv_ref, refs = refs[0], refs[1:]
    whole, sem = refs[:2]
    plan = spans(length)[0]
    step = pl.program_id(0)

    @pl.when(step == 0)
    def _():
        start_load(w, wr, whole, sem)
        if collect:
            start_collect(w, wr, kv_ref.shape[1], *refs[2:])
        wait_load(whole, sem)
        if collect:
            wait_load(*refs[2:])
            kv_ref[...] = refs[2][0]

    lane = pl.multiple_of((group * GROUP_STEPS + step) * LANES, LANES)
    pk = kv_ref[:, pl.ds(lane, LANES)]
    pv = kv_ref[:, pl.ds(kv_ref.shape[1] // 2 + lane, LANES)]

    at = pl.multiple_of(step * 3 * LANES, 3 * LANES)
    shift = row_of(v_ref, QKV_SHIFT, 3 * LANES, group * GROUP_STEPS * 3 * LANES + at)
    qkv_ref[...] = (dot(x_ref[...], whole[:, pl.ds(at, 3 * LANES)]) + shift).astype(bf16)

    def score(i):
        first, key, keys, _ = plan[i]
        q = qkv_ref[pl.ds(first, BQ), pl.ds(0, LANES)] * jnp.asarray(HD**-0.5, bf16)
        ks = jnp.concatenate([pk, qkv_ref[pl.ds(key, keys - PW), pl.ds(LANES, LANES)]], 0)
        return dot(ks, stack_heads(q), NT)

    def soft(i, s):
        first, _, keys, at = plan[i]
        s = s + jnp.concatenate([bias_ref[pl.ds(at, keys), :]] * HEADS, 1)
        e = jnp.exp(s - jnp.max(s, axis=0, keepdims=True))
        probs = (e * (1.0 / jnp.sum(e, axis=0, keepdims=True))).astype(bf16)
        p_ref[0, pl.ds(at, keys), :] = probs
        for h in range(HEADS):
            pp_ref[pl.ds(h * PW, PW), pl.ds(first, BQ)] = probs[:PW, h * BQ : (h + 1) * BQ]
        return probs

    def mix(i, probs):
        first, key, keys, _ = plan[i]
        vs = jnp.concatenate([pv, qkv_ref[pl.ds(key, keys - PW), pl.ds(2 * LANES, LANES)]], 0)
        o_ref[pl.ds(first, BQ), :] = pick_heads(dot(probs, vs, TN)).astype(bf16)

    n = len(plan)
    s, held = score(0), None
    for i in range(n):
        later = score(i + 1) if i + 1 < n else None
        probs = soft(i, s)
        if held is not None:
            mix(i - 1, held)
        s, held = later, probs
    mix(n - 1, held)


def start_collect(w, refs, cols, kv, sem):
    here = w.net.position()
    part = cols // 4
    for array in range(len(refs)):
        x, y, c = w.net.source(array, *here[1:])
        at = pl.multiple_of((2 * y + c) * part, part)
        pltpu.make_async_copy(
            refs[array].at[pl.ds(w.net.planes * w.block, PW), pl.ds(0, part)],
            kv.at[(x + here[1]) % 2, :, pl.ds(at, part)],
            sem,
        ).start()


def attend(group, x, w, vecs, prefix_kv, bias, ties=()):
    length, model = x.shape
    steps = w.cols // (3 * LANES)
    total = spans(length)[1]
    collect = prefix_kv is None
    kv_spec = whole_spec((PW, 2 * model))
    out_specs = [
        pl.BlockSpec((length, 3 * LANES), lambda i: (0, i)),
        pl.BlockSpec((length, LANES), lambda i: (0, i)),
        pl.BlockSpec((1, total, HEADS * BQ), lambda i: (i, 0, 0)),
        pl.BlockSpec((HEADS * PW, length), lambda i: (i, 0)),
    ]
    out_shape = [
        jax.ShapeDtypeStruct((length, w.cols), bf16),
        jax.ShapeDtypeStruct((length, steps * LANES), bf16),
        jax.ShapeDtypeStruct((steps, total, HEADS * BQ), bf16),
        jax.ShapeDtypeStruct((steps * HEADS * PW, length), bf16),
    ]
    scratch = w.scratch()
    if collect:
        out_specs.append(kv_spec)
        out_shape.append(jax.ShapeDtypeStruct((PW, 2 * model), bf16))
        scratch = scratch + [pltpu.VMEM((2, PW, 2 * model), bf16), pltpu.SemaphoreType.DMA]
    return pl.pallas_call(
        tied(functools.partial(attend_kernel, length, group, w, collect), len(ties)),
        grid=(steps,),
        in_specs=tie_specs(ties)
        + [whole_spec(x.shape), whole_spec(vecs.shape), whole_spec((total, BQ))]
        + ([] if collect else [kv_spec])
        + w.specs(),
        out_specs=out_specs,
        out_shape=out_shape,
        scratch_shapes=scratch,
        compiler_params=params(LIMIT),
        cost_estimate=cost(8 * steps),
        name="attend",
    )(*ties, x, vecs, bias, *([] if collect else [prefix_kv]), *w.arrays)


def prefix_specs(steps, first):
    return [pl.BlockSpec((PW, LANES), lambda i, at=at: (0, at + first + i)) for at in (0, steps)]


def attend_back_kernel(length, w, first, last, *refs):
    (qkv_ref, p_ref, pk_ref, pv_ref, do_ref), refs = refs[:5], refs[5:]
    if not first:
        gn_in, refs = refs[0], refs[1:]
    if last:
        (x_hbm, gm_hbm, v_ref), refs = refs[:3], refs[3:]
    wr, refs = refs[: w.count()], refs[w.count() :]
    if last:
        (out_ref, gn), refs = refs[:2], refs[2:]
    else:
        gn, refs = refs[0], refs[1:]
    ak, av, dqkv, whole, sem, io_sem = refs[:6]
    step, steps = pl.program_id(0), pl.num_programs(0)
    copies = [] if first else [pltpu.make_async_copy(gn_in, gn, io_sem.at[0])]
    if last:
        x_vm, gm_vm = refs[6:]
        copies.append(pltpu.make_async_copy(x_hbm, x_vm, io_sem.at[1]))
        copies.append(pltpu.make_async_copy(gm_hbm, gm_vm, io_sem.at[2]))

    @pl.when(step == 0)
    def _():
        start_load(w, wr, whole, sem)
        for copy in copies:
            copy.start()

    ak[...] = jnp.zeros_like(ak)
    av[...] = jnp.zeros_like(av)
    plan = spans(length)[0]

    def scores(i):
        first, key, keys, _ = plan[i]
        dos = stack_heads(do_ref[pl.ds(first, BQ), :])
        vs = jnp.concatenate([pv_ref[...], qkv_ref[pl.ds(key, keys - PW), pl.ds(2 * LANES, LANES)]], 0)
        return dos, dot(vs, dos, NT)

    def soft(i, dos, dp):
        _, _, keys, at = plan[i]
        probs = p_ref[0, pl.ds(at, keys), :]
        wide = probs.astype(f32)
        t = wide * dp
        return dos, probs, (t - wide * jnp.sum(t, axis=0, keepdims=True)).astype(bf16)

    def mix(i, dos, probs, ds):
        first, key, keys, _ = plan[i]
        n = keys - PW
        qs = stack_heads(qkv_ref[pl.ds(first, BQ), pl.ds(0, LANES)] * jnp.asarray(HD**-0.5, bf16))
        ks = jnp.concatenate([pk_ref[...], qkv_ref[pl.ds(key, n), pl.ds(LANES, LANES)]], 0)
        ak[pl.ds(key, n), :] += dot(ds[PW:], qs)
        av[pl.ds(key, n), :] += dot(probs[PW:], dos)
        dqkv[pl.ds(first, BQ), pl.ds(0, LANES)] = (pick_heads(dot(ds, ks, TN)) * HD**-0.5).astype(bf16)

    n = len(plan)
    s, held = scores(0), None
    for i in range(n):
        later = scores(i + 1) if i + 1 < n else None
        done = soft(i, *s)
        if held is not None:
            mix(i - 1, *held)
        s, held = later, done
    mix(n - 1, *held)
    dqkv[:, pl.ds(LANES, LANES)] = ak[...].astype(bf16)
    dqkv[:, pl.ds(2 * LANES, LANES)] = av[...].astype(bf16)

    @pl.when(step == 0)
    def _():
        wait_load(whole, sem)

    at = pl.multiple_of(step * 3 * LANES, 3 * LANES)
    part = dot(dqkv[...], whole[:, pl.ds(at, 3 * LANES)], NT)

    @pl.when(step == 0)
    def _():
        if first:
            gn[...] = part
        else:
            copies[0].wait()
            gn[...] += part

    @pl.when(step > 0)
    def _():
        gn[...] += part

    if last:

        @pl.when(step == steps - 1)
        def _():
            for copy in copies[-2:]:
                copy.wait()

            def rows(i, carry):
                at = pl.ds(pl.multiple_of(i * BM, BM), BM)
                back = norm_back(x_vm[at, :].astype(f32), row_of(v_ref, GAIN1, out_ref.shape[1]), gn[at, :])
                out_ref[at, :] = (gm_vm[at, :] + back).astype(bf16)
                return carry

            lax.fori_loop(0, length // BM, rows, 0)


def attend_back(group, qkv, probs, prefix_kv, do, so_far, w, rest=None, ties=()):
    length, model = do.shape
    steps = GROUP_STEPS
    total = spans(length)[1]
    first, last = so_far is None, rest is not None
    hbm = pl.BlockSpec(memory_space=pl.ANY)
    args = [qkv, probs, prefix_kv, prefix_kv, do]
    specs = [
        pl.BlockSpec((length, 3 * LANES), lambda i: (0, i)),
        pl.BlockSpec((1, total, HEADS * BQ), lambda i: (i, 0, 0)),
        *prefix_specs(GROUPS * steps, group * steps),
        pl.BlockSpec((length, LANES), lambda i: (0, group * steps + i)),
    ]
    if not first:
        args, specs = args + [so_far], specs + [hbm]
    if last:
        args, specs = args + list(rest), specs + [hbm, hbm, whole_spec(rest[2].shape)]
    scratch = [pltpu.VMEM((length, LANES), f32)] * 2 + [pltpu.VMEM((length, 3 * LANES), bf16)] + w.scratch()
    scratch = scratch + [pltpu.SemaphoreType.DMA((3,))]
    if last:
        scratch = [pltpu.VMEM((length, model), f32)] + scratch
        scratch = scratch + [pltpu.VMEM((length, model), bf16), pltpu.VMEM((length, model), f32)]
    return pl.pallas_call(
        tied(functools.partial(attend_back_kernel, length, w, first, last), len(ties)),
        grid=(steps,),
        in_specs=tie_specs(ties) + specs + w.specs(),
        out_specs=whole_spec((length, model)),
        out_shape=jax.ShapeDtypeStruct((length, model), bf16 if last else f32),
        scratch_shapes=scratch,
        compiler_params=params(LIMIT),
        cost_estimate=cost(17),
        name="attend_back",
    )(*ties, *args, *w.arrays)


def prefix_kernel(e_ref, w1_ref, b1_ref, w2_ref, b2_ref, h_ref, low_ref, kv_ref):
    rows, model = e_ref.shape
    emb = jnp.concatenate([e_ref[...].astype(f32), jnp.zeros((PW - rows, model), f32)], 0).astype(bf16)
    mid, cols = b1_ref.shape[0], b2_ref.shape[0]
    hidden = jnp.tanh(dot(emb, w1_ref[...], NT) + b1_ref[...].astype(f32).reshape(1, mid))
    low = hidden.astype(bf16)
    h_ref[...] = hidden
    low_ref[...] = low
    kv_ref[:, pl.ds(0, cols)] = (dot(low, w2_ref[...]) + b2_ref[...].astype(f32).reshape(1, cols)).astype(bf16)
    if cols < kv_ref.shape[1]:
        kv_ref[:, pl.ds(cols, kv_ref.shape[1] - cols)] = jnp.zeros((PW, kv_ref.shape[1] - cols), bf16)


def prefix_forward(emb, weight1, bias1, weight2, bias2, room):
    mid, cols = weight2.shape
    args = (emb, weight1, bias1, weight2, bias2)
    outs = [((PW, mid), f32), ((PW, mid), bf16), ((PW, max(cols, room)), bf16)]
    return pl.pallas_call(
        prefix_kernel,
        grid=(1,),
        in_specs=[whole_spec(a.shape) for a in args],
        out_specs=[whole_spec(shape) for shape, _ in outs],
        out_shape=[jax.ShapeDtypeStruct(*a) for a in outs],
        compiler_params=params(LIMIT),
        cost_estimate=cost(3),
        name="prefix_forward",
    )(*args)


def add_pairs(refs):
    if len(refs) == 1:
        return refs[0][...]
    return (refs[0][...] + refs[1][...]) + (refs[2][...] + refs[3][...])


def real_rows(values, rows):
    return jnp.where(lax.broadcasted_iota(jnp.int32, values.shape, 0) < rows, values, 0.0)


def add_terms(terms):
    def kernel(a_ref, b_ref, c_ref, d_ref, o_ref):
        o_ref[...] = (a_ref[...] + b_ref[...]) + (c_ref[...] + d_ref[...])

    spec = whole_spec(terms[0].shape)
    return pl.pallas_call(
        kernel,
        grid=(1,),
        in_specs=[spec] * 4,
        out_specs=spec,
        out_shape=jax.ShapeDtypeStruct(terms[0].shape, f32),
        compiler_params=params(LIMIT),
        cost_estimate=cost(1),
        name="add_terms",
    )(*terms)


def second_layer_kernel(n, rows, *refs):
    parts, (low_ref, w_ref, wg_ref, bg_ref, hg_ref) = refs[:n], refs[n:]
    kv = real_rows(add_pairs(parts), rows).astype(bf16)
    bg_ref[...] = jnp.sum(kv.astype(f32), axis=0)
    wg_ref[...] = dot(low_ref[...], kv, TN)
    hg_ref[...] = dot(kv, w_ref[...], NT)


def second_layer_back(parts, rows, hidden_low, weight):
    mid, cols = weight.shape
    args = (*parts, hidden_low, weight)
    shapes = [(mid, cols), (cols,), (PW, mid)]
    return pl.pallas_call(
        functools.partial(second_layer_kernel, len(parts), rows),
        grid=(1,),
        in_specs=[whole_spec(a.shape) for a in args],
        out_specs=[whole_spec(a) for a in shapes],
        out_shape=[jax.ShapeDtypeStruct(a, f32) for a in shapes],
        compiler_params=params(LIMIT),
        cost_estimate=cost(3),
        name="second_layer_back",
    )(*args)


def first_layer_kernel(n, *refs):
    parts, (hidden_ref, e_ref, w_ref, wg_ref, bg_ref, eg_ref) = refs[:n], refs[n:]
    hidden = hidden_ref[...]
    low = real_rows(add_pairs(parts) * (1.0 - hidden * hidden), e_ref.shape[0]).astype(bf16)
    bg_ref[...] = jnp.sum(low.astype(f32), axis=0)
    rows, model = e_ref.shape
    emb = jnp.concatenate([e_ref[...].astype(f32), jnp.zeros((PW - rows, model), f32)], 0).astype(bf16)
    wg_ref[...] = dot(low, emb, TN)
    eg_ref[...] = dot(low, w_ref[...])[:rows]


def first_layer_back(parts, hidden, emb, weight):
    mid, model = weight.shape
    shapes = [(mid, model), (mid,), emb.shape]
    args = (*parts, hidden, emb, weight)
    return pl.pallas_call(
        functools.partial(first_layer_kernel, len(parts)),
        grid=(1,),
        in_specs=[whole_spec(a.shape) for a in args],
        out_specs=[whole_spec(a) for a in shapes],
        out_shape=[jax.ShapeDtypeStruct(a, f32) for a in shapes],
        compiler_params=params(LIMIT),
        cost_estimate=cost(4),
        name="first_layer_back",
    )(*args)


def after(value, *others):
    return lax.optimization_barrier((value, *others))[0]


class Plain:
    def position(self):
        return ()

    def gather(self, shard):
        whole = lax.all_gather(shard, ALL, axis=0, tiled=True)
        rows, cols = whole.shape
        return Weight(self, [whole], rows, [(0, 0, lambda: 0)], rows, cols)

    def sum_columns(self, keys, values):
        part = jnp.concatenate([keys, values], 1)
        return [lax.psum_scatter(lax.psum(part, "rows"), "pre", scatter_dimension=1, tiled=True)]

    def over_pre(self, part):
        return [lax.psum(part, "pre")]


class Grid:
    planes = 4

    def __init__(self):
        self.places = [(z, x, y, c) for z in range(4) for x in range(2) for y in range(2) for c in range(2)]

    def position(self):
        rows, pre = lax.axis_index("rows"), lax.axis_index("pre")
        return rows // 2, rows % 2, pre // 2, pre % 2

    @staticmethod
    def number(z, x, y, c):
        return z * 8 + x * 4 + y * 2 + c

    @staticmethod
    def side(x, y, c, second):
        along_x = (c + second + 1) % 2
        return (x + along_x) % 2, (y + 1 - along_x) % 2

    def send(self, value, where):
        return lax.ppermute(value, ALL, [(self.number(*p), self.number(*where(*p))) for p in self.places])

    def plane(self, block, k):
        return self.send(block, lambda z, x, y, c: (z ^ k, x, y, c))

    def planes_of(self, block):
        return [self.plane(block, k) for k in range(1, self.planes)]

    def line_in_order(self, block):
        groups = [[self.number(z, x, y, c) for z in range(4)] for x in range(2) for y in range(2) for c in range(2)]
        return lax.all_gather(block, ALL, axis=0, tiled=True, axis_index_groups=groups)

    def beside(self, value, second):
        return self.send(value, lambda z, x, y, c: (z, *self.side(x, y, c, second), c))

    def core(self, value):
        return self.send(value, lambda z, x, y, c: (z, x, y, 1 - c))

    def source(self, array, x, y, c):
        if array >= 4:
            c = 1 - c
        if array % 4 >= 2:
            x, y = self.side(x, y, c, 1)
        if array % 2:
            x, y = self.side(x, y, c, 0)
        return x, y, c

    def arrays_of(self, line, near, far, end):
        own = [line, near, far, end]
        return own + [self.core(a) for a in own]

    def weight(self, arrays, rows, cols, at=0):
        def place(array, k):
            return lambda z, x, y, c: rows * self.number(z ^ k, *self.source(array, x, y, c))

        pieces = [(a, k * rows, place(a, k)) for a in range(8) for k in range(4)]
        return Weight(self, arrays, rows, pieces, rows * len(self.places), cols, at)

    def hidden_weights(self, arrays, rows_in, rows_out):
        devices, cols = len(self.places), arrays[0].shape[1]

        def inner(array, k):
            return lambda z, x, y, c: rows_in * self.number(k, *self.source(array, x, y, c))

        def outer(array):
            return lambda z, x, y, c: rows_out * self.number(0, *self.source(array, x, y, c))

        return (
            Weight(
                self,
                arrays,
                rows_in,
                [(a, rows_out + rows_in * k, inner(a, k)) for a in range(8) for k in range(4)],
                rows_in * devices,
                cols,
            ),
            Weight(self, arrays, rows_out, [(a, 0, outer(a)) for a in range(8)], rows_out * devices // 4, cols),
        )

    def sum_cores(self, keys, values):
        _, _, y, c = self.position()
        half = keys.shape[1] // 2
        both = jnp.stack([keys, values])
        low, high = both[:, :, :half], both[:, :, half:]
        both = jnp.where(c == 0, low, high) + self.core(jnp.where(c == 0, high, low))
        return jnp.where(y == 0, both[0], both[1]), jnp.where(y == 0, both[1], both[0])

    def send_across(self, mine, other):
        along_x = self.send(mine, lambda z, x, y, c: (z, 1 - x, y, c))
        along_y = self.send(other, lambda z, x, y, c: (z, x, 1 - y, c))
        across = self.send(other, lambda z, x, y, c: (z, 1 - x, 1 - y, c))
        return [mine, along_x, along_y, across]

    def over_pre(self, part):
        along = self.send(part, lambda z, x, y, c: (z, x, 1 - y, c))
        across = self.send(part, lambda z, x, y, c: (z, x, 1 - y, 1 - c))
        return [part, self.core(part), along, across]


def per_device(
    tokens,
    seg_ids,
    valid,
    out_grad,
    ln1_gain,
    ln1_bias,
    qkv_weight,
    qkv_bias,
    proj_weight,
    proj_bias,
    ln2_gain,
    ln2_bias,
    fc_weight,
    fc_bias,
    out_weight,
    out_bias,
    prefix_emb,
    rep_weight1,
    rep_bias1,
    rep_weight2,
    rep_bias2,
):
    x, og = tokens[0], out_grad[0]
    model = x.shape[1]
    hidden_units = fc_weight.shape[1]
    prefix_len = prefix_emb.shape[0]
    own_q, own_o = qkv_weight.shape[0], out_weight.shape[0]
    width = hidden_units // CHUNKS
    part = model // GROUPS
    on_grid = (lax.axis_size("rows"), lax.axis_size("pre")) == (8, 4)
    net = Grid() if on_grid else Plain()

    def step_starts(g):
        return [i * model + g * part + k * LANES for k in range(GROUP_STEPS) for i in range(3)]

    def by_step(g):
        return [(0, k * LANES, 0, 0, at, own_q, LANES) for k, at in enumerate(step_starts(g))]

    second = by_step(1) + [(0, 3 * part, 1, 0, 0, own_q, model)]
    (shard,) = arrange(
        [((own_q, 6 * part + model), by_step(0) + [(0, 3 * part + at, *rest) for _, at, *rest in second])],
        qkv_weight,
        proj_weight,
    )
    if on_grid:
        others = net.planes_of(shard)
    starts = [at for g in range(GROUPS) for at in step_starts(g)]
    one = [(0, 0, model)]
    vecs = pack(
        [(GAIN1, one), (SHIFT1, one), (GAIN2, one), (SHIFT2, one), (PROJ_SHIFT, one), (OUT_SHIFT, one)]
        + [(QKV_SHIFT, [(k * LANES, at, LANES) for k, at in enumerate(starts)]), (FC_SHIFT, [(0, 0, hidden_units)])],
        hidden_units,
        ln1_gain,
        ln1_bias,
        ln2_gain,
        ln2_bias,
        proj_bias,
        out_bias,
        qkv_bias,
        fc_bias,
    )
    hidden, hidden_low, kv_local = prefix_forward(
        prefix_emb, rep_weight1.T, rep_bias1, rep_weight2, rep_bias2, 3 * part if on_grid else 0
    )

    def run_hidden(j, so_far, normed2, w_in, w_out, ties=()):
        back = (mixes, pprobs, qkvs, prefix_kv)
        w_last = w_proj if j == CHUNKS - 1 else None
        return hidden_part(j, normed2, og, vecs, mid, so_far, w_in, w_out, w_last, back, ties)

    so_far = None
    if not on_grid:
        prefix_kv = lax.all_gather(kv_local, "pre", axis=1, tiled=True)
        w_qkv = [net.gather(shard[:, g * 3 * part : (g + 1) * 3 * part]) for g in range(GROUPS)]
        w_proj = net.gather(proj_weight)
        out_all = lax.all_gather(out_weight, ALL, axis=0, tiled=True)
        normed1, bias = first_norm(x, vecs), mask_bias(seg_ids, valid, prefix_len)
        qkvs, mixes, probs, pprobs = zip(
            *[attend(g, normed1, w_qkv[g], vecs, prefix_kv, bias) for g in range(GROUPS)], strict=True
        )
        mid, normed2 = middle_block(mixes, x, w_proj, vecs)
        for j in range(CHUNKS):
            w_in = net.gather(fc_weight[:, j * width : (j + 1) * width])
            w_out = Weight(net, [out_all], width, [(0, j * width, lambda: 0)], width, model)
            so_far = run_hidden(j, so_far, normed2, w_in, w_out)
    else:
        own_h = own_o + CHUNKS * own_q

        def send_lines(parts, ties):
            return arrange(
                [
                    (
                        (own_o + net.planes * own_q, model),
                        [(0, 0, 0, j * own_h, 0, own_o, model)]
                        + [
                            (own_o + z * own_q, 0, 0, z * own_h + own_o + j * own_q, 0, own_q, model)
                            for z in range(net.planes)
                        ],
                    )
                    for j in parts
                ],
                line_h,
                ties=ties,
            )

        rows, wide = net.planes * own_q, 3 * part + model
        (line_a,) = arrange(
            [
                (
                    (rows + PW, 3 * part),
                    [(k * own_q, 0, k, 0, 0, own_q, 3 * part) for k in range(net.planes)]
                    + [(rows, 0, net.planes, 0, 0, PW, 3 * part)],
                ),
            ],
            shard,
            *others,
            kv_local,
        )
        (shard_h,) = arrange(
            [
                (
                    (own_o + CHUNKS * own_q, model),
                    [(0, 0, 0, 0, 0, own_o, model)]
                    + [(own_o + j * own_q, 0, 1, 0, j * width, own_q, width) for j in range(CHUNKS)],
                )
            ],
            out_weight,
            fc_weight,
            ties=(line_a,),
        )
        line_h = net.line_in_order(shard_h)
        near_a, far_a = net.beside(line_a, False), net.beside(line_a, True)
        normed1 = first_norm(x, vecs, (line_a,))
        end_a = net.beside(near_a, True)
        bias = mask_bias(seg_ids, valid, prefix_len, (normed1,))
        (line_b,) = arrange(
            [((rows, wide), [(k * own_q, 0, k, 0, 3 * part, own_q, wide) for k in range(net.planes)])],
            shard,
            *others,
            ties=(near_a, far_a, bias),
        )
        near_b, far_b = net.beside(line_b, False), net.beside(line_b, True)
        end_b = net.beside(near_b, True)
        w_a = net.weight(net.arrays_of(line_a, near_a, far_a, end_a), own_q, 3 * part)
        qkv_a, mix_a, probs_a, pprobs_a, prefix_kv = attend(0, normed1, w_a, vecs, None, bias, (near_b,))
        far_b, end_b = gate((far_b, end_b), (mix_a,))
        lines = list(send_lines((0, 1), (far_b, end_b)))
        arrays_b = net.arrays_of(line_b, near_b, far_b, end_b)
        w_b, w_proj = net.weight(arrays_b, own_q, 3 * part), net.weight(arrays_b, own_q, model, 3 * part)
        nears = [net.beside(a, False) for a in lines]
        fars = [net.beside(a, True) for a in lines]
        qkv_b, mix_b, probs_b, pprobs_b = attend(1, normed1, w_b, vecs, prefix_kv, bias, tuple(lines))
        ends = [net.beside(after(a, mix_b), True) for a in nears]
        mid, normed2 = middle_block([mix_a, mix_b], x, w_proj, vecs, tuple(nears))
        lines += send_lines((2, 3), (mid, ends[0]))
        nears += [net.beside(a, False) for a in lines[2:]]
        fars += [net.beside(a, True) for a in lines[2:]]
        w_qkv, qkvs, probs = [w_a, w_b], [qkv_a, qkv_b], [probs_a, probs_b]
        mixes, pprobs = [mix_a, mix_b], [pprobs_a, pprobs_b]
        latest = mid
        for j in range(CHUNKS):
            arrays = net.arrays_of(lines[j], nears[j], after(fars[j], latest), after(ends[j], latest))
            w_in, w_out = net.hidden_weights(arrays, own_q, own_o)
            ties = tuple(lines[2:]) if j == 0 else ()
            if 0 < j < CHUNKS - 1:
                ends.append(net.beside(after(nears[j + 1], latest), True))
                ties = (nears[j + 1],)
            so_far = run_hidden(j, so_far, normed2, w_in, w_out, ties)
            latest = so_far[0]
    output, grad_mid, grad_attn, dpk, dpv = so_far
    rest = (x, grad_mid, vecs)
    if on_grid:
        mine, other = net.sum_cores(dpk, dpv)
        terms = net.send_across(mine, other)
        so_far = attend_back(0, qkvs[0], probs[0], prefix_kv, grad_attn, None, w_qkv[0], ties=(mine, other))
        plane = add_terms(terms)
        sums = [plane, *net.planes_of(plane)]
        in_grad = attend_back(1, qkvs[1], probs[1], prefix_kv, grad_attn, so_far, w_qkv[1], rest, ties=(plane,))
    else:
        sums = net.sum_columns(dpk, dpv)
        so_far = attend_back(0, qkvs[0], probs[0], prefix_kv, grad_attn, None, w_qkv[0])
        in_grad = attend_back(1, qkvs[1], probs[1], prefix_kv, grad_attn, so_far, w_qkv[1], rest)
    weight2_grad, bias2_grad, hid_grad = second_layer_back(sums, prefix_len, hidden_low, rep_weight2)
    hid_grads = net.over_pre(hid_grad)
    weight1_grad, bias1_grad, emb_grad = first_layer_back(hid_grads, hidden, prefix_emb, rep_weight1.T)
    return output[None], in_grad[None], emb_grad, weight1_grad.T, bias1_grad, weight2_grad, bias2_grad


def solution(mesh):
    split_all = P(ALL, None)
    whole = P()
    return jax.shard_map(
        per_device,
        mesh=mesh,
        in_specs=(
            P(ALL, None, None),
            split_all,
            split_all,
            P(ALL, None, None),
            whole,
            whole,
            split_all,
            whole,
            split_all,
            whole,
            whole,
            whole,
            split_all,
            whole,
            split_all,
            whole,
            whole,
            whole,
            whole,
            P(None, "pre"),
            P("pre"),
        ),
        out_specs=(
            P(ALL, None, None),
            P(ALL, None, None),
            whole,
            whole,
            whole,
            P(None, "pre"),
            P("pre"),
        ),
        check_vma=False,
    )
```

```python
import functools

import jax
import jax.numpy as jnp
from jax import lax
from jax.experimental import pallas as pl
from jax.experimental.pallas import tpu as pltpu
from jax.sharding import PartitionSpec as P

f32 = jnp.float32
bf16 = jnp.bfloat16
ALL = ("rows", "pre")
NEG = -1e30
EPS = 1e-05
HD = 64
SPAN = 256
BQ = 128
PW = 16
LANES = 256
HEADS = LANES // HD
GROUPS = 2
GROUP_STEPS = 2
CHUNKS = 4
BM = 256
BIG = 512
LIMIT = 58
ROOM = 52
SUB = 256

NN = (((1,), (0,)), ((), ()))
NT = (((1,), (1,)), ((), ()))
TN = (((0,), (0,)), ((), ()))


def dot(a, b, dims=NN):
    return lax.dot_general(a, b, dims, preferred_element_type=f32)


def params(mebibytes):
    return pltpu.CompilerParams(vmem_limit_bytes=mebibytes << 20)


def cost(microseconds):
    return pl.CostEstimate(flops=int(microseconds * 1.65e+08), bytes_accessed=1, transcendentals=0)


class Weight:
    def __init__(self, net, arrays, block, pieces, rows, cols, at=0):
        self.net, self.arrays, self.block, self.pieces = net, arrays, block, pieces
        self.rows, self.cols, self.at = rows, cols, at

    def specs(self):
        return [pl.BlockSpec(memory_space=pl.ANY) for _ in self.arrays]

    def count(self):
        return len(self.arrays)

    def scratch(self):
        return [pltpu.VMEM((self.rows, self.cols), bf16), pltpu.SemaphoreType.DMA]


def start_load(w, refs, whole, sem, at=0, cols=None):
    cols = cols or w.cols
    here = w.net.position()
    for array, row, place in w.pieces:
        first = pl.multiple_of(place(*here), w.block)
        pltpu.make_async_copy(
            refs[array].at[pl.ds(row, w.block), pl.ds(w.at + at, cols)],
            whole.at[pl.ds(first, w.block), pl.ds(at, cols)],
            sem,
        ).start()


def wait_load(whole, sem):
    pltpu.make_async_copy(whole, whole, sem).wait()


def tied(kernel, count):
    return lambda *refs: kernel(*refs[count:])


def tie_specs(ties):
    return [pl.BlockSpec(memory_space=pl.ANY)] * len(ties)


def arrange(plan, *arrays, ties=()):
    def kernel(*refs):
        ins, outs, sems = refs[: len(arrays)], refs[len(arrays) + len(ties) : -1], refs[-1]
        for k, (_, parts) in enumerate(plan):
            for row, col, array, from_row, from_col, rows, cols in parts:
                pltpu.make_async_copy(
                    ins[array].at[pl.ds(from_row, rows), pl.ds(from_col, cols)],
                    outs[k].at[pl.ds(row, rows), pl.ds(col, cols)],
                    sems.at[k],
                ).start()
        for k in range(len(plan)):
            pltpu.make_async_copy(outs[k], outs[k], sems.at[k]).wait()

    return pl.pallas_call(
        kernel,
        grid=(1,),
        in_specs=[pl.BlockSpec(memory_space=pl.ANY)] * (len(arrays) + len(ties)),
        out_specs=[whole_spec(shape) for shape, _ in plan],
        out_shape=[jax.ShapeDtypeStruct(shape, bf16) for shape, _ in plan],
        scratch_shapes=[pltpu.SemaphoreType.DMA((len(plan),))],
        compiler_params=params(LIMIT),
        cost_estimate=cost(0),
        name="arrange",
    )(*arrays, *ties)


def gate(arrays, ties):
    n = len(arrays)
    spec = pl.BlockSpec(memory_space=pl.ANY)
    return pl.pallas_call(
        lambda *refs: None,
        grid=(1,),
        in_specs=[spec] * (n + len(ties)),
        out_specs=[spec] * n,
        out_shape=[jax.ShapeDtypeStruct(a.shape, a.dtype) for a in arrays],
        input_output_aliases={i: i for i in range(n)},
        compiler_params=params(LIMIT),
        cost_estimate=cost(1),
        name="gate",
    )(*arrays, *ties)


def join(*arrays, ties=()):
    parts, at = [], 0
    for k, a in enumerate(arrays):
        parts.append((at, 0, k, 0, 0, *a.shape))
        at += a.shape[0]
    return arrange([((at, arrays[0].shape[1]), parts)], *arrays, ties=ties)[0]


GAIN1, SHIFT1, GAIN2, SHIFT2, PROJ_SHIFT, OUT_SHIFT, QKV_SHIFT, FC_SHIFT = range(8)


def pack_kernel(plan, *refs):
    out = refs[-1]
    out[...] = jnp.zeros_like(out)
    for ref, row in zip(refs[:-1], plan, strict=True):
        for at, start, size in row[1]:
            out[pl.ds(row[0], 1), pl.ds(at, size)] = ref[pl.ds(start, size)].astype(f32).reshape(1, size)


def pack(plan, width, *vectors):
    return pl.pallas_call(
        functools.partial(pack_kernel, plan),
        grid=(1,),
        in_specs=[whole_spec(v.shape) for v in vectors],
        out_specs=whole_spec((8, width)),
        out_shape=jax.ShapeDtypeStruct((8, width), f32),
        compiler_params=params(LIMIT),
        cost_estimate=cost(0),
        name="pack",
    )(*vectors)


def row_of(ref, row, size, at=0):
    return ref[pl.ds(row, 1), pl.ds(at, size)]


def norm(values):
    center = values - jnp.mean(values, axis=-1, keepdims=True)
    rate = lax.rsqrt(jnp.mean(center * center, axis=-1, keepdims=True) + EPS)
    return center * rate, rate


def norm_back(values, gain, grad):
    n, rate = norm(values)
    w = grad * gain
    return rate * (
        w - jnp.mean(w, axis=-1, keepdims=True) - n * jnp.mean(w * n, axis=-1, keepdims=True)
    )


def rows_spec(cols, at=0, rows=None):
    return pl.BlockSpec((rows or BM, cols), lambda i: (i, at))


def whole_spec(shape):
    return pl.BlockSpec(shape, lambda i: (0,) * len(shape))


def middle_kernel(w, *refs):
    parts, (x_ref, v_ref), refs = refs[:GROUPS], refs[GROUPS : GROUPS + 2], refs[GROUPS + 2 :]
    wr = refs[: w.count()]
    mid_ref, n_ref, whole, sem = refs[w.count() :]
    model = w.cols

    @pl.when(pl.program_id(0) == 0)
    def _():
        start_load(w, wr, whole, sem)
        wait_load(whole, sem)

    attn = jnp.concatenate([p[...] for p in parts], 1)
    mid = x_ref[...].astype(f32) + (dot(attn, whole[...]) + row_of(v_ref, PROJ_SHIFT, model))
    mid_ref[...] = mid.astype(bf16)
    n_ref[...] = (norm(mid)[0] * row_of(v_ref, GAIN2, model) + row_of(v_ref, SHIFT2, model)).astype(bf16)


def middle_block(parts, x, w, vecs, ties=()):
    length, model = x.shape
    return pl.pallas_call(
        tied(functools.partial(middle_kernel, w), len(ties)),
        grid=(length // BIG,),
        in_specs=tie_specs(ties) + [rows_spec(p.shape[1], rows=BIG) for p in parts] + [rows_spec(model, rows=BIG), whole_spec(vecs.shape)] + w.specs(),
        out_specs=[rows_spec(model, rows=BIG)] * 2,
        out_shape=[
            jax.ShapeDtypeStruct((length, model), bf16),
            jax.ShapeDtypeStruct((length, model), bf16),
        ],
        scratch_shapes=w.scratch(),
        compiler_params=params(ROOM),
        cost_estimate=cost(8.5),
        name="middle_block",
    )(*ties, *parts, x, vecs, *w.arrays)


def gelu_both(v):
    c, a = 0.7978845608, 0.044715
    sq = v * v
    t = jnp.tanh(v * (c + (c * a) * sq))
    half = 0.5 + 0.5 * t
    act = v * half
    slope = half + (0.5 * v) * (1.0 - t * t) * (c + (3.0 * c * a) * sq)
    return act, slope


def hidden_kernel(w_in, w_out, w_proj, chunk, *refs):
    refs = list(refs)
    first, last = chunk == 0, w_proj is not None
    model, width = w_in.rows, w_in.cols
    (n_ref, og_ref, v_ref), refs = refs[:3], refs[3:]
    if first or last:
        mid_ref = refs.pop(0)
    if not first:
        (out_in, gn_in), refs = refs[:2], refs[2:]
    if last:
        back, refs = refs[: BACK_REFS], refs[BACK_REFS:]
    wi, refs = refs[: w_in.count()], refs[w_in.count() :]
    wo, refs = refs[: w_out.count()], refs[w_out.count() :]
    if last:
        wp, refs = refs[: w_proj.count()], refs[w_proj.count() :]
        (out_ref, gm_ref, ga_ref, dp_ref), refs = refs[:4], refs[4:]
    else:
        (out_ref, gn_ref), refs = refs[:2], refs[2:]
    fc, fc_sem, ow, ow_sem = refs[:4]

    @pl.when(pl.program_id(0) == 0)
    def _():
        start_load(w_in, wi, fc, fc_sem)
        start_load(w_out, wo, ow, ow_sem)
        if last:
            start_load(w_proj, wp, refs[4], refs[5])
            start_back(back, refs[6:11])
        wait_load(fc, fc_sem)
        wait_load(ow, ow_sem)
        if last:
            wait_load(refs[4], refs[5])

    normed, og = n_ref[...], og_ref[...]
    acts, grads = [], []
    for j in range(0, width, SUB):
        at = pl.ds(j, SUB)
        act, slope = gelu_both(dot(normed, fc[:, at]) + row_of(v_ref, FC_SHIFT, SUB, chunk * width + j))
        acts.append(act.astype(bf16))
        grads.append((dot(og, ow[at, :], NT) * slope).astype(bf16))
    out = dot(jnp.concatenate(acts, 1), ow[...])
    gn = dot(jnp.concatenate(grads, 1), fc[...], NT)
    if first:
        out = out + (mid_ref[...].astype(f32) + row_of(v_ref, OUT_SHIFT, model))
    else:
        out = out + out_in[...].astype(f32)
        gn = gn + gn_in[...].astype(f32)
    out_ref[...] = out.astype(out_ref.dtype)
    if last:
        gm = og.astype(f32) + norm_back(mid_ref[...].astype(f32), row_of(v_ref, GAIN2, model), gn)
        low = gm.astype(bf16)
        gm_ref[...] = low
        ga = dot(low, refs[4][...], NT).astype(bf16)
        ga_ref[...] = ga
        refs[9][pl.ds(pl.multiple_of(pl.program_id(0) * BM, BM), BM), :] = ga

        @pl.when(pl.program_id(0) == pl.num_programs(0) - 1)
        def _():
            finish_back(back[-1], dp_ref, refs[6:11])
    else:
        gn_ref[...] = gn.astype(bf16)


BACK_REFS = 2 * GROUPS + GROUPS + 1


def start_back(refs, scratch):
    mixes, probs, qkvs = refs[:GROUPS], refs[GROUPS : 2 * GROUPS], refs[2 * GROUPS : 3 * GROUPS]
    q_all, mix_all, p_all, _, sems = scratch[:5]
    wide = GROUP_STEPS * LANES
    for g in range(GROUPS):
        rows = probs[g].shape[0]
        pltpu.make_async_copy(probs[g], p_all.at[pl.ds(g * rows, rows)], sems.at[0]).start()
        pltpu.make_async_copy(mixes[g], mix_all.at[:, pl.ds(g * wide, wide)], sems.at[1]).start()
        for k in range(GROUP_STEPS):
            pltpu.make_async_copy(
                qkvs[g].at[:, pl.ds(3 * LANES * k, LANES)], q_all.at[:, pl.ds(g * wide + k * LANES, LANES)], sems.at[2]
            ).start()


def own_head(rows, each, model):
    head = lax.broadcasted_iota(jnp.int32, (rows, model), 0) // each
    return head == lax.broadcasted_iota(jnp.int32, (rows, model), 1) // HD


def finish_back(pv_ref, dp_ref, scratch):
    q_all, mix_all, p_all, do_all, sems = scratch
    for k, ref in enumerate((p_all, mix_all, q_all)):
        pltpu.make_async_copy(ref, ref, sems.at[k]).wait()
    model = do_all.shape[1]
    heads = model // HD
    do = do_all[...]
    own = own_head(heads * PW, PW, model)
    pv = jnp.concatenate([pv_ref[...]] * heads, 0)
    dp = dot(jnp.where(own, pv, jnp.zeros_like(pv)), do, NT)
    ones = jnp.where(own_head(heads, 1, model), 1.0, 0.0).astype(bf16)
    delta = dot(ones, (do.astype(f32) * mix_all[...].astype(f32)).astype(bf16), NT)
    delta = jnp.concatenate([jnp.broadcast_to(delta[h : h + 1], (PW, delta.shape[1])) for h in range(heads)], 0)
    p = p_all[...]
    ds = (p.astype(f32) * (dp - delta)).astype(bf16)
    for k, (total, scale) in enumerate(((dot(ds, q_all[...]), HD**-0.5), (dot(p, do), 1.0))):
        kept = jnp.where(own, total, 0.0)
        dp_ref[k] = sum(kept[h * PW : (h + 1) * PW] for h in range(heads)) * scale


def hidden_part(chunk, normed, og, vecs, mid, so_far, w_in, w_out, w_proj, back, ties=()):
    length, model = og.shape
    first, last = chunk == 0, w_proj is not None
    full = rows_spec(model)
    specs, args = [full, full, whole_spec(vecs.shape)], [normed, og, vecs]
    if first or last:
        specs, args = specs + [full], args + [mid]
    if not first:
        specs, args = specs + [full, full], args + list(so_far)
    if last:
        mixes, probs, qkvs, prefix_kv = back
        specs = specs + tie_specs([*mixes, *probs, *qkvs]) + [pl.BlockSpec((PW, model), lambda i: (0, 1))]
        args = args + [*mixes, *probs, *qkvs, prefix_kv]
    specs, args = specs + w_in.specs() + w_out.specs(), args + list(w_in.arrays) + list(w_out.arrays)
    scratch = w_in.scratch() + w_out.scratch()
    outs = [bf16, bf16]
    if last:
        specs, args = specs + w_proj.specs(), args + list(w_proj.arrays)
        scratch = scratch + w_proj.scratch()
        scratch = scratch + [
            pltpu.VMEM((length, model), bf16),
            pltpu.VMEM((length, model), bf16),
            pltpu.VMEM((model // HD * PW, length), bf16),
            pltpu.VMEM((length, model), bf16),
            pltpu.SemaphoreType.DMA((3,)),
        ]
        outs = [bf16, bf16, bf16]
    out_specs = [full] * len(outs)
    out_shape = [jax.ShapeDtypeStruct((length, model), t) for t in outs]
    if last:
        out_specs = out_specs + [whole_spec((2, PW, model))]
        out_shape = out_shape + [jax.ShapeDtypeStruct((2, PW, model), f32)]
    return pl.pallas_call(
        tied(functools.partial(hidden_kernel, w_in, w_out, w_proj, chunk), len(ties)),
        grid=(length // BM,),
        in_specs=tie_specs(ties) + specs,
        out_specs=out_specs,
        out_shape=out_shape,
        scratch_shapes=scratch,
        compiler_params=params(ROOM),
        cost_estimate=cost(25 if last else 15),
        name="hidden_part",
    )(*ties, *args)


def spans(length):
    out, at = [], 0
    for first in range(0, length, BQ):
        key = max(0, first - SPAN)
        keys = PW + first + BQ - key
        out.append((first, key, keys, at))
        at += keys
    return out, at


def mask_kernel(length, prefix, seg_ref, valid_ref, o_ref):
    keyed = jnp.where(valid_ref[...] > 0, seg_ref[...], -1).astype(f32)
    columns = [jnp.broadcast_to(keyed[:, i : i + BQ], (BQ, BQ)).T for i in range(0, length, BQ)]
    column = jnp.concatenate(columns, 0)
    for first, key, keys, at in spans(length)[0]:
        n = keys - PW
        pad = lax.broadcasted_iota(jnp.int32, (PW, BQ), 0) < prefix
        o_ref[pl.ds(at, PW), :] = jnp.where(pad, 0.0, NEG)
        key_at = key + lax.broadcasted_iota(jnp.int32, (n, BQ), 0)
        query_at = first + lax.broadcasted_iota(jnp.int32, (n, BQ), 1)
        seen = (column[key : key + n] == seg_ref[:, pl.ds(first, BQ)].astype(f32)) & (key_at <= query_at)
        o_ref[pl.ds(at + PW, n), :] = jnp.where(seen, 0.0, NEG)


def mask_bias(seg, valid, prefix, ties=()):
    length = seg.shape[1]
    total = spans(length)[1]
    return pl.pallas_call(
        tied(functools.partial(mask_kernel, length, prefix), len(ties)),
        grid=(1,),
        in_specs=tie_specs(ties) + [whole_spec((1, length))] * 2,
        out_specs=whole_spec((total, BQ)),
        out_shape=jax.ShapeDtypeStruct((total, BQ), f32),
        compiler_params=params(LIMIT),
        cost_estimate=cost(0),
        name="mask_bias",
    )(*ties, seg, valid)


def first_norm_kernel(x_ref, v_ref, o_ref):
    model = x_ref.shape[1]
    normed = norm(x_ref[...].astype(f32))[0]
    o_ref[...] = (normed * row_of(v_ref, GAIN1, model) + row_of(v_ref, SHIFT1, model)).astype(bf16)


def first_norm(x, vecs, ties=()):
    length, model = x.shape
    return pl.pallas_call(
        tied(first_norm_kernel, len(ties)),
        grid=(length // BM,),
        in_specs=tie_specs(ties) + [rows_spec(model), whole_spec(vecs.shape)],
        out_specs=rows_spec(model),
        out_shape=jax.ShapeDtypeStruct((length, model), bf16),
        compiler_params=params(LIMIT),
        cost_estimate=cost(0),
        name="first_norm",
    )(*ties, x, vecs)


def of_head(shape, head):
    lane = lax.broadcasted_iota(jnp.int32, shape, 1)
    return (lane >= HD * head) & (lane < HD * (head + 1))


def stack_heads(q):
    return jnp.concatenate([jnp.where(of_head(q.shape, h), q, jnp.zeros_like(q)) for h in range(HEADS)], 0)


def pick_heads(o):
    out = o[:BQ]
    for h in range(1, HEADS):
        out = jnp.where(of_head(out.shape, h), o[h * BQ : (h + 1) * BQ], out)
    return out


def attend_kernel(length, group, w, collect, *refs):
    (x_ref, v_ref, bias_ref), refs = refs[:3], refs[3:]
    if not collect:
        kv_ref, refs = refs[0], refs[1:]
    wr, refs = refs[: w.count()], refs[w.count() :]
    (qkv_ref, o_ref, p_ref, pp_ref), refs = refs[:4], refs[4:]
    if collect:
        kv_ref, refs = refs[0], refs[1:]
    whole, sem = refs[:2]
    plan = spans(length)[0]
    step = pl.program_id(0)

    width = 3 * LANES

    @pl.when(step == 0)
    def _():
        if collect:
            start_collect(w, wr, kv_ref.shape[1], *refs[2:])
        for k in range(GROUP_STEPS):
            start_load(w, wr, whole, sem.at[k], k * width, width)
        if collect:
            wait_load(*refs[2:])
            kv_ref[...] = refs[2][0]

    for k in range(GROUP_STEPS):

        @pl.when(step == k)
        def _():
            wait_load(whole.at[:, pl.ds(k * width, width)], sem.at[k])

    lane = pl.multiple_of((group * GROUP_STEPS + step) * LANES, LANES)
    pk = kv_ref[:, pl.ds(lane, LANES)]
    pv = kv_ref[:, pl.ds(kv_ref.shape[1] // 2 + lane, LANES)]

    at = pl.multiple_of(step * 3 * LANES, 3 * LANES)
    shift = row_of(v_ref, QKV_SHIFT, 3 * LANES, group * GROUP_STEPS * 3 * LANES + at)
    qkv_ref[...] = (dot(x_ref[...], whole[:, pl.ds(at, 3 * LANES)]) + shift).astype(bf16)

    def score(i):
        first, key, keys, _ = plan[i]
        q = qkv_ref[pl.ds(first, BQ), pl.ds(0, LANES)] * jnp.asarray(HD**-0.5, bf16)
        ks = jnp.concatenate([pk, qkv_ref[pl.ds(key, keys - PW), pl.ds(LANES, LANES)]], 0)
        return dot(ks, stack_heads(q), NT)

    def soft(i, s):
        first, _, keys, at = plan[i]
        s = s + jnp.concatenate([bias_ref[pl.ds(at, keys), :]] * HEADS, 1)
        e = jnp.exp(s - jnp.max(s, axis=0, keepdims=True))
        probs = (e * (1.0 / jnp.sum(e, axis=0, keepdims=True))).astype(bf16)
        p_ref[0, pl.ds(at, keys), :] = probs
        for h in range(HEADS):
            pp_ref[pl.ds(h * PW, PW), pl.ds(first, BQ)] = probs[:PW, h * BQ : (h + 1) * BQ]
        return probs

    def mix(i, probs):
        first, key, keys, _ = plan[i]
        vs = jnp.concatenate([pv, qkv_ref[pl.ds(key, keys - PW), pl.ds(2 * LANES, LANES)]], 0)
        o_ref[pl.ds(first, BQ), :] = pick_heads(dot(probs, vs, TN)).astype(bf16)

    n = len(plan)
    s, held = score(0), None
    for i in range(n):
        later = score(i + 1) if i + 1 < n else None
        probs = soft(i, s)
        if held is not None:
            mix(i - 1, held)
        s, held = later, probs
    mix(n - 1, held)


def start_collect(w, refs, cols, kv, sem):
    here = w.net.position()
    part = cols // 4
    for array in range(len(refs)):
        x, y, c = w.net.source(array, *here[1:])
        at = pl.multiple_of((2 * y + c) * part, part)
        pltpu.make_async_copy(
            refs[array].at[pl.ds(w.net.planes * w.block, PW), pl.ds(0, part)],
            kv.at[(x + here[1]) % 2, :, pl.ds(at, part)],
            sem,
        ).start()


def attend(group, x, w, vecs, prefix_kv, bias, ties=()):
    length, model = x.shape
    steps = w.cols // (3 * LANES)
    total = spans(length)[1]
    collect = prefix_kv is None
    kv_spec = whole_spec((PW, 2 * model))
    out_specs = [
        pl.BlockSpec((length, 3 * LANES), lambda i: (0, i)),
        pl.BlockSpec((length, LANES), lambda i: (0, i)),
        pl.BlockSpec((1, total, HEADS * BQ), lambda i: (i, 0, 0)),
        pl.BlockSpec((HEADS * PW, length), lambda i: (i, 0)),
    ]
    out_shape = [
        jax.ShapeDtypeStruct((length, w.cols), bf16),
        jax.ShapeDtypeStruct((length, steps * LANES), bf16),
        jax.ShapeDtypeStruct((steps, total, HEADS * BQ), bf16),
        jax.ShapeDtypeStruct((steps * HEADS * PW, length), bf16),
    ]
    scratch = [pltpu.VMEM((w.rows, w.cols), bf16), pltpu.SemaphoreType.DMA((GROUP_STEPS,))]
    if collect:
        out_specs.append(kv_spec)
        out_shape.append(jax.ShapeDtypeStruct((PW, 2 * model), bf16))
        scratch = scratch + [pltpu.VMEM((2, PW, 2 * model), bf16), pltpu.SemaphoreType.DMA]
    return pl.pallas_call(
        tied(functools.partial(attend_kernel, length, group, w, collect), len(ties)),
        grid=(steps,),
        in_specs=tie_specs(ties)
        + [whole_spec(x.shape), whole_spec(vecs.shape), whole_spec((total, BQ))]
        + ([] if collect else [kv_spec])
        + w.specs(),
        out_specs=out_specs,
        out_shape=out_shape,
        scratch_shapes=scratch,
        compiler_params=params(ROOM),
        cost_estimate=cost(8 * steps),
        name="attend",
    )(*ties, x, vecs, bias, *([] if collect else [prefix_kv]), *w.arrays)


def prefix_specs(steps, first):
    return [pl.BlockSpec((PW, LANES), lambda i, at=at: (0, at + first + i)) for at in (0, steps)]


def attend_back_kernel(length, w, first, last, *refs):
    (qkv_ref, p_ref, pk_ref, pv_ref, do_ref), refs = refs[:5], refs[5:]
    if not first:
        gn_in, refs = refs[0], refs[1:]
    if last:
        (x_hbm, gm_hbm, v_ref), refs = refs[:3], refs[3:]
    wr, refs = refs[: w.count()], refs[w.count() :]
    (out_ref, gn, ak, av, dqkv, whole, sem, io_sem), refs = refs[:8], refs[8:]
    step, steps = pl.program_id(0), pl.num_programs(0)
    if not first:
        gn_vm, refs = refs[0], refs[1:]
    copies = [] if first else [pltpu.make_async_copy(gn_in, gn_vm, io_sem.at[0])]
    if last:
        x_vm, gm_vm = refs
        copies.append(pltpu.make_async_copy(x_hbm, x_vm, io_sem.at[1]))
        copies.append(pltpu.make_async_copy(gm_hbm, gm_vm, io_sem.at[2]))

    @pl.when(step == 0)
    def _():
        start_load(w, wr, whole, sem)
        for copy in copies:
            copy.start()

    ak[...] = jnp.zeros_like(ak)
    av[...] = jnp.zeros_like(av)
    plan = spans(length)[0]

    def scores(i):
        first, key, keys, _ = plan[i]
        dos = stack_heads(do_ref[pl.ds(first, BQ), :])
        vs = jnp.concatenate([pv_ref[...], qkv_ref[pl.ds(key, keys - PW), pl.ds(2 * LANES, LANES)]], 0)
        return dos, dot(vs, dos, NT)

    def soft(i, dos, dp):
        _, _, keys, at = plan[i]
        probs = p_ref[0, pl.ds(at, keys), :]
        wide = probs.astype(f32)
        t = wide * dp
        return dos, probs, (t - wide * jnp.sum(t, axis=0, keepdims=True)).astype(bf16)

    def mix(i, dos, probs, ds):
        first, key, keys, _ = plan[i]
        n = keys - PW
        qs = stack_heads(qkv_ref[pl.ds(first, BQ), pl.ds(0, LANES)] * jnp.asarray(HD**-0.5, bf16))
        ks = jnp.concatenate([pk_ref[...], qkv_ref[pl.ds(key, n), pl.ds(LANES, LANES)]], 0)
        ak[pl.ds(key, n), :] += dot(ds[PW:], qs)
        av[pl.ds(key, n), :] += dot(probs[PW:], dos)
        dqkv[pl.ds(first, BQ), pl.ds(0, LANES)] = (pick_heads(dot(ds, ks, TN)) * HD**-0.5).astype(bf16)

    n = len(plan)
    s, held = scores(0), None
    for i in range(n):
        later = scores(i + 1) if i + 1 < n else None
        done = soft(i, *s)
        if held is not None:
            mix(i - 1, *held)
        s, held = later, done
    mix(n - 1, *held)
    dqkv[:, pl.ds(LANES, LANES)] = ak[...].astype(bf16)
    dqkv[:, pl.ds(2 * LANES, LANES)] = av[...].astype(bf16)

    @pl.when(step == 0)
    def _():
        wait_load(whole, sem)

    at = pl.multiple_of(step * 3 * LANES, 3 * LANES)
    part = dot(dqkv[...], whole[:, pl.ds(at, 3 * LANES)], NT)

    @pl.when(step == 0)
    def _():
        if first:
            gn[...] = part
        else:
            copies[0].wait()
            gn[...] = part + gn_vm[...].astype(f32)

    @pl.when(step > 0)
    def _():
        gn[...] += part

    if last:

        @pl.when(step == steps - 1)
        def _():
            for copy in copies[-2:]:
                copy.wait()

            def rows(i, carry):
                at = pl.ds(pl.multiple_of(i * BM, BM), BM)
                back = norm_back(x_vm[at, :].astype(f32), row_of(v_ref, GAIN1, out_ref.shape[1]), gn[at, :])
                out_ref[at, :] = (gm_vm[at, :].astype(f32) + back).astype(bf16)
                return carry

            lax.fori_loop(0, length // BM, rows, 0)

    else:

        @pl.when(step == steps - 1)
        def _():
            out_ref[...] = gn[...].astype(bf16)


def attend_back(group, qkv, probs, prefix_kv, do, so_far, w, rest=None, ties=()):
    length, model = do.shape
    steps = GROUP_STEPS
    total = spans(length)[1]
    first, last = so_far is None, rest is not None
    hbm = pl.BlockSpec(memory_space=pl.ANY)
    args = [qkv, probs, prefix_kv, prefix_kv, do]
    specs = [
        pl.BlockSpec((length, 3 * LANES), lambda i: (0, i)),
        pl.BlockSpec((1, total, HEADS * BQ), lambda i: (i, 0, 0)),
        *prefix_specs(GROUPS * steps, group * steps),
        pl.BlockSpec((length, LANES), lambda i: (0, group * steps + i)),
    ]
    if not first:
        args, specs = args + [so_far], specs + [hbm]
    if last:
        args, specs = args + list(rest), specs + [hbm, hbm, whole_spec(rest[2].shape)]
    scratch = [pltpu.VMEM((length, model), f32)] + [pltpu.VMEM((length, LANES), f32)] * 2
    scratch = scratch + [pltpu.VMEM((length, 3 * LANES), bf16)] + w.scratch() + [pltpu.SemaphoreType.DMA((3,))]
    if not first:
        scratch = scratch + [pltpu.VMEM((length, model), bf16)]
    if last:
        scratch = scratch + [pltpu.VMEM((length, model), bf16)] * 2
    return pl.pallas_call(
        tied(functools.partial(attend_back_kernel, length, w, first, last), len(ties)),
        grid=(steps,),
        in_specs=tie_specs(ties) + specs + w.specs(),
        out_specs=whole_spec((length, model)),
        out_shape=jax.ShapeDtypeStruct((length, model), bf16),
        scratch_shapes=scratch,
        compiler_params=params(LIMIT),
        cost_estimate=cost(17),
        name="attend_back",
    )(*ties, *args, *w.arrays)


def prefix_kernel(e_ref, w1_ref, b1_ref, w2_ref, b2_ref, h_ref, low_ref, kv_ref):
    rows, model = e_ref.shape
    emb = jnp.concatenate([e_ref[...].astype(f32), jnp.zeros((PW - rows, model), f32)], 0).astype(bf16)
    mid, cols = b1_ref.shape[0], b2_ref.shape[0]
    hidden = jnp.tanh(dot(emb, w1_ref[...], NT) + b1_ref[...].astype(f32).reshape(1, mid))
    low = hidden.astype(bf16)
    h_ref[...] = hidden
    low_ref[...] = low
    kv_ref[:, pl.ds(0, cols)] = (dot(low, w2_ref[...]) + b2_ref[...].astype(f32).reshape(1, cols)).astype(bf16)
    if cols < kv_ref.shape[1]:
        kv_ref[:, pl.ds(cols, kv_ref.shape[1] - cols)] = jnp.zeros((PW, kv_ref.shape[1] - cols), bf16)


def prefix_forward(emb, weight1, bias1, weight2, bias2, room):
    mid, cols = weight2.shape
    args = (emb, weight1, bias1, weight2, bias2)
    outs = [((PW, mid), f32), ((PW, mid), bf16), ((PW, max(cols, room)), bf16)]
    return pl.pallas_call(
        prefix_kernel,
        grid=(1,),
        in_specs=[whole_spec(a.shape) for a in args],
        out_specs=[whole_spec(shape) for shape, _ in outs],
        out_shape=[jax.ShapeDtypeStruct(*a) for a in outs],
        compiler_params=params(LIMIT),
        cost_estimate=cost(0),
        name="prefix_forward",
    )(*args)


def add_pairs(refs):
    if len(refs) == 1:
        return refs[0][...]
    return (refs[0][...] + refs[1][...]) + (refs[2][...] + refs[3][...])


def real_rows(values, rows):
    return jnp.where(lax.broadcasted_iota(jnp.int32, values.shape, 0) < rows, values, 0.0)


def add_terms(terms):
    def kernel(a_ref, b_ref, c_ref, d_ref, o_ref):
        o_ref[...] = (a_ref[...] + b_ref[...]) + (c_ref[...] + d_ref[...])

    spec = whole_spec(terms[0].shape)
    return pl.pallas_call(
        kernel,
        grid=(1,),
        in_specs=[spec] * 4,
        out_specs=spec,
        out_shape=jax.ShapeDtypeStruct(terms[0].shape, f32),
        compiler_params=params(LIMIT),
        cost_estimate=cost(1),
        name="add_terms",
    )(*terms)


def second_layer_kernel(n, rows, *refs):
    parts, (low_ref, w_ref, wg_ref, bg_ref, hg_ref) = refs[:n], refs[n:]
    kv = real_rows(add_pairs(parts), rows).astype(bf16)
    bg_ref[...] = jnp.sum(kv.astype(f32), axis=0)
    wg_ref[...] = dot(low_ref[...], kv, TN)
    hg_ref[...] = dot(kv, w_ref[...], NT)


def second_layer_back(parts, rows, hidden_low, weight):
    mid, cols = weight.shape
    args = (*parts, hidden_low, weight)
    shapes = [(mid, cols), (cols,), (PW, mid)]
    return pl.pallas_call(
        functools.partial(second_layer_kernel, len(parts), rows),
        grid=(1,),
        in_specs=[whole_spec(a.shape) for a in args],
        out_specs=[whole_spec(a) for a in shapes],
        out_shape=[jax.ShapeDtypeStruct(a, f32) for a in shapes],
        compiler_params=params(LIMIT),
        cost_estimate=cost(3),
        name="second_layer_back",
    )(*args)


def first_layer_kernel(n, *refs):
    parts, (hidden_ref, e_ref, w_ref, wg_ref, bg_ref, eg_ref) = refs[:n], refs[n:]
    hidden = hidden_ref[...]
    low = real_rows(add_pairs(parts) * (1.0 - hidden * hidden), e_ref.shape[0]).astype(bf16)
    bg_ref[...] = jnp.sum(low.astype(f32), axis=0)
    rows, model = e_ref.shape
    emb = jnp.concatenate([e_ref[...].astype(f32), jnp.zeros((PW - rows, model), f32)], 0).astype(bf16)
    wg_ref[...] = dot(low, emb, TN)
    eg_ref[...] = dot(low, w_ref[...])[:rows]


def first_layer_back(parts, hidden, emb, weight):
    mid, model = weight.shape
    shapes = [(mid, model), (mid,), emb.shape]
    args = (*parts, hidden, emb, weight)
    return pl.pallas_call(
        functools.partial(first_layer_kernel, len(parts)),
        grid=(1,),
        in_specs=[whole_spec(a.shape) for a in args],
        out_specs=[whole_spec(a) for a in shapes],
        out_shape=[jax.ShapeDtypeStruct(a, f32) for a in shapes],
        compiler_params=params(LIMIT),
        cost_estimate=cost(4),
        name="first_layer_back",
    )(*args)


def after(value, *others):
    return lax.optimization_barrier((value, *others))[0]


def gather_lines(net, parts, planes, rows_out, rows_in, ties):
    cols = planes[0].shape[1]
    size = rows_out + net.planes * rows_in

    def kernel(*refs):
        ins, outs, sems = refs[: net.planes], refs[net.planes : -1], refs[-1]
        here = net.position()[0]
        for n, part in enumerate(parts):
            for k in range(net.planes):
                plane = here ^ k
                at = pl.multiple_of(rows_out + rows_in * plane, rows_in)
                pltpu.make_async_copy(
                    ins[k].at[pl.ds(rows_out + rows_in * part, rows_in)], outs[n].at[pl.ds(at, rows_in)], sems.at[n]
                ).start()

                @pl.when(plane == part)
                def _():
                    pltpu.make_async_copy(
                        ins[k].at[pl.ds(0, rows_out)], outs[n].at[pl.ds(0, rows_out)], sems.at[n]
                    ).start()

        for n in range(len(parts)):
            pltpu.make_async_copy(outs[n], outs[n], sems.at[n]).wait()

    shape = jax.ShapeDtypeStruct((size, cols), bf16)
    return pl.pallas_call(
        tied(kernel, len(ties)),
        grid=(1,),
        in_specs=tie_specs(ties) + [pl.BlockSpec(memory_space=pl.ANY)] * net.planes,
        out_specs=[whole_spec((size, cols))] * len(parts),
        out_shape=[shape] * len(parts),
        scratch_shapes=[pltpu.SemaphoreType.DMA((len(parts),))],
        compiler_params=params(ROOM),
        cost_estimate=cost(2),
        name="gather_lines",
    )(*ties, *planes)


class Plain:
    def position(self):
        return ()

    def gather(self, shard):
        whole = lax.all_gather(shard, ALL, axis=0, tiled=True)
        rows, cols = whole.shape
        return Weight(self, [whole], rows, [(0, 0, lambda: 0)], rows, cols)

    def sum_columns(self, both):
        part = jnp.concatenate([both[0], both[1]], 1)
        return [lax.psum_scatter(lax.psum(part, "rows"), "pre", scatter_dimension=1, tiled=True)]

    def over_pre(self, part):
        return [lax.psum(part, "pre")]


class Grid:
    planes = 4

    def __init__(self):
        self.places = [(z, x, y, c) for z in range(4) for x in range(2) for y in range(2) for c in range(2)]

    def position(self):
        rows, pre = lax.axis_index("rows"), lax.axis_index("pre")
        return rows // 2, rows % 2, pre // 2, pre % 2

    @staticmethod
    def number(z, x, y, c):
        return z * 8 + x * 4 + y * 2 + c

    @staticmethod
    def side(x, y, c, second):
        along_x = (c + second + 1) % 2
        return (x + along_x) % 2, (y + 1 - along_x) % 2

    def send(self, value, where):
        return lax.ppermute(value, ALL, [(self.number(*p), self.number(*where(*p))) for p in self.places])

    def plane(self, block, k):
        return self.send(block, lambda z, x, y, c: (z ^ k, x, y, c))

    def planes_of(self, block):
        return [self.plane(block, k) for k in range(1, self.planes)]

    def planes_by_relay(self, block):
        two = self.plane(block, 2)
        return [block, self.plane(block, 1), two, self.plane(two, 1)]

    def beside(self, value, second):
        return self.send(value, lambda z, x, y, c: (z, *self.side(x, y, c, second), c))

    def across(self, value):
        return self.send(value, lambda z, x, y, c: (z, 1 - x, 1 - y, c))

    def core(self, value):
        return self.send(value, lambda z, x, y, c: (z, x, y, 1 - c))

    def source(self, array, x, y, c):
        if array >= 4:
            c = 1 - c
        if array % 4 >= 2:
            x, y = self.side(x, y, c, 1)
        if array % 2:
            x, y = self.side(x, y, c, 0)
        return x, y, c

    def arrays_of(self, line, near, far, end):
        own = [line, near, far, end]
        return own + [self.core(a) for a in own]

    def weight(self, arrays, rows, cols, at=0):
        def place(array, k):
            return lambda z, x, y, c: rows * self.number(z ^ k, *self.source(array, x, y, c))

        pieces = [(a, k * rows, place(a, k)) for a in range(8) for k in range(4)]
        return Weight(self, arrays, rows, pieces, rows * len(self.places), cols, at)

    def hidden_weights(self, arrays, rows_in, rows_out):
        devices, cols = len(self.places), arrays[0].shape[1]

        def inner(array, k):
            return lambda z, x, y, c: rows_in * self.number(k, *self.source(array, x, y, c))

        def outer(array):
            return lambda z, x, y, c: rows_out * self.number(0, *self.source(array, x, y, c))

        return (
            Weight(
                self,
                arrays,
                rows_in,
                [(a, rows_out + rows_in * k, inner(a, k)) for a in range(8) for k in range(4)],
                rows_in * devices,
                cols,
            ),
            Weight(self, arrays, rows_out, [(a, 0, outer(a)) for a in range(8)], rows_out * devices // 4, cols),
        )

    def sum_cores(self, both):
        _, _, y, c = self.position()
        both = both + self.core(both)
        cols = both.shape[2] // 2
        both = jnp.where(c == 0, both[:, :, :cols], both[:, :, cols:])
        return jnp.where(y == 0, both[0], both[1]), jnp.where(y == 0, both[1], both[0])

    def send_across(self, mine, other):
        along_x = self.send(mine, lambda z, x, y, c: (z, 1 - x, y, c))
        along_y = self.send(other, lambda z, x, y, c: (z, x, 1 - y, c))
        across = self.send(other, lambda z, x, y, c: (z, 1 - x, 1 - y, c))
        return [mine, along_x, along_y, across]

    def over_pre(self, part):
        along = self.send(part, lambda z, x, y, c: (z, x, 1 - y, c))
        across = self.send(part, lambda z, x, y, c: (z, x, 1 - y, 1 - c))
        return [part, self.core(part), along, across]


def per_device(
    tokens,
    seg_ids,
    valid,
    out_grad,
    ln1_gain,
    ln1_bias,
    qkv_weight,
    qkv_bias,
    proj_weight,
    proj_bias,
    ln2_gain,
    ln2_bias,
    fc_weight,
    fc_bias,
    out_weight,
    out_bias,
    prefix_emb,
    rep_weight1,
    rep_bias1,
    rep_weight2,
    rep_bias2,
):
    x, og = tokens[0], out_grad[0]
    model = x.shape[1]
    hidden_units = fc_weight.shape[1]
    prefix_len = prefix_emb.shape[0]
    own_q, own_o = qkv_weight.shape[0], out_weight.shape[0]
    width = hidden_units // CHUNKS
    part = model // GROUPS
    on_grid = (lax.axis_size("rows"), lax.axis_size("pre")) == (8, 4)
    net = Grid() if on_grid else Plain()

    def step_starts(g):
        return [i * model + g * part + k * LANES for k in range(GROUP_STEPS) for i in range(3)]

    def by_step(g):
        return [(0, k * LANES, 0, 0, at, own_q, LANES) for k, at in enumerate(step_starts(g))]

    second = by_step(1) + [(0, 3 * part, 1, 0, 0, own_q, model)]
    (shard,) = arrange(
        [((own_q, 6 * part + model), by_step(0) + [(0, 3 * part + at, *rest) for _, at, *rest in second])],
        qkv_weight,
        proj_weight,
    )
    if on_grid:
        others = net.planes_of(shard)
    starts = [at for g in range(GROUPS) for at in step_starts(g)]
    one = [(0, 0, model)]
    vecs = pack(
        [(GAIN1, one), (SHIFT1, one), (GAIN2, one), (SHIFT2, one), (PROJ_SHIFT, one), (OUT_SHIFT, one)]
        + [(QKV_SHIFT, [(k * LANES, at, LANES) for k, at in enumerate(starts)]), (FC_SHIFT, [(0, 0, hidden_units)])],
        hidden_units,
        ln1_gain,
        ln1_bias,
        ln2_gain,
        ln2_bias,
        proj_bias,
        out_bias,
        qkv_bias,
        fc_bias,
    )
    hidden, hidden_low, kv_local = prefix_forward(
        prefix_emb, rep_weight1.T, rep_bias1, rep_weight2, rep_bias2, 3 * part if on_grid else 0
    )

    def run_hidden(j, so_far, normed2, w_in, w_out, ties=()):
        back = (mixes, pprobs, qkvs, prefix_kv)
        w_last = w_proj if j == CHUNKS - 1 else None
        return hidden_part(j, normed2, og, vecs, mid, so_far, w_in, w_out, w_last, back, ties)

    so_far = None
    if not on_grid:
        prefix_kv = lax.all_gather(kv_local, "pre", axis=1, tiled=True)
        w_qkv = [net.gather(shard[:, g * 3 * part : (g + 1) * 3 * part]) for g in range(GROUPS)]
        w_proj = net.gather(proj_weight)
        out_all = lax.all_gather(out_weight, ALL, axis=0, tiled=True)
        normed1, bias = first_norm(x, vecs), mask_bias(seg_ids, valid, prefix_len)
        qkvs, mixes, probs, pprobs = zip(
            *[attend(g, normed1, w_qkv[g], vecs, prefix_kv, bias) for g in range(GROUPS)], strict=True
        )
        mid, normed2 = middle_block(mixes, x, w_proj, vecs)
        for j in range(CHUNKS):
            w_in = net.gather(fc_weight[:, j * width : (j + 1) * width])
            w_out = Weight(net, [out_all], width, [(0, j * width, lambda: 0)], width, model)
            so_far = run_hidden(j, so_far, normed2, w_in, w_out)
    else:
        def send_lines(parts, ties):
            return gather_lines(net, parts, planes_h, own_o, own_q, ties)

        rows, wide = net.planes * own_q, 3 * part + model
        normed1, bias = first_norm(x, vecs), mask_bias(seg_ids, valid, prefix_len)
        (line_a,) = arrange(
            [
                (
                    (rows + PW, 3 * part),
                    [(k * own_q, 0, k, 0, 0, own_q, 3 * part) for k in range(net.planes)]
                    + [(rows, 0, net.planes, 0, 0, PW, 3 * part)],
                ),
            ],
            shard,
            *others,
            kv_local,
            ties=(normed1, bias),
        )
        (shard_h,) = arrange(
            [
                (
                    (own_o + CHUNKS * own_q, model),
                    [(0, 0, 0, 0, 0, own_o, model)]
                    + [(own_o + j * own_q, 0, 1, 0, j * width, own_q, width) for j in range(CHUNKS)],
                )
            ],
            out_weight,
            fc_weight,
            ties=(line_a,),
        )
        planes_h = net.planes_by_relay(shard_h)
        near_a, far_a = net.beside(line_a, False), net.beside(line_a, True)
        end_a = net.across(line_a)
        (line_b,) = arrange(
            [((rows, wide), [(k * own_q, 0, k, 0, 3 * part, own_q, wide) for k in range(net.planes)])],
            shard,
            *others,
            ties=(shard_h,),
        )
        near_b, far_b = net.beside(line_b, False), net.beside(line_b, True)
        end_b = net.beside(near_b, True)
        w_a = net.weight(net.arrays_of(line_a, near_a, far_a, end_a), own_q, 3 * part)
        qkv_a, mix_a, probs_a, pprobs_a, prefix_kv = attend(0, normed1, w_a, vecs, None, bias, (near_b, planes_h[1], planes_h[2]))
        far_b, end_b = gate((far_b, end_b), (mix_a,))
        lines = list(send_lines((0, 1), (far_b, end_b)))
        arrays_b = net.arrays_of(line_b, near_b, far_b, end_b)
        w_b, w_proj = net.weight(arrays_b, own_q, 3 * part), net.weight(arrays_b, own_q, model, 3 * part)
        nears = [net.beside(a, False) for a in lines]
        fars = [net.beside(a, True) for a in lines]
        qkv_b, mix_b, probs_b, pprobs_b = attend(1, normed1, w_b, vecs, prefix_kv, bias, tuple(lines))
        ends = [net.beside(after(a, mix_b), True) for a in nears]
        mid, normed2 = middle_block([mix_a, mix_b], x, w_proj, vecs, tuple(nears))
        lines += send_lines((2, 3), (mid, ends[0]))
        nears += [net.beside(a, False) for a in lines[2:]]
        fars += [net.beside(a, True) for a in lines[2:]]
        w_qkv, qkvs, probs = [w_a, w_b], [qkv_a, qkv_b], [probs_a, probs_b]
        mixes, pprobs = [mix_a, mix_b], [pprobs_a, pprobs_b]
        latest = mid
        for j in range(CHUNKS):
            arrays = net.arrays_of(lines[j], nears[j], after(fars[j], latest), after(ends[j], latest))
            w_in, w_out = net.hidden_weights(arrays, own_q, own_o)
            ties = tuple(lines[2:]) if j == 0 else ()
            if 0 < j < CHUNKS - 1:
                ends.append(net.beside(after(nears[j + 1], latest), True))
                ties = (nears[j + 1],)
            so_far = run_hidden(j, so_far, normed2, w_in, w_out, ties)
            latest = so_far[0]
    output, grad_mid, grad_attn, prefix_grad = so_far
    rest = (x, grad_mid, vecs)
    if on_grid:
        mine, other = net.sum_cores(prefix_grad)
        terms = net.send_across(mine, other)
        so_far = attend_back(0, qkvs[0], probs[0], prefix_kv, grad_attn, None, w_qkv[0], ties=(mine, other))
        plane = add_terms(terms)
        sums = [plane, *net.planes_of(plane)]
        in_grad = attend_back(1, qkvs[1], probs[1], prefix_kv, grad_attn, so_far, w_qkv[1], rest, ties=(plane,))
    else:
        sums = net.sum_columns(prefix_grad)
        so_far = attend_back(0, qkvs[0], probs[0], prefix_kv, grad_attn, None, w_qkv[0])
        in_grad = attend_back(1, qkvs[1], probs[1], prefix_kv, grad_attn, so_far, w_qkv[1], rest)
    weight2_grad, bias2_grad, hid_grad = second_layer_back(sums, prefix_len, hidden_low, rep_weight2)
    hid_grads = net.over_pre(hid_grad)
    weight1_grad, bias1_grad, emb_grad = first_layer_back(hid_grads, hidden, prefix_emb, rep_weight1.T)
    return output[None], in_grad[None], emb_grad, weight1_grad.T, bias1_grad, weight2_grad, bias2_grad


def solution(mesh):
    split_all = P(ALL, None)
    whole = P()
    return jax.shard_map(
        per_device,
        mesh=mesh,
        in_specs=(
            P(ALL, None, None),
            split_all,
            split_all,
            P(ALL, None, None),
            whole,
            whole,
            split_all,
            whole,
            split_all,
            whole,
            whole,
            whole,
            split_all,
            whole,
            split_all,
            whole,
            whole,
            whole,
            whole,
            P(None, "pre"),
            P("pre"),
        ),
        out_specs=(
            P(ALL, None, None),
            P(ALL, None, None),
            whole,
            whole,
            whole,
            P(None, "pre"),
            P("pre"),
        ),
        check_vma=False,
    )
```

```python
import functools

import jax
import jax.numpy as jnp
from jax import lax
from jax.experimental import pallas as pl
from jax.experimental.pallas import tpu as pltpu
from jax.sharding import PartitionSpec as P

f32 = jnp.float32
bf16 = jnp.bfloat16
ALL = ("rows", "pre")
NEG = -1e30
EPS = 1e-05
HD = 64
SPAN = 256
BQ = 128
PW = 16
LANES = 256
HEADS = LANES // HD
GROUPS = 2
GROUP_STEPS = 2
CHUNKS = 4
BM = 256
BIG = 512
LIMIT = 58
ROOM = 52
SUB = 256

NN = (((1,), (0,)), ((), ()))
NT = (((1,), (1,)), ((), ()))
TN = (((0,), (0,)), ((), ()))


def dot(a, b, dims=NN):
    return lax.dot_general(a, b, dims, preferred_element_type=f32)


def params(mebibytes):
    return pltpu.CompilerParams(vmem_limit_bytes=mebibytes << 20)


def cost(microseconds):
    return pl.CostEstimate(flops=int(microseconds * 1.65e+08), bytes_accessed=1, transcendentals=0)


class Weight:
    def __init__(self, net, arrays, block, pieces, rows, cols, at=0):
        self.net, self.arrays, self.block, self.pieces = net, arrays, block, pieces
        self.rows, self.cols, self.at = rows, cols, at

    def specs(self):
        return [pl.BlockSpec(memory_space=pl.ANY) for _ in self.arrays]

    def count(self):
        return len(self.arrays)

    def scratch(self):
        return [pltpu.VMEM((self.rows, self.cols), bf16), pltpu.SemaphoreType.DMA]


def start_load(w, refs, whole, sem, at=0, cols=None):
    cols = cols or w.cols
    here = w.net.position()
    for array, row, place in w.pieces:
        first = pl.multiple_of(place(*here), w.block)
        pltpu.make_async_copy(
            refs[array].at[pl.ds(row, w.block), pl.ds(w.at + at, cols)],
            whole.at[pl.ds(first, w.block), pl.ds(at, cols)],
            sem,
        ).start()


def wait_load(whole, sem):
    pltpu.make_async_copy(whole, whole, sem).wait()


def tied(kernel, count):
    return lambda *refs: kernel(*refs[count:])


def tie_specs(ties):
    return [pl.BlockSpec(memory_space=pl.ANY)] * len(ties)


def arrange(plan, *arrays, ties=()):
    def kernel(*refs):
        ins, outs, sems = refs[: len(arrays)], refs[len(arrays) + len(ties) : -1], refs[-1]
        for k, (_, parts) in enumerate(plan):
            for row, col, array, from_row, from_col, rows, cols in parts:
                pltpu.make_async_copy(
                    ins[array].at[pl.ds(from_row, rows), pl.ds(from_col, cols)],
                    outs[k].at[pl.ds(row, rows), pl.ds(col, cols)],
                    sems.at[k],
                ).start()
        for k in range(len(plan)):
            pltpu.make_async_copy(outs[k], outs[k], sems.at[k]).wait()

    return pl.pallas_call(
        kernel,
        grid=(1,),
        in_specs=[pl.BlockSpec(memory_space=pl.ANY)] * (len(arrays) + len(ties)),
        out_specs=[whole_spec(shape) for shape, _ in plan],
        out_shape=[jax.ShapeDtypeStruct(shape, bf16) for shape, _ in plan],
        scratch_shapes=[pltpu.SemaphoreType.DMA((len(plan),))],
        compiler_params=params(LIMIT),
        cost_estimate=cost(0),
        name="arrange",
    )(*arrays, *ties)


def gate(arrays, ties):
    n = len(arrays)
    spec = pl.BlockSpec(memory_space=pl.ANY)
    return pl.pallas_call(
        lambda *refs: None,
        grid=(1,),
        in_specs=[spec] * (n + len(ties)),
        out_specs=[spec] * n,
        out_shape=[jax.ShapeDtypeStruct(a.shape, a.dtype) for a in arrays],
        input_output_aliases={i: i for i in range(n)},
        compiler_params=params(LIMIT),
        cost_estimate=cost(1),
        name="gate",
    )(*arrays, *ties)


def join(*arrays, ties=()):
    parts, at = [], 0
    for k, a in enumerate(arrays):
        parts.append((at, 0, k, 0, 0, *a.shape))
        at += a.shape[0]
    return arrange([((at, arrays[0].shape[1]), parts)], *arrays, ties=ties)[0]


GAIN1, SHIFT1, GAIN2, SHIFT2, PROJ_SHIFT, OUT_SHIFT, QKV_SHIFT, FC_SHIFT = range(8)


def pack_kernel(plan, *refs):
    out = refs[-1]
    out[...] = jnp.zeros_like(out)
    for ref, row in zip(refs[:-1], plan, strict=True):
        for at, start, size in row[1]:
            out[pl.ds(row[0], 1), pl.ds(at, size)] = ref[pl.ds(start, size)].astype(f32).reshape(1, size)


def pack(plan, width, *vectors):
    return pl.pallas_call(
        functools.partial(pack_kernel, plan),
        grid=(1,),
        in_specs=[whole_spec(v.shape) for v in vectors],
        out_specs=whole_spec((8, width)),
        out_shape=jax.ShapeDtypeStruct((8, width), f32),
        compiler_params=params(LIMIT),
        cost_estimate=cost(0),
        name="pack",
    )(*vectors)


def row_of(ref, row, size, at=0):
    return ref[pl.ds(row, 1), pl.ds(at, size)]


def norm(values):
    center = values - jnp.mean(values, axis=-1, keepdims=True)
    rate = lax.rsqrt(jnp.mean(center * center, axis=-1, keepdims=True) + EPS)
    return center * rate, rate


def norm_back(values, gain, grad):
    n, rate = norm(values)
    w = grad * gain
    return rate * (
        w - jnp.mean(w, axis=-1, keepdims=True) - n * jnp.mean(w * n, axis=-1, keepdims=True)
    )


def rows_spec(cols, at=0, rows=None):
    return pl.BlockSpec((rows or BM, cols), lambda i: (i, at))


def whole_spec(shape):
    return pl.BlockSpec(shape, lambda i: (0,) * len(shape))


def middle_kernel(w, *refs):
    parts, (x_ref, v_ref), refs = refs[:GROUPS], refs[GROUPS : GROUPS + 2], refs[GROUPS + 2 :]
    wr = refs[: w.count()]
    mid_ref, n_ref, whole, sem = refs[w.count() :]
    model = w.cols

    @pl.when(pl.program_id(0) == 0)
    def _():
        start_load(w, wr, whole, sem)
        wait_load(whole, sem)

    for i in range(0, x_ref.shape[0], BM):
        at = pl.ds(i, BM)
        attn = jnp.concatenate([p[at, :] for p in parts], 1)
        mid = x_ref[at, :].astype(f32) + (dot(attn, whole[...]) + row_of(v_ref, PROJ_SHIFT, model))
        mid_ref[at, :] = mid.astype(bf16)
        n_ref[at, :] = (norm(mid)[0] * row_of(v_ref, GAIN2, model) + row_of(v_ref, SHIFT2, model)).astype(bf16)


def middle_block(parts, x, w, vecs, ties=()):
    length, model = x.shape
    return pl.pallas_call(
        tied(functools.partial(middle_kernel, w), len(ties)),
        grid=(length // BIG,),
        in_specs=tie_specs(ties) + [rows_spec(p.shape[1], rows=BIG) for p in parts] + [rows_spec(model, rows=BIG), whole_spec(vecs.shape)] + w.specs(),
        out_specs=[rows_spec(model, rows=BIG)] * 2,
        out_shape=[
            jax.ShapeDtypeStruct((length, model), bf16),
            jax.ShapeDtypeStruct((length, model), bf16),
        ],
        scratch_shapes=w.scratch(),
        compiler_params=params(ROOM),
        cost_estimate=cost(8.5),
        name="middle_block",
    )(*ties, *parts, x, vecs, *w.arrays)


def gelu_both(v):
    c, a = 0.7978845608, 0.044715
    sq = v * v
    t = jnp.tanh(v * (c + (c * a) * sq))
    half = 0.5 + 0.5 * t
    act = v * half
    slope = half + (0.5 * v) * (1.0 - t * t) * (c + (3.0 * c * a) * sq)
    return act, slope


def hidden_kernel(w_in, w_out, w_proj, chunk, *refs):
    refs = list(refs)
    first, last = chunk == 0, w_proj is not None
    model, width = w_in.rows, w_in.cols
    (n_ref, og_ref, v_ref), refs = refs[:3], refs[3:]
    if first or last:
        mid_ref = refs.pop(0)
    if not first:
        (out_in, gn_in), refs = refs[:2], refs[2:]
    if last:
        back, refs = refs[: BACK_REFS], refs[BACK_REFS:]
    wi, refs = refs[: w_in.count()], refs[w_in.count() :]
    wo, refs = refs[: w_out.count()], refs[w_out.count() :]
    if last:
        wp, refs = refs[: w_proj.count()], refs[w_proj.count() :]
        (out_ref, gm_ref, ga_ref, dp_ref), refs = refs[:4], refs[4:]
    else:
        (out_ref, gn_ref), refs = refs[:2], refs[2:]
    fc, fc_sem, ow, ow_sem = refs[:4]

    step = pl.program_id(0)

    @pl.when(step == 0)
    def _():
        start_load(w_out, wo, ow, ow_sem)
        start_load(w_in, wi, fc, fc_sem)
        if last:
            start_load(w_proj, wp, refs[4], refs[5])
            start_back(back, refs[6:11])
        wait_load(ow, ow_sem)
        wait_load(fc, fc_sem)
        if last:
            wait_load(refs[4], refs[5])

    normed, og = n_ref[...], og_ref[...]
    acts, grads = [], []
    for j in range(0, width, SUB):
        at = pl.ds(j, SUB)
        act, slope = gelu_both(dot(normed, fc[:, at]) + row_of(v_ref, FC_SHIFT, SUB, chunk * width + j))
        acts.append(act.astype(bf16))
        grads.append((dot(og, ow[at, :], NT) * slope).astype(bf16))
    gn = dot(jnp.concatenate(grads, 1), fc[...], NT)
    if not first:
        gn = gn + gn_in[...].astype(f32)
    if last:
        gm = og.astype(f32) + norm_back(mid_ref[...].astype(f32), row_of(v_ref, GAIN2, model), gn)
        low = gm.astype(bf16)
    out = dot(jnp.concatenate(acts, 1), ow[...])
    if first:
        out = out + (mid_ref[...].astype(f32) + row_of(v_ref, OUT_SHIFT, model))
    else:
        out = out + out_in[...].astype(f32)
    out_ref[...] = out.astype(bf16)
    if last:
        gm_ref[...] = low
        ga = dot(low, refs[4][...], NT).astype(bf16)
        ga_ref[...] = ga
        refs[9][pl.ds(pl.multiple_of(step * BM, BM), BM), :] = ga

        @pl.when(step == pl.num_programs(0) - 1)
        def _():
            finish_back(back[-1], dp_ref, refs[6:11])
    else:
        gn_ref[...] = gn.astype(bf16)


BACK_REFS = 2 * GROUPS + GROUPS + 1


def start_back(refs, scratch):
    mixes, probs, qkvs = refs[:GROUPS], refs[GROUPS : 2 * GROUPS], refs[2 * GROUPS : 3 * GROUPS]
    q_all, mix_all, p_all, _, sems = scratch[:5]
    wide = GROUP_STEPS * LANES
    for g in range(GROUPS):
        rows = probs[g].shape[0]
        pltpu.make_async_copy(probs[g], p_all.at[pl.ds(g * rows, rows)], sems.at[0]).start()
        pltpu.make_async_copy(mixes[g], mix_all.at[:, pl.ds(g * wide, wide)], sems.at[1]).start()
        for k in range(GROUP_STEPS):
            pltpu.make_async_copy(
                qkvs[g].at[:, pl.ds(3 * LANES * k, LANES)], q_all.at[:, pl.ds(g * wide + k * LANES, LANES)], sems.at[2]
            ).start()


def own_head(rows, each, model):
    head = lax.broadcasted_iota(jnp.int32, (rows, model), 0) // each
    return head == lax.broadcasted_iota(jnp.int32, (rows, model), 1) // HD


def finish_back(pv_ref, dp_ref, scratch):
    q_all, mix_all, p_all, do_all, sems = scratch
    for k, ref in enumerate((p_all, mix_all, q_all)):
        pltpu.make_async_copy(ref, ref, sems.at[k]).wait()
    model = do_all.shape[1]
    heads = model // HD
    do = do_all[...]
    own = own_head(heads * PW, PW, model)
    pv = jnp.concatenate([pv_ref[...]] * heads, 0)
    dp = dot(jnp.where(own, pv, jnp.zeros_like(pv)), do, NT)
    ones = jnp.where(own_head(heads, 1, model), 1.0, 0.0).astype(bf16)
    delta = dot(ones, (do.astype(f32) * mix_all[...].astype(f32)).astype(bf16), NT)
    delta = jnp.concatenate([jnp.broadcast_to(delta[h : h + 1], (PW, delta.shape[1])) for h in range(heads)], 0)
    p = p_all[...]
    ds = (p.astype(f32) * (dp - delta)).astype(bf16)
    for k, (total, scale) in enumerate(((dot(ds, q_all[...]), HD**-0.5), (dot(p, do), 1.0))):
        kept = jnp.where(own, total, 0.0)
        dp_ref[k] = sum(kept[h * PW : (h + 1) * PW] for h in range(heads)) * scale


def hidden_part(chunk, normed, og, vecs, mid, so_far, w_in, w_out, w_proj, back, ties=()):
    length, model = og.shape
    first, last = chunk == 0, w_proj is not None
    full = rows_spec(model)
    specs, args = [full, full, whole_spec(vecs.shape)], [normed, og, vecs]
    if first or last:
        specs, args = specs + [full], args + [mid]
    if not first:
        specs, args = specs + [full, full], args + list(so_far)
    if last:
        mixes, probs, qkvs, prefix_kv = back
        specs = specs + tie_specs([*mixes, *probs, *qkvs]) + [pl.BlockSpec((PW, model), lambda i: (0, 1))]
        args = args + [*mixes, *probs, *qkvs, prefix_kv]
    specs, args = specs + w_in.specs() + w_out.specs(), args + list(w_in.arrays) + list(w_out.arrays)
    scratch = w_in.scratch() + w_out.scratch()
    outs = [bf16, bf16]
    if last:
        specs, args = specs + w_proj.specs(), args + list(w_proj.arrays)
        scratch = scratch + w_proj.scratch()
        scratch = scratch + [
            pltpu.VMEM((length, model), bf16),
            pltpu.VMEM((length, model), bf16),
            pltpu.VMEM((model // HD * PW, length), bf16),
            pltpu.VMEM((length, model), bf16),
            pltpu.SemaphoreType.DMA((3,)),
        ]
        outs = [bf16, bf16, bf16]
    out_specs = [full] * len(outs)
    out_shape = [jax.ShapeDtypeStruct((length, model), t) for t in outs]
    if last:
        out_specs = out_specs + [whole_spec((2, PW, model))]
        out_shape = out_shape + [jax.ShapeDtypeStruct((2, PW, model), f32)]
    return pl.pallas_call(
        tied(functools.partial(hidden_kernel, w_in, w_out, w_proj, chunk), len(ties)),
        grid=(length // BM,),
        in_specs=tie_specs(ties) + specs,
        out_specs=out_specs,
        out_shape=out_shape,
        scratch_shapes=scratch,
        compiler_params=params(ROOM),
        cost_estimate=cost(25 if last else 15),
        name="hidden_part",
    )(*ties, *args)


def spans(length):
    out, at = [], 0
    for first in range(0, length, BQ):
        key = max(0, first - SPAN)
        keys = PW + first + BQ - key
        out.append((first, key, keys, at))
        at += keys
    return out, at


def mask_kernel(length, prefix, seg_ref, valid_ref, o_ref):
    keyed = jnp.where(valid_ref[...] > 0, seg_ref[...], -1).astype(f32)
    columns = [jnp.broadcast_to(keyed[:, i : i + BQ], (BQ, BQ)).T for i in range(0, length, BQ)]
    column = jnp.concatenate(columns, 0)
    for first, key, keys, at in spans(length)[0]:
        n = keys - PW
        pad = lax.broadcasted_iota(jnp.int32, (PW, BQ), 0) < prefix
        o_ref[pl.ds(at, PW), :] = jnp.where(pad, 0.0, NEG)
        key_at = key + lax.broadcasted_iota(jnp.int32, (n, BQ), 0)
        query_at = first + lax.broadcasted_iota(jnp.int32, (n, BQ), 1)
        seen = (column[key : key + n] == seg_ref[:, pl.ds(first, BQ)].astype(f32)) & (key_at <= query_at)
        o_ref[pl.ds(at + PW, n), :] = jnp.where(seen, 0.0, NEG)


def mask_bias(seg, valid, prefix, ties=()):
    length = seg.shape[1]
    total = spans(length)[1]
    return pl.pallas_call(
        tied(functools.partial(mask_kernel, length, prefix), len(ties)),
        grid=(1,),
        in_specs=tie_specs(ties) + [whole_spec((1, length))] * 2,
        out_specs=whole_spec((total, BQ)),
        out_shape=jax.ShapeDtypeStruct((total, BQ), f32),
        compiler_params=params(LIMIT),
        cost_estimate=cost(0),
        name="mask_bias",
    )(*ties, seg, valid)


def first_norm_kernel(x_ref, v_ref, o_ref):
    model = x_ref.shape[1]
    normed = norm(x_ref[...].astype(f32))[0]
    o_ref[...] = (normed * row_of(v_ref, GAIN1, model) + row_of(v_ref, SHIFT1, model)).astype(bf16)


def first_norm(x, vecs, ties=()):
    length, model = x.shape
    return pl.pallas_call(
        tied(first_norm_kernel, len(ties)),
        grid=(length // BM,),
        in_specs=tie_specs(ties) + [rows_spec(model), whole_spec(vecs.shape)],
        out_specs=rows_spec(model),
        out_shape=jax.ShapeDtypeStruct((length, model), bf16),
        compiler_params=params(LIMIT),
        cost_estimate=cost(0),
        name="first_norm",
    )(*ties, x, vecs)


def of_head(shape, head):
    lane = lax.broadcasted_iota(jnp.int32, shape, 1)
    return (lane >= HD * head) & (lane < HD * (head + 1))


def stack_heads(q):
    return jnp.concatenate([jnp.where(of_head(q.shape, h), q, jnp.zeros_like(q)) for h in range(HEADS)], 0)


def pick_heads(o):
    out = o[:BQ]
    for h in range(1, HEADS):
        out = jnp.where(of_head(out.shape, h), o[h * BQ : (h + 1) * BQ], out)
    return out


def attend_kernel(length, group, w, collect, *refs):
    (x_ref, v_ref, bias_ref), refs = refs[:3], refs[3:]
    if not collect:
        kv_ref, refs = refs[0], refs[1:]
    wr, refs = refs[: w.count()], refs[w.count() :]
    (qkv_ref, o_ref, p_ref, pp_ref), refs = refs[:4], refs[4:]
    if collect:
        kv_ref, refs = refs[0], refs[1:]
    whole, sem = refs[:2]
    plan = spans(length)[0]
    step = pl.program_id(0)

    width = 3 * LANES

    @pl.when(step == 0)
    def _():
        if collect:
            start_collect(w, wr, kv_ref.shape[1], *refs[2:])
        for k in range(GROUP_STEPS):
            start_load(w, wr, whole, sem.at[k], k * width, width)
        if collect:
            wait_load(*refs[2:])
            kv_ref[...] = refs[2][0]

    for k in range(GROUP_STEPS):

        @pl.when(step == k)
        def _():
            wait_load(whole.at[:, pl.ds(k * width, width)], sem.at[k])

    lane = pl.multiple_of((group * GROUP_STEPS + step) * LANES, LANES)
    pk = kv_ref[:, pl.ds(lane, LANES)]
    pv = kv_ref[:, pl.ds(kv_ref.shape[1] // 2 + lane, LANES)]

    at = pl.multiple_of(step * 3 * LANES, 3 * LANES)
    shift = row_of(v_ref, QKV_SHIFT, 3 * LANES, group * GROUP_STEPS * 3 * LANES + at)
    qkv_ref[...] = (dot(x_ref[...], whole[:, pl.ds(at, 3 * LANES)]) + shift).astype(bf16)

    def score(i):
        first, key, keys, _ = plan[i]
        q = qkv_ref[pl.ds(first, BQ), pl.ds(0, LANES)] * jnp.asarray(HD**-0.5, bf16)
        ks = jnp.concatenate([pk, qkv_ref[pl.ds(key, keys - PW), pl.ds(LANES, LANES)]], 0)
        return dot(ks, stack_heads(q), NT)

    def soft(i, s):
        first, _, keys, at = plan[i]
        s = s + jnp.concatenate([bias_ref[pl.ds(at, keys), :]] * HEADS, 1)
        e = jnp.exp(s - jnp.max(s, axis=0, keepdims=True))
        probs = (e * (1.0 / jnp.sum(e, axis=0, keepdims=True))).astype(bf16)
        p_ref[0, pl.ds(at, keys), :] = probs
        for h in range(HEADS):
            pp_ref[pl.ds(h * PW, PW), pl.ds(first, BQ)] = probs[:PW, h * BQ : (h + 1) * BQ]
        return probs

    def mix(i, probs):
        first, key, keys, _ = plan[i]
        vs = jnp.concatenate([pv, qkv_ref[pl.ds(key, keys - PW), pl.ds(2 * LANES, LANES)]], 0)
        o_ref[pl.ds(first, BQ), :] = pick_heads(dot(probs, vs, TN)).astype(bf16)

    n = len(plan)
    s, held = score(0), None
    for i in range(n):
        later = score(i + 1) if i + 1 < n else None
        probs = soft(i, s)
        if held is not None:
            mix(i - 1, held)
        s, held = later, probs
    mix(n - 1, held)


def start_collect(w, refs, cols, kv, sem):
    here = w.net.position()
    part = cols // 4
    for array in range(len(refs)):
        x, y, c = w.net.source(array, *here[1:])
        at = pl.multiple_of((2 * y + c) * part, part)
        pltpu.make_async_copy(
            refs[array].at[pl.ds(w.net.planes * w.block, PW), pl.ds(0, part)],
            kv.at[(x + here[1]) % 2, :, pl.ds(at, part)],
            sem,
        ).start()


def attend(group, x, w, vecs, prefix_kv, bias, ties=()):
    length, model = x.shape
    steps = w.cols // (3 * LANES)
    total = spans(length)[1]
    collect = prefix_kv is None
    kv_spec = whole_spec((PW, 2 * model))
    out_specs = [
        pl.BlockSpec((length, 3 * LANES), lambda i: (0, i)),
        pl.BlockSpec((length, LANES), lambda i: (0, i)),
        pl.BlockSpec((1, total, HEADS * BQ), lambda i: (i, 0, 0)),
        pl.BlockSpec((HEADS * PW, length), lambda i: (i, 0)),
    ]
    out_shape = [
        jax.ShapeDtypeStruct((length, w.cols), bf16),
        jax.ShapeDtypeStruct((length, steps * LANES), bf16),
        jax.ShapeDtypeStruct((steps, total, HEADS * BQ), bf16),
        jax.ShapeDtypeStruct((steps * HEADS * PW, length), bf16),
    ]
    scratch = [pltpu.VMEM((w.rows, w.cols), bf16), pltpu.SemaphoreType.DMA((GROUP_STEPS,))]
    if collect:
        out_specs.append(kv_spec)
        out_shape.append(jax.ShapeDtypeStruct((PW, 2 * model), bf16))
        scratch = scratch + [pltpu.VMEM((2, PW, 2 * model), bf16), pltpu.SemaphoreType.DMA]
    return pl.pallas_call(
        tied(functools.partial(attend_kernel, length, group, w, collect), len(ties)),
        grid=(steps,),
        in_specs=tie_specs(ties)
        + [whole_spec(x.shape), whole_spec(vecs.shape), whole_spec((total, BQ))]
        + ([] if collect else [kv_spec])
        + w.specs(),
        out_specs=out_specs,
        out_shape=out_shape,
        scratch_shapes=scratch,
        compiler_params=params(ROOM),
        cost_estimate=cost(8 * steps),
        name="attend",
    )(*ties, x, vecs, bias, *([] if collect else [prefix_kv]), *w.arrays)


def prefix_specs(steps, first):
    return [pl.BlockSpec((PW, LANES), lambda i, at=at: (0, at + first + i)) for at in (0, steps)]


def attend_back_kernel(length, w, first, last, *refs):
    (qkv_ref, p_ref, pk_ref, pv_ref, do_ref), refs = refs[:5], refs[5:]
    if not first:
        gn_in, refs = refs[0], refs[1:]
    if last:
        (x_hbm, gm_hbm, v_ref), refs = refs[:3], refs[3:]
    wr, refs = refs[: w.count()], refs[w.count() :]
    (out_ref, gn, ak, av, dqkv, whole, sem, io_sem), refs = refs[:8], refs[8:]
    step, steps = pl.program_id(0), pl.num_programs(0)
    if not first:
        gn_vm, refs = refs[0], refs[1:]
    copies = [] if first else [pltpu.make_async_copy(gn_in, gn_vm, io_sem.at[0])]
    if last:
        x_vm, gm_vm = refs
        copies.append(pltpu.make_async_copy(x_hbm, x_vm, io_sem.at[1]))
        copies.append(pltpu.make_async_copy(gm_hbm, gm_vm, io_sem.at[2]))

    @pl.when(step == 0)
    def _():
        start_load(w, wr, whole, sem)
        for copy in copies:
            copy.start()

    ak[...] = jnp.zeros_like(ak)
    av[...] = jnp.zeros_like(av)
    plan = spans(length)[0]

    def scores(i):
        first, key, keys, _ = plan[i]
        dos = stack_heads(do_ref[pl.ds(first, BQ), :])
        vs = jnp.concatenate([pv_ref[...], qkv_ref[pl.ds(key, keys - PW), pl.ds(2 * LANES, LANES)]], 0)
        return dos, dot(vs, dos, NT)

    def soft(i, dos, dp):
        _, _, keys, at = plan[i]
        probs = p_ref[0, pl.ds(at, keys), :]
        wide = probs.astype(f32)
        t = wide * dp
        return dos, probs, (t - wide * jnp.sum(t, axis=0, keepdims=True)).astype(bf16)

    def mix(i, dos, probs, ds):
        first, key, keys, _ = plan[i]
        n = keys - PW
        qs = stack_heads(qkv_ref[pl.ds(first, BQ), pl.ds(0, LANES)] * jnp.asarray(HD**-0.5, bf16))
        ks = jnp.concatenate([pk_ref[...], qkv_ref[pl.ds(key, n), pl.ds(LANES, LANES)]], 0)
        ak[pl.ds(key, n), :] += dot(ds[PW:], qs)
        av[pl.ds(key, n), :] += dot(probs[PW:], dos)
        dqkv[pl.ds(first, BQ), pl.ds(0, LANES)] = (pick_heads(dot(ds, ks, TN)) * HD**-0.5).astype(bf16)

    n = len(plan)
    s, held = scores(0), None
    for i in range(n):
        later = scores(i + 1) if i + 1 < n else None
        done = soft(i, *s)
        if held is not None:
            mix(i - 1, *held)
        s, held = later, done
    mix(n - 1, *held)
    dqkv[:, pl.ds(LANES, LANES)] = ak[...].astype(bf16)
    dqkv[:, pl.ds(2 * LANES, LANES)] = av[...].astype(bf16)

    @pl.when(step == 0)
    def _():
        wait_load(whole, sem)

    mine = whole[:, pl.ds(pl.multiple_of(step * 3 * LANES, 3 * LANES), 3 * LANES)]

    @pl.when(step == 0)
    def _():
        part = dot(dqkv[...], mine, NT)
        if first:
            gn[...] = part
        else:
            copies[0].wait()
            gn[...] = part + gn_vm[...].astype(f32)

    @pl.when((step > 0) & (step < steps - 1))
    def _():
        gn[...] += dot(dqkv[...], mine, NT)

    @pl.when(step == steps - 1)
    def _():
        for copy in copies[-2:] if last else []:
            copy.wait()
        for i in range(0, length, BM):
            at = pl.ds(i, BM)
            grad = gn[at, :] + dot(dqkv[at, :], mine, NT)
            if last:
                back = norm_back(x_vm[at, :].astype(f32), row_of(v_ref, GAIN1, out_ref.shape[1]), grad)
                grad = gm_vm[at, :].astype(f32) + back
            out_ref[at, :] = grad.astype(bf16)


def attend_back(group, qkv, probs, prefix_kv, do, so_far, w, rest=None, ties=()):
    length, model = do.shape
    steps = GROUP_STEPS
    total = spans(length)[1]
    first, last = so_far is None, rest is not None
    hbm = pl.BlockSpec(memory_space=pl.ANY)
    args = [qkv, probs, prefix_kv, prefix_kv, do]
    specs = [
        pl.BlockSpec((length, 3 * LANES), lambda i: (0, i)),
        pl.BlockSpec((1, total, HEADS * BQ), lambda i: (i, 0, 0)),
        *prefix_specs(GROUPS * steps, group * steps),
        pl.BlockSpec((length, LANES), lambda i: (0, group * steps + i)),
    ]
    if not first:
        args, specs = args + [so_far], specs + [hbm]
    if last:
        args, specs = args + list(rest), specs + [hbm, hbm, whole_spec(rest[2].shape)]
    scratch = [pltpu.VMEM((length, model), f32)] + [pltpu.VMEM((length, LANES), f32)] * 2
    scratch = scratch + [pltpu.VMEM((length, 3 * LANES), bf16)] + w.scratch() + [pltpu.SemaphoreType.DMA((3,))]
    if not first:
        scratch = scratch + [pltpu.VMEM((length, model), bf16)]
    if last:
        scratch = scratch + [pltpu.VMEM((length, model), bf16)] * 2
    return pl.pallas_call(
        tied(functools.partial(attend_back_kernel, length, w, first, last), len(ties)),
        grid=(steps,),
        in_specs=tie_specs(ties) + specs + w.specs(),
        out_specs=whole_spec((length, model)),
        out_shape=jax.ShapeDtypeStruct((length, model), bf16),
        scratch_shapes=scratch,
        compiler_params=params(LIMIT),
        cost_estimate=cost(17),
        name="attend_back",
    )(*ties, *args, *w.arrays)


def prefix_kernel(e_ref, w1_ref, b1_ref, w2_ref, b2_ref, h_ref, low_ref, kv_ref):
    rows, model = e_ref.shape
    emb = jnp.concatenate([e_ref[...].astype(f32), jnp.zeros((PW - rows, model), f32)], 0).astype(bf16)
    mid, cols = b1_ref.shape[0], b2_ref.shape[0]
    hidden = jnp.tanh(dot(emb, w1_ref[...], NT) + b1_ref[...].astype(f32).reshape(1, mid))
    low = hidden.astype(bf16)
    h_ref[...] = hidden
    low_ref[...] = low
    kv_ref[:, pl.ds(0, cols)] = (dot(low, w2_ref[...]) + b2_ref[...].astype(f32).reshape(1, cols)).astype(bf16)
    if cols < kv_ref.shape[1]:
        kv_ref[:, pl.ds(cols, kv_ref.shape[1] - cols)] = jnp.zeros((PW, kv_ref.shape[1] - cols), bf16)


def prefix_forward(emb, weight1, bias1, weight2, bias2, room):
    mid, cols = weight2.shape
    args = (emb, weight1, bias1, weight2, bias2)
    outs = [((PW, mid), f32), ((PW, mid), bf16), ((PW, max(cols, room)), bf16)]
    return pl.pallas_call(
        prefix_kernel,
        grid=(1,),
        in_specs=[whole_spec(a.shape) for a in args],
        out_specs=[whole_spec(shape) for shape, _ in outs],
        out_shape=[jax.ShapeDtypeStruct(*a) for a in outs],
        compiler_params=params(LIMIT),
        cost_estimate=cost(0),
        name="prefix_forward",
    )(*args)


def add_pairs(refs):
    if len(refs) == 1:
        return refs[0][...]
    return (refs[0][...] + refs[1][...]) + (refs[2][...] + refs[3][...])


def real_rows(values, rows):
    return jnp.where(lax.broadcasted_iota(jnp.int32, values.shape, 0) < rows, values, 0.0)


def add_terms(terms):
    def kernel(a_ref, b_ref, c_ref, d_ref, o_ref):
        o_ref[...] = (a_ref[...] + b_ref[...]) + (c_ref[...] + d_ref[...])

    spec = whole_spec(terms[0].shape)
    return pl.pallas_call(
        kernel,
        grid=(1,),
        in_specs=[spec] * 4,
        out_specs=spec,
        out_shape=jax.ShapeDtypeStruct(terms[0].shape, f32),
        compiler_params=params(LIMIT),
        cost_estimate=cost(1),
        name="add_terms",
    )(*terms)


def second_layer_kernel(n, rows, *refs):
    parts, (low_ref, w_ref, wg_ref, bg_ref, hg_ref) = refs[:n], refs[n:]
    kv = real_rows(add_pairs(parts), rows).astype(bf16)
    bg_ref[...] = jnp.sum(kv.astype(f32), axis=0)
    wg_ref[...] = dot(low_ref[...], kv, TN)
    hg_ref[...] = dot(kv, w_ref[...], NT)


def second_layer_back(parts, rows, hidden_low, weight):
    mid, cols = weight.shape
    args = (*parts, hidden_low, weight)
    shapes = [(mid, cols), (cols,), (PW, mid)]
    return pl.pallas_call(
        functools.partial(second_layer_kernel, len(parts), rows),
        grid=(1,),
        in_specs=[whole_spec(a.shape) for a in args],
        out_specs=[whole_spec(a) for a in shapes],
        out_shape=[jax.ShapeDtypeStruct(a, f32) for a in shapes],
        compiler_params=params(LIMIT),
        cost_estimate=cost(3),
        name="second_layer_back",
    )(*args)


def first_layer_kernel(n, *refs):
    parts, (hidden_ref, e_ref, w_ref, wg_ref, bg_ref, eg_ref) = refs[:n], refs[n:]
    hidden = hidden_ref[...]
    low = real_rows(add_pairs(parts) * (1.0 - hidden * hidden), e_ref.shape[0]).astype(bf16)
    bg_ref[...] = jnp.sum(low.astype(f32), axis=0)
    rows, model = e_ref.shape
    emb = jnp.concatenate([e_ref[...].astype(f32), jnp.zeros((PW - rows, model), f32)], 0).astype(bf16)
    wg_ref[...] = dot(low, emb, TN)
    eg_ref[...] = dot(low, w_ref[...])[:rows]


def first_layer_back(parts, hidden, emb, weight):
    mid, model = weight.shape
    shapes = [(mid, model), (mid,), emb.shape]
    args = (*parts, hidden, emb, weight)
    return pl.pallas_call(
        functools.partial(first_layer_kernel, len(parts)),
        grid=(1,),
        in_specs=[whole_spec(a.shape) for a in args],
        out_specs=[whole_spec(a) for a in shapes],
        out_shape=[jax.ShapeDtypeStruct(a, f32) for a in shapes],
        compiler_params=params(LIMIT),
        cost_estimate=cost(4),
        name="first_layer_back",
    )(*args)


def after(value, *others):
    return lax.optimization_barrier((value, *others))[0]


def gather_lines(net, parts, planes, rows_out, rows_in, ties):
    cols = planes[0].shape[1]
    size = rows_out + net.planes * rows_in

    def kernel(*refs):
        ins, outs, sems = refs[: net.planes], refs[net.planes : -1], refs[-1]
        here = net.position()[0]
        for n, part in enumerate(parts):
            for k in range(net.planes):
                plane = here ^ k
                at = pl.multiple_of(rows_out + rows_in * plane, rows_in)
                pltpu.make_async_copy(
                    ins[k].at[pl.ds(rows_out + rows_in * part, rows_in)], outs[n].at[pl.ds(at, rows_in)], sems.at[n]
                ).start()

                @pl.when(plane == part)
                def _():
                    pltpu.make_async_copy(
                        ins[k].at[pl.ds(0, rows_out)], outs[n].at[pl.ds(0, rows_out)], sems.at[n]
                    ).start()

        for n in range(len(parts)):
            pltpu.make_async_copy(outs[n], outs[n], sems.at[n]).wait()

    shape = jax.ShapeDtypeStruct((size, cols), bf16)
    return pl.pallas_call(
        tied(kernel, len(ties)),
        grid=(1,),
        in_specs=tie_specs(ties) + [pl.BlockSpec(memory_space=pl.ANY)] * net.planes,
        out_specs=[whole_spec((size, cols))] * len(parts),
        out_shape=[shape] * len(parts),
        scratch_shapes=[pltpu.SemaphoreType.DMA((len(parts),))],
        compiler_params=params(ROOM),
        cost_estimate=cost(2),
        name="gather_lines",
    )(*ties, *planes)


class Plain:
    def position(self):
        return ()

    def gather(self, shard):
        whole = lax.all_gather(shard, ALL, axis=0, tiled=True)
        rows, cols = whole.shape
        return Weight(self, [whole], rows, [(0, 0, lambda: 0)], rows, cols)

    def sum_columns(self, both):
        part = jnp.concatenate([both[0], both[1]], 1)
        return [lax.psum_scatter(lax.psum(part, "rows"), "pre", scatter_dimension=1, tiled=True)]

    def over_pre(self, part):
        return [lax.psum(part, "pre")]


class Grid:
    planes = 4

    def __init__(self):
        self.places = [(z, x, y, c) for z in range(4) for x in range(2) for y in range(2) for c in range(2)]

    def position(self):
        rows, pre = lax.axis_index("rows"), lax.axis_index("pre")
        return rows // 2, rows % 2, pre // 2, pre % 2

    @staticmethod
    def number(z, x, y, c):
        return z * 8 + x * 4 + y * 2 + c

    @staticmethod
    def side(x, y, c, second):
        along_x = (c + second + 1) % 2
        return (x + along_x) % 2, (y + 1 - along_x) % 2

    def send(self, value, where):
        return lax.ppermute(value, ALL, [(self.number(*p), self.number(*where(*p))) for p in self.places])

    def plane(self, block, k):
        return self.send(block, lambda z, x, y, c: (z ^ k, x, y, c))

    def planes_of(self, block):
        return [self.plane(block, k) for k in range(1, self.planes)]

    def planes_by_relay(self, block):
        two = self.plane(block, 2)
        return [block, self.plane(block, 1), two, self.plane(two, 1)]

    def beside(self, value, second):
        return self.send(value, lambda z, x, y, c: (z, *self.side(x, y, c, second), c))

    def across(self, value):
        return self.send(value, lambda z, x, y, c: (z, 1 - x, 1 - y, c))

    def core(self, value):
        return self.send(value, lambda z, x, y, c: (z, x, y, 1 - c))

    def source(self, array, x, y, c):
        if array >= 4:
            c = 1 - c
        if array % 4 >= 2:
            x, y = self.side(x, y, c, 1)
        if array % 2:
            x, y = self.side(x, y, c, 0)
        return x, y, c

    def arrays_of(self, line, near, far, end):
        own = [line, near, far, end]
        return own + [self.core(a) for a in own]

    def weight(self, arrays, rows, cols, at=0):
        def place(array, k):
            return lambda z, x, y, c: rows * self.number(z ^ k, *self.source(array, x, y, c))

        pieces = [(a, k * rows, place(a, k)) for a in range(8) for k in range(4)]
        return Weight(self, arrays, rows, pieces, rows * len(self.places), cols, at)

    def hidden_weights(self, arrays, rows_in, rows_out):
        devices, cols = len(self.places), arrays[0].shape[1]

        def inner(array, k):
            return lambda z, x, y, c: rows_in * self.number(k, *self.source(array, x, y, c))

        def outer(array):
            return lambda z, x, y, c: rows_out * self.number(0, *self.source(array, x, y, c))

        return (
            Weight(
                self,
                arrays,
                rows_in,
                [(a, rows_out + rows_in * k, inner(a, k)) for a in range(8) for k in range(4)],
                rows_in * devices,
                cols,
            ),
            Weight(self, arrays, rows_out, [(a, 0, outer(a)) for a in range(8)], rows_out * devices // 4, cols),
        )

    def sum_cores(self, both):
        _, _, y, c = self.position()
        both = both + self.core(both)
        cols = both.shape[2] // 2
        both = jnp.where(c == 0, both[:, :, :cols], both[:, :, cols:])
        return jnp.where(y == 0, both[0], both[1]), jnp.where(y == 0, both[1], both[0])

    def send_across(self, mine, other):
        along_x = self.send(mine, lambda z, x, y, c: (z, 1 - x, y, c))
        along_y = self.send(other, lambda z, x, y, c: (z, x, 1 - y, c))
        across = self.send(other, lambda z, x, y, c: (z, 1 - x, 1 - y, c))
        return [mine, along_x, along_y, across]

    def over_pre(self, part):
        along = self.send(part, lambda z, x, y, c: (z, x, 1 - y, c))
        across = self.send(part, lambda z, x, y, c: (z, x, 1 - y, 1 - c))
        return [part, self.core(part), along, across]


def per_device(
    tokens,
    seg_ids,
    valid,
    out_grad,
    ln1_gain,
    ln1_bias,
    qkv_weight,
    qkv_bias,
    proj_weight,
    proj_bias,
    ln2_gain,
    ln2_bias,
    fc_weight,
    fc_bias,
    out_weight,
    out_bias,
    prefix_emb,
    rep_weight1,
    rep_bias1,
    rep_weight2,
    rep_bias2,
):
    x, og = tokens[0], out_grad[0]
    model = x.shape[1]
    hidden_units = fc_weight.shape[1]
    prefix_len = prefix_emb.shape[0]
    own_q, own_o = qkv_weight.shape[0], out_weight.shape[0]
    width = hidden_units // CHUNKS
    part = model // GROUPS
    on_grid = (lax.axis_size("rows"), lax.axis_size("pre")) == (8, 4)
    net = Grid() if on_grid else Plain()

    def step_starts(g):
        return [i * model + g * part + k * LANES for k in range(GROUP_STEPS) for i in range(3)]

    def by_step(g):
        return [(0, k * LANES, 0, 0, at, own_q, LANES) for k, at in enumerate(step_starts(g))]

    second = by_step(1) + [(0, 3 * part, 1, 0, 0, own_q, model)]
    (shard,) = arrange(
        [((own_q, 6 * part + model), by_step(0) + [(0, 3 * part + at, *rest) for _, at, *rest in second])],
        qkv_weight,
        proj_weight,
    )
    if on_grid:
        others = net.planes_of(shard)
    starts = [at for g in range(GROUPS) for at in step_starts(g)]
    one = [(0, 0, model)]
    vecs = pack(
        [(GAIN1, one), (SHIFT1, one), (GAIN2, one), (SHIFT2, one), (PROJ_SHIFT, one), (OUT_SHIFT, one)]
        + [(QKV_SHIFT, [(k * LANES, at, LANES) for k, at in enumerate(starts)]), (FC_SHIFT, [(0, 0, hidden_units)])],
        hidden_units,
        ln1_gain,
        ln1_bias,
        ln2_gain,
        ln2_bias,
        proj_bias,
        out_bias,
        qkv_bias,
        fc_bias,
    )
    hidden, hidden_low, kv_local = prefix_forward(
        prefix_emb, rep_weight1.T, rep_bias1, rep_weight2, rep_bias2, 3 * part if on_grid else 0
    )

    def run_hidden(j, so_far, normed2, w_in, w_out, ties=()):
        back = (mixes, pprobs, qkvs, prefix_kv)
        w_last = w_proj if j == CHUNKS - 1 else None
        return hidden_part(j, normed2, og, vecs, mid, so_far, w_in, w_out, w_last, back, ties)

    so_far = None
    if not on_grid:
        prefix_kv = lax.all_gather(kv_local, "pre", axis=1, tiled=True)
        w_qkv = [net.gather(shard[:, g * 3 * part : (g + 1) * 3 * part]) for g in range(GROUPS)]
        w_proj = net.gather(proj_weight)
        out_all = lax.all_gather(out_weight, ALL, axis=0, tiled=True)
        normed1, bias = first_norm(x, vecs), mask_bias(seg_ids, valid, prefix_len)
        qkvs, mixes, probs, pprobs = zip(
            *[attend(g, normed1, w_qkv[g], vecs, prefix_kv, bias) for g in range(GROUPS)], strict=True
        )
        mid, normed2 = middle_block(mixes, x, w_proj, vecs)
        for j in range(CHUNKS):
            w_in = net.gather(fc_weight[:, j * width : (j + 1) * width])
            w_out = Weight(net, [out_all], width, [(0, j * width, lambda: 0)], width, model)
            so_far = run_hidden(j, so_far, normed2, w_in, w_out)
    else:
        def send_lines(parts, ties):
            return gather_lines(net, parts, planes_h, own_o, own_q, ties)

        rows, wide = net.planes * own_q, 3 * part + model
        normed1, bias = first_norm(x, vecs), mask_bias(seg_ids, valid, prefix_len)
        (line_a,) = arrange(
            [
                (
                    (rows + PW, 3 * part),
                    [(k * own_q, 0, k, 0, 0, own_q, 3 * part) for k in range(net.planes)]
                    + [(rows, 0, net.planes, 0, 0, PW, 3 * part)],
                ),
            ],
            shard,
            *others,
            kv_local,
            ties=(normed1, bias),
        )
        (shard_h,) = arrange(
            [
                (
                    (own_o + CHUNKS * own_q, model),
                    [(0, 0, 0, 0, 0, own_o, model)]
                    + [(own_o + j * own_q, 0, 1, 0, j * width, own_q, width) for j in range(CHUNKS)],
                )
            ],
            out_weight,
            fc_weight,
            ties=(line_a,),
        )
        planes_h = net.planes_by_relay(shard_h)
        near_a, far_a = net.beside(line_a, False), net.beside(line_a, True)
        end_a = net.across(line_a)
        (line_b,) = arrange(
            [((rows, wide), [(k * own_q, 0, k, 0, 3 * part, own_q, wide) for k in range(net.planes)])],
            shard,
            *others,
            ties=(shard_h,),
        )
        near_b, far_b = net.beside(line_b, False), net.beside(line_b, True)
        end_b = net.beside(near_b, True)
        w_a = net.weight(net.arrays_of(line_a, near_a, far_a, end_a), own_q, 3 * part)
        qkv_a, mix_a, probs_a, pprobs_a, prefix_kv = attend(0, normed1, w_a, vecs, None, bias, (near_b, planes_h[1], planes_h[2]))
        far_b, end_b = gate((far_b, end_b), (mix_a,))
        lines = list(send_lines((0, 1), (far_b, end_b)))
        arrays_b = net.arrays_of(line_b, near_b, far_b, end_b)
        w_b, w_proj = net.weight(arrays_b, own_q, 3 * part), net.weight(arrays_b, own_q, model, 3 * part)
        nears = [net.beside(a, False) for a in lines]
        fars = [net.beside(a, True) for a in lines]
        qkv_b, mix_b, probs_b, pprobs_b = attend(1, normed1, w_b, vecs, prefix_kv, bias, tuple(lines))
        ends = [net.beside(after(a, mix_b), True) for a in nears]
        mid, normed2 = middle_block([mix_a, mix_b], x, w_proj, vecs, tuple(nears))
        lines += send_lines((2, 3), (mid, ends[0]))
        nears += [net.beside(a, False) for a in lines[2:]]
        fars += [net.beside(a, True) for a in lines[2:]]
        w_qkv, qkvs, probs = [w_a, w_b], [qkv_a, qkv_b], [probs_a, probs_b]
        mixes, pprobs = [mix_a, mix_b], [pprobs_a, pprobs_b]
        latest = mid
        for j in range(CHUNKS):
            arrays = net.arrays_of(lines[j], nears[j], after(fars[j], latest), after(ends[j], latest))
            w_in, w_out = net.hidden_weights(arrays, own_q, own_o)
            ties = tuple(lines[2:]) if j == 0 else ()
            if 0 < j < CHUNKS - 1:
                ends.append(net.beside(after(nears[j + 1], latest), True))
                ties = (nears[j + 1],)
            so_far = run_hidden(j, so_far, normed2, w_in, w_out, ties)
            latest = so_far[0]
    output, grad_mid, grad_attn, prefix_grad = so_far
    rest = (x, grad_mid, vecs)
    if on_grid:
        mine, other = net.sum_cores(prefix_grad)
        terms = net.send_across(mine, other)
        so_far = attend_back(0, qkvs[0], probs[0], prefix_kv, grad_attn, None, w_qkv[0], ties=(mine, other))
        plane = add_terms(terms)
        sums = [plane, *net.planes_of(plane)]
        in_grad = attend_back(1, qkvs[1], probs[1], prefix_kv, grad_attn, so_far, w_qkv[1], rest, ties=(plane,))
    else:
        sums = net.sum_columns(prefix_grad)
        so_far = attend_back(0, qkvs[0], probs[0], prefix_kv, grad_attn, None, w_qkv[0])
        in_grad = attend_back(1, qkvs[1], probs[1], prefix_kv, grad_attn, so_far, w_qkv[1], rest)
    weight2_grad, bias2_grad, hid_grad = second_layer_back(sums, prefix_len, hidden_low, rep_weight2)
    hid_grads = net.over_pre(hid_grad)
    weight1_grad, bias1_grad, emb_grad = first_layer_back(hid_grads, hidden, prefix_emb, rep_weight1.T)
    return output[None], in_grad[None], emb_grad, weight1_grad.T, bias1_grad, weight2_grad, bias2_grad


def solution(mesh):
    split_all = P(ALL, None)
    whole = P()
    return jax.shard_map(
        per_device,
        mesh=mesh,
        in_specs=(
            P(ALL, None, None),
            split_all,
            split_all,
            P(ALL, None, None),
            whole,
            whole,
            split_all,
            whole,
            split_all,
            whole,
            whole,
            whole,
            split_all,
            whole,
            split_all,
            whole,
            whole,
            whole,
            whole,
            P(None, "pre"),
            P("pre"),
        ),
        out_specs=(
            P(ALL, None, None),
            P(ALL, None, None),
            whole,
            whole,
            whole,
            P(None, "pre"),
            P("pre"),
        ),
        check_vma=False,
    )
```

```python
import functools

import jax
import jax.numpy as jnp
from jax import lax
from jax.experimental import pallas as pl
from jax.experimental.pallas import tpu as pltpu
from jax.sharding import PartitionSpec as P

f32 = jnp.float32
bf16 = jnp.bfloat16
ALL = ("rows", "pre")
NEG = -1e30
EPS = 1e-05
HD = 64
SPAN = 256
BQ = 128
PW = 16
LANES = 256
HEADS = LANES // HD
GROUPS = 2
GROUP_STEPS = 2
CHUNKS = 4
BM = 256
BIG = 512
LIMIT = 58
ROOM = 52
SUB = 256

NN = (((1,), (0,)), ((), ()))
NT = (((1,), (1,)), ((), ()))
TN = (((0,), (0,)), ((), ()))


def dot(a, b, dims=NN):
    return lax.dot_general(a, b, dims, preferred_element_type=f32)


def params(mebibytes):
    return pltpu.CompilerParams(vmem_limit_bytes=mebibytes << 20)


def cost(microseconds):
    return pl.CostEstimate(flops=int(microseconds * 1.65e+08), bytes_accessed=1, transcendentals=0)


class Weight:
    def __init__(self, net, arrays, block, pieces, rows, cols, at=0):
        self.net, self.arrays, self.block, self.pieces = net, arrays, block, pieces
        self.rows, self.cols, self.at = rows, cols, at

    def specs(self):
        return [pl.BlockSpec(memory_space=pl.ANY) for _ in self.arrays]

    def count(self):
        return len(self.arrays)

    def scratch(self):
        return [pltpu.VMEM((self.rows, self.cols), bf16), pltpu.SemaphoreType.DMA]


def start_load(w, refs, whole, sem, at=0, cols=None):
    cols = cols or w.cols
    here = w.net.position()
    for array, row, place in w.pieces:
        first = pl.multiple_of(place(*here), w.block)
        pltpu.make_async_copy(
            refs[array].at[pl.ds(row, w.block), pl.ds(w.at + at, cols)],
            whole.at[pl.ds(first, w.block), pl.ds(at, cols)],
            sem,
        ).start()


def wait_load(whole, sem):
    pltpu.make_async_copy(whole, whole, sem).wait()


def tied(kernel, count):
    return lambda *refs: kernel(*refs[count:])


def tie_specs(ties):
    return [pl.BlockSpec(memory_space=pl.ANY)] * len(ties)


def arrange(plan, *arrays, ties=()):
    def kernel(*refs):
        ins, outs, sems = refs[: len(arrays)], refs[len(arrays) + len(ties) : -1], refs[-1]
        for k, (_, parts) in enumerate(plan):
            for row, col, array, from_row, from_col, rows, cols in parts:
                pltpu.make_async_copy(
                    ins[array].at[pl.ds(from_row, rows), pl.ds(from_col, cols)],
                    outs[k].at[pl.ds(row, rows), pl.ds(col, cols)],
                    sems.at[k],
                ).start()
        for k in range(len(plan)):
            pltpu.make_async_copy(outs[k], outs[k], sems.at[k]).wait()

    return pl.pallas_call(
        kernel,
        grid=(1,),
        in_specs=[pl.BlockSpec(memory_space=pl.ANY)] * (len(arrays) + len(ties)),
        out_specs=[whole_spec(shape) for shape, _ in plan],
        out_shape=[jax.ShapeDtypeStruct(shape, bf16) for shape, _ in plan],
        scratch_shapes=[pltpu.SemaphoreType.DMA((len(plan),))],
        compiler_params=params(12),
        cost_estimate=cost(0),
        name="arrange",
    )(*arrays, *ties)


def gate(arrays, ties):
    n = len(arrays)
    spec = pl.BlockSpec(memory_space=pl.ANY)
    return pl.pallas_call(
        lambda *refs: None,
        grid=(1,),
        in_specs=[spec] * (n + len(ties)),
        out_specs=[spec] * n,
        out_shape=[jax.ShapeDtypeStruct(a.shape, a.dtype) for a in arrays],
        input_output_aliases={i: i for i in range(n)},
        compiler_params=params(LIMIT),
        cost_estimate=cost(1),
        name="gate",
    )(*arrays, *ties)


def join(*arrays, ties=()):
    parts, at = [], 0
    for k, a in enumerate(arrays):
        parts.append((at, 0, k, 0, 0, *a.shape))
        at += a.shape[0]
    return arrange([((at, arrays[0].shape[1]), parts)], *arrays, ties=ties)[0]


GAIN1, SHIFT1, GAIN2, SHIFT2, PROJ_SHIFT, OUT_SHIFT, QKV_SHIFT, FC_SHIFT = range(8)


def pack_kernel(plan, *refs):
    out = refs[-1]
    out[...] = jnp.zeros_like(out)
    for ref, row in zip(refs[:-1], plan, strict=True):
        for at, start, size in row[1]:
            out[pl.ds(row[0], 1), pl.ds(at, size)] = ref[pl.ds(start, size)].astype(f32).reshape(1, size)


def pack(plan, width, *vectors):
    return pl.pallas_call(
        functools.partial(pack_kernel, plan),
        grid=(1,),
        in_specs=[whole_spec(v.shape) for v in vectors],
        out_specs=whole_spec((8, width)),
        out_shape=jax.ShapeDtypeStruct((8, width), f32),
        compiler_params=params(LIMIT),
        cost_estimate=cost(0),
        name="pack",
    )(*vectors)


def row_of(ref, row, size, at=0):
    return ref[pl.ds(row, 1), pl.ds(at, size)]


def norm(values):
    center = values - jnp.mean(values, axis=-1, keepdims=True)
    rate = lax.rsqrt(jnp.mean(center * center, axis=-1, keepdims=True) + EPS)
    return center * rate, rate


def norm_back(values, gain, grad):
    n, rate = norm(values)
    w = grad * gain
    return rate * (
        w - jnp.mean(w, axis=-1, keepdims=True) - n * jnp.mean(w * n, axis=-1, keepdims=True)
    )


def rows_spec(cols, at=0, rows=None):
    return pl.BlockSpec((rows or BM, cols), lambda i: (i, at))


def whole_spec(shape):
    return pl.BlockSpec(shape, lambda i: (0,) * len(shape))


def middle_kernel(w, *refs):
    parts, (x_ref, v_ref), refs = refs[:GROUPS], refs[GROUPS : GROUPS + 2], refs[GROUPS + 2 :]
    wr = refs[: w.count()]
    mid_ref, n_ref, whole, sem = refs[w.count() :]
    model = w.cols

    @pl.when(pl.program_id(0) == 0)
    def _():
        start_load(w, wr, whole, sem)
        wait_load(whole, sem)

    for i in range(0, x_ref.shape[0], BM):
        at = pl.ds(i, BM)
        attn = jnp.concatenate([p[at, :] for p in parts], 1)
        mid = x_ref[at, :].astype(f32) + (dot(attn, whole[...]) + row_of(v_ref, PROJ_SHIFT, model))
        mid_ref[at, :] = mid.astype(bf16)
        n_ref[at, :] = (norm(mid)[0] * row_of(v_ref, GAIN2, model) + row_of(v_ref, SHIFT2, model)).astype(bf16)


def middle_block(parts, x, w, vecs, ties=()):
    length, model = x.shape
    return pl.pallas_call(
        tied(functools.partial(middle_kernel, w), len(ties)),
        grid=(length // BIG,),
        in_specs=tie_specs(ties) + [rows_spec(p.shape[1], rows=BIG) for p in parts] + [rows_spec(model, rows=BIG), whole_spec(vecs.shape)] + w.specs(),
        out_specs=[rows_spec(model, rows=BIG)] * 2,
        out_shape=[
            jax.ShapeDtypeStruct((length, model), bf16),
            jax.ShapeDtypeStruct((length, model), bf16),
        ],
        scratch_shapes=w.scratch(),
        compiler_params=params(ROOM),
        cost_estimate=cost(8.5),
        name="middle_block",
    )(*ties, *parts, x, vecs, *w.arrays)


def gelu_both(v):
    c, a = 0.7978845608, 0.044715
    sq = v * v
    t = jnp.tanh(v * (c + (c * a) * sq))
    half = 0.5 + 0.5 * t
    act = v * half
    slope = half + (0.5 * v) * (1.0 - t * t) * (c + (3.0 * c * a) * sq)
    return act, slope


def hidden_kernel(w_in, w_out, w_proj, chunk, *refs):
    refs = list(refs)
    first, last = chunk == 0, w_proj is not None
    model, width = w_in.rows, w_in.cols
    (n_ref, og_ref, v_ref), refs = refs[:3], refs[3:]
    if first or last:
        mid_ref = refs.pop(0)
    if not first:
        (out_in, gn_in), refs = refs[:2], refs[2:]
    if last:
        back, refs = refs[: BACK_REFS], refs[BACK_REFS:]
    wi, refs = refs[: w_in.count()], refs[w_in.count() :]
    wo, refs = refs[: w_out.count()], refs[w_out.count() :]
    if last:
        wp, refs = refs[: w_proj.count()], refs[w_proj.count() :]
        (out_ref, gm_ref, ga_ref, dp_ref), refs = refs[:4], refs[4:]
    else:
        (out_ref, gn_ref), refs = refs[:2], refs[2:]
    fc, fc_sem, ow, ow_sem = refs[:4]

    step = pl.program_id(0)

    @pl.when(step == 0)
    def _():
        start_load(w_out, wo, ow, ow_sem)
        start_load(w_in, wi, fc, fc_sem)
        if last:
            start_load(w_proj, wp, refs[4], refs[5])
            start_back(back, refs[6:11])
        wait_load(ow, ow_sem)
        wait_load(fc, fc_sem)
        if last:
            wait_load(refs[4], refs[5])

    normed, og = n_ref[...], og_ref[...]
    acts, grads = [], []
    for j in range(0, width, SUB):
        at = pl.ds(j, SUB)
        act, slope = gelu_both(dot(normed, fc[:, at]) + row_of(v_ref, FC_SHIFT, SUB, chunk * width + j))
        acts.append(act.astype(bf16))
        grads.append((dot(og, ow[at, :], NT) * slope).astype(bf16))
    gn = dot(jnp.concatenate(grads, 1), fc[...], NT)
    if not first:
        gn = gn + gn_in[...].astype(f32)
    if last:
        gm = og.astype(f32) + norm_back(mid_ref[...].astype(f32), row_of(v_ref, GAIN2, model), gn)
        low = gm.astype(bf16)
    out = dot(jnp.concatenate(acts, 1), ow[...])
    if first:
        out = out + (mid_ref[...].astype(f32) + row_of(v_ref, OUT_SHIFT, model))
    else:
        out = out + out_in[...].astype(f32)
    out_ref[...] = out.astype(bf16)
    if last:
        gm_ref[...] = low
        ga = dot(low, refs[4][...], NT).astype(bf16)
        ga_ref[...] = ga
        refs[9][pl.ds(pl.multiple_of(step * BM, BM), BM), :] = ga

        @pl.when(step == pl.num_programs(0) - 1)
        def _():
            finish_back(back[-1], dp_ref, refs[6:11])
    else:
        gn_ref[...] = gn.astype(bf16)


BACK_REFS = 2 * GROUPS + GROUPS + 1


def start_back(refs, scratch):
    mixes, probs, qkvs = refs[:GROUPS], refs[GROUPS : 2 * GROUPS], refs[2 * GROUPS : 3 * GROUPS]
    q_all, mix_all, p_all, _, sems = scratch[:5]
    wide = GROUP_STEPS * LANES
    for g in range(GROUPS):
        rows = probs[g].shape[0]
        pltpu.make_async_copy(probs[g], p_all.at[pl.ds(g * rows, rows)], sems.at[0]).start()
        pltpu.make_async_copy(mixes[g], mix_all.at[:, pl.ds(g * wide, wide)], sems.at[1]).start()
        for k in range(GROUP_STEPS):
            pltpu.make_async_copy(
                qkvs[g].at[:, pl.ds(3 * LANES * k, LANES)], q_all.at[:, pl.ds(g * wide + k * LANES, LANES)], sems.at[2]
            ).start()


def own_head(rows, each, model):
    head = lax.broadcasted_iota(jnp.int32, (rows, model), 0) // each
    return head == lax.broadcasted_iota(jnp.int32, (rows, model), 1) // HD


def finish_back(pv_ref, dp_ref, scratch):
    q_all, mix_all, p_all, do_all, sems = scratch
    for k, ref in enumerate((p_all, mix_all, q_all)):
        pltpu.make_async_copy(ref, ref, sems.at[k]).wait()
    model = do_all.shape[1]
    heads = model // HD
    do = do_all[...]
    own = own_head(heads * PW, PW, model)
    pv = jnp.concatenate([pv_ref[...]] * heads, 0)
    dp = dot(jnp.where(own, pv, jnp.zeros_like(pv)), do, NT)
    ones = jnp.where(own_head(heads, 1, model), 1.0, 0.0).astype(bf16)
    delta = dot(ones, (do.astype(f32) * mix_all[...].astype(f32)).astype(bf16), NT)
    delta = jnp.concatenate([jnp.broadcast_to(delta[h : h + 1], (PW, delta.shape[1])) for h in range(heads)], 0)
    p = p_all[...]
    ds = (p.astype(f32) * (dp - delta)).astype(bf16)
    for k, (total, scale) in enumerate(((dot(ds, q_all[...]), HD**-0.5), (dot(p, do), 1.0))):
        kept = jnp.where(own, total, 0.0)
        dp_ref[k] = sum(kept[h * PW : (h + 1) * PW] for h in range(heads)) * scale


def hidden_part(chunk, normed, og, vecs, mid, so_far, w_in, w_out, w_proj, back, ties=()):
    length, model = og.shape
    first, last = chunk == 0, w_proj is not None
    full = rows_spec(model)
    specs, args = [full, full, whole_spec(vecs.shape)], [normed, og, vecs]
    if first or last:
        specs, args = specs + [full], args + [mid]
    if not first:
        specs, args = specs + [full, full], args + list(so_far)
    if last:
        mixes, probs, qkvs, prefix_kv = back
        specs = specs + tie_specs([*mixes, *probs, *qkvs]) + [pl.BlockSpec((PW, model), lambda i: (0, 1))]
        args = args + [*mixes, *probs, *qkvs, prefix_kv]
    specs, args = specs + w_in.specs() + w_out.specs(), args + list(w_in.arrays) + list(w_out.arrays)
    scratch = w_in.scratch() + w_out.scratch()
    outs = [bf16, bf16]
    if last:
        specs, args = specs + w_proj.specs(), args + list(w_proj.arrays)
        scratch = scratch + w_proj.scratch()
        scratch = scratch + [
            pltpu.VMEM((length, model), bf16),
            pltpu.VMEM((length, model), bf16),
            pltpu.VMEM((model // HD * PW, length), bf16),
            pltpu.VMEM((length, model), bf16),
            pltpu.SemaphoreType.DMA((3,)),
        ]
        outs = [bf16, bf16, bf16]
    out_specs = [full] * len(outs)
    out_shape = [jax.ShapeDtypeStruct((length, model), t) for t in outs]
    if last:
        out_specs = out_specs + [whole_spec((2, PW, model))]
        out_shape = out_shape + [jax.ShapeDtypeStruct((2, PW, model), f32)]
    return pl.pallas_call(
        tied(functools.partial(hidden_kernel, w_in, w_out, w_proj, chunk), len(ties)),
        grid=(length // BM,),
        in_specs=tie_specs(ties) + specs,
        out_specs=out_specs,
        out_shape=out_shape,
        scratch_shapes=scratch,
        compiler_params=params(ROOM),
        cost_estimate=cost(25 if last else 15),
        name="hidden_part",
    )(*ties, *args)


def spans(length):
    out, at = [], 0
    for first in range(0, length, BQ):
        key = max(0, first - SPAN)
        keys = PW + first + BQ - key
        out.append((first, key, keys, at))
        at += keys
    return out, at


def mask_kernel(length, prefix, seg_ref, valid_ref, o_ref):
    keyed = jnp.where(valid_ref[...] > 0, seg_ref[...], -1).astype(f32)
    columns = [jnp.broadcast_to(keyed[:, i : i + BQ], (BQ, BQ)).T for i in range(0, length, BQ)]
    column = jnp.concatenate(columns, 0)
    for first, key, keys, at in spans(length)[0]:
        n = keys - PW
        pad = lax.broadcasted_iota(jnp.int32, (PW, BQ), 0) < prefix
        o_ref[pl.ds(at, PW), :] = jnp.where(pad, 0.0, NEG)
        key_at = key + lax.broadcasted_iota(jnp.int32, (n, BQ), 0)
        query_at = first + lax.broadcasted_iota(jnp.int32, (n, BQ), 1)
        seen = (column[key : key + n] == seg_ref[:, pl.ds(first, BQ)].astype(f32)) & (key_at <= query_at)
        o_ref[pl.ds(at + PW, n), :] = jnp.where(seen, 0.0, NEG)


def mask_bias(seg, valid, prefix, ties=()):
    length = seg.shape[1]
    total = spans(length)[1]
    return pl.pallas_call(
        tied(functools.partial(mask_kernel, length, prefix), len(ties)),
        grid=(1,),
        in_specs=tie_specs(ties) + [whole_spec((1, length))] * 2,
        out_specs=whole_spec((total, BQ)),
        out_shape=jax.ShapeDtypeStruct((total, BQ), f32),
        compiler_params=params(16),
        cost_estimate=cost(0),
        name="mask_bias",
    )(*ties, seg, valid)


def first_norm_kernel(x_ref, v_ref, o_ref):
    model = x_ref.shape[1]
    normed = norm(x_ref[...].astype(f32))[0]
    o_ref[...] = (normed * row_of(v_ref, GAIN1, model) + row_of(v_ref, SHIFT1, model)).astype(bf16)


def first_norm(x, vecs, ties=()):
    length, model = x.shape
    return pl.pallas_call(
        tied(first_norm_kernel, len(ties)),
        grid=(length // BM,),
        in_specs=tie_specs(ties) + [rows_spec(model), whole_spec(vecs.shape)],
        out_specs=rows_spec(model),
        out_shape=jax.ShapeDtypeStruct((length, model), bf16),
        compiler_params=params(16),
        cost_estimate=cost(0),
        name="first_norm",
    )(*ties, x, vecs)


def of_head(shape, head):
    lane = lax.broadcasted_iota(jnp.int32, shape, 1)
    return (lane >= HD * head) & (lane < HD * (head + 1))


def stack_heads(q):
    return jnp.concatenate([jnp.where(of_head(q.shape, h), q, jnp.zeros_like(q)) for h in range(HEADS)], 0)


def pick_heads(o):
    out = o[:BQ]
    for h in range(1, HEADS):
        out = jnp.where(of_head(out.shape, h), o[h * BQ : (h + 1) * BQ], out)
    return out


def attend_kernel(length, group, w, collect, *refs):
    (x_ref, v_ref, bias_ref), refs = refs[:3], refs[3:]
    if not collect:
        kv_ref, refs = refs[0], refs[1:]
    wr, refs = refs[: w.count()], refs[w.count() :]
    (qkv_hbm, o_ref, p_hbm, pp_ref), refs = refs[:4], refs[4:]
    if collect:
        kv_ref, refs = refs[0], refs[1:]
    (whole, sem, qkv_all, p_all, out_sem), refs = refs[:5], refs[5:]
    plan = spans(length)[0]
    step = pl.program_id(0)
    width = 3 * LANES
    qkv_ref, p_ref = qkv_all.at[step], p_all.at[step]

    def qkv_copy(k):
        return pltpu.make_async_copy(
            qkv_all.at[k], qkv_hbm.at[:, pl.ds(pl.multiple_of(k * width, width), width)], out_sem.at[0, k]
        )

    @pl.when(step == 0)
    def _():
        if collect:
            start_collect(w, wr, kv_ref.shape[1], *refs)
        for k in range(GROUP_STEPS):
            start_load(w, wr, whole, sem.at[k], k * width, width)
        if collect:
            wait_load(*refs)
            kv_ref[...] = refs[0][0]

    for k in range(GROUP_STEPS):

        @pl.when(step == k)
        def _():
            wait_load(whole.at[:, pl.ds(k * width, width)], sem.at[k])

    lane = pl.multiple_of((group * GROUP_STEPS + step) * LANES, LANES)
    pk = kv_ref[:, pl.ds(lane, LANES)]
    pv = kv_ref[:, pl.ds(kv_ref.shape[1] // 2 + lane, LANES)]

    at = pl.multiple_of(step * 3 * LANES, 3 * LANES)
    shift = row_of(v_ref, QKV_SHIFT, 3 * LANES, group * GROUP_STEPS * 3 * LANES + at)
    qkv_ref[...] = (dot(x_ref[...], whole[:, pl.ds(at, 3 * LANES)]) + shift).astype(bf16)
    qkv_copy(step).start()

    def score(i):
        first, key, keys, _ = plan[i]
        q = qkv_ref[pl.ds(first, BQ), pl.ds(0, LANES)] * jnp.asarray(HD**-0.5, bf16)
        ks = jnp.concatenate([pk, qkv_ref[pl.ds(key, keys - PW), pl.ds(LANES, LANES)]], 0)
        return dot(ks, stack_heads(q), NT)

    def soft(i, s):
        first, _, keys, at = plan[i]
        s = s + jnp.concatenate([bias_ref[pl.ds(at, keys), :]] * HEADS, 1)
        e = jnp.exp(s - jnp.max(s, axis=0, keepdims=True))
        probs = (e * (1.0 / jnp.sum(e, axis=0, keepdims=True))).astype(bf16)
        rows = pl.ds(at, keys)
        p_ref[rows, :] = probs
        pltpu.make_async_copy(p_ref.at[rows], p_hbm.at[step, rows], out_sem.at[1, step]).start()
        for h in range(HEADS):
            pp_ref[pl.ds(h * PW, PW), pl.ds(first, BQ)] = probs[:PW, h * BQ : (h + 1) * BQ]
        return probs

    def mix(i, probs):
        first, key, keys, _ = plan[i]
        vs = jnp.concatenate([pv, qkv_ref[pl.ds(key, keys - PW), pl.ds(2 * LANES, LANES)]], 0)
        o_ref[pl.ds(first, BQ), :] = pick_heads(dot(probs, vs, TN)).astype(bf16)

    n = len(plan)
    s, held = score(0), None
    for i in range(n):
        later = score(i + 1) if i + 1 < n else None
        probs = soft(i, s)
        if held is not None:
            mix(i - 1, held)
        s, held = later, probs
    mix(n - 1, held)

    @pl.when(step == GROUP_STEPS - 1)
    def _():
        for k in range(GROUP_STEPS):
            qkv_copy(k).wait()
            pltpu.make_async_copy(p_all.at[k], p_hbm.at[k], out_sem.at[1, k]).wait()


def start_collect(w, refs, cols, kv, sem):
    here = w.net.position()
    part = cols // 4
    for array in range(len(refs)):
        x, y, c = w.net.source(array, *here[1:])
        at = pl.multiple_of((2 * y + c) * part, part)
        pltpu.make_async_copy(
            refs[array].at[pl.ds(w.net.planes * w.block, PW), pl.ds(0, part)],
            kv.at[(x + here[1]) % 2, :, pl.ds(at, part)],
            sem,
        ).start()


def attend(group, x, w, vecs, prefix_kv, bias, ties=()):
    length, model = x.shape
    steps = w.cols // (3 * LANES)
    total = spans(length)[1]
    collect = prefix_kv is None
    kv_spec = whole_spec((PW, 2 * model))
    out_specs = [
        pl.BlockSpec(memory_space=pl.ANY),
        pl.BlockSpec((length, LANES), lambda i: (0, i)),
        pl.BlockSpec(memory_space=pl.ANY),
        pl.BlockSpec((HEADS * PW, length), lambda i: (i, 0)),
    ]
    out_shape = [
        jax.ShapeDtypeStruct((length, w.cols), bf16),
        jax.ShapeDtypeStruct((length, steps * LANES), bf16),
        jax.ShapeDtypeStruct((steps, total, HEADS * BQ), bf16),
        jax.ShapeDtypeStruct((steps * HEADS * PW, length), bf16),
    ]
    scratch = [pltpu.VMEM((w.rows, w.cols), bf16), pltpu.SemaphoreType.DMA((GROUP_STEPS,))]
    scratch = scratch + [
        pltpu.VMEM((steps, length, 3 * LANES), bf16),
        pltpu.VMEM((steps, total, HEADS * BQ), bf16),
        pltpu.SemaphoreType.DMA((2, steps)),
    ]
    if collect:
        out_specs.append(kv_spec)
        out_shape.append(jax.ShapeDtypeStruct((PW, 2 * model), bf16))
        scratch = scratch + [pltpu.VMEM((2, PW, 2 * model), bf16), pltpu.SemaphoreType.DMA]
    return pl.pallas_call(
        tied(functools.partial(attend_kernel, length, group, w, collect), len(ties)),
        grid=(steps,),
        in_specs=tie_specs(ties)
        + [whole_spec(x.shape), whole_spec(vecs.shape), whole_spec((total, BQ))]
        + ([] if collect else [kv_spec])
        + w.specs(),
        out_specs=out_specs,
        out_shape=out_shape,
        scratch_shapes=scratch,
        compiler_params=params(ROOM),
        cost_estimate=cost(8 * steps),
        name="attend",
    )(*ties, x, vecs, bias, *([] if collect else [prefix_kv]), *w.arrays)


def prefix_specs(steps, first):
    return [pl.BlockSpec((PW, LANES), lambda i, at=at: (0, at + first + i)) for at in (0, steps)]


def attend_back_kernel(length, w, first, last, *refs):
    (qkv_ref, p_ref, pk_ref, pv_ref, do_ref), refs = refs[:5], refs[5:]
    if not first:
        gn_in, refs = refs[0], refs[1:]
    if last:
        (x_hbm, gm_hbm, v_ref), refs = refs[:3], refs[3:]
    wr, refs = refs[: w.count()], refs[w.count() :]
    (out_ref, gn, ak, av, dqkv, whole, sem, io_sem), refs = refs[:8], refs[8:]
    step, steps = pl.program_id(0), pl.num_programs(0)
    if not first:
        gn_vm, refs = refs[0], refs[1:]
    copies = [] if first else [pltpu.make_async_copy(gn_in, gn_vm, io_sem.at[0])]
    if last:
        x_vm, gm_vm = refs
        copies.append(pltpu.make_async_copy(x_hbm, x_vm, io_sem.at[1]))
        copies.append(pltpu.make_async_copy(gm_hbm, gm_vm, io_sem.at[2]))

    @pl.when(step == 0)
    def _():
        start_load(w, wr, whole, sem)
        for copy in copies:
            copy.start()

    ak[...] = jnp.zeros_like(ak)
    av[...] = jnp.zeros_like(av)
    plan = spans(length)[0]

    def scores(i):
        first, key, keys, _ = plan[i]
        dos = stack_heads(do_ref[pl.ds(first, BQ), :])
        vs = jnp.concatenate([pv_ref[...], qkv_ref[pl.ds(key, keys - PW), pl.ds(2 * LANES, LANES)]], 0)
        return dos, dot(vs, dos, NT)

    def soft(i, dos, dp):
        _, _, keys, at = plan[i]
        probs = p_ref[0, pl.ds(at, keys), :]
        wide = probs.astype(f32)
        t = wide * dp
        return dos, probs, (t - wide * jnp.sum(t, axis=0, keepdims=True)).astype(bf16)

    def mix(i, dos, probs, ds):
        first, key, keys, _ = plan[i]
        n = keys - PW
        qs = stack_heads(qkv_ref[pl.ds(first, BQ), pl.ds(0, LANES)] * jnp.asarray(HD**-0.5, bf16))
        ks = jnp.concatenate([pk_ref[...], qkv_ref[pl.ds(key, n), pl.ds(LANES, LANES)]], 0)
        ak[pl.ds(key, n), :] += dot(ds[PW:], qs)
        av[pl.ds(key, n), :] += dot(probs[PW:], dos)
        dqkv[pl.ds(first, BQ), pl.ds(0, LANES)] = (pick_heads(dot(ds, ks, TN)) * HD**-0.5).astype(bf16)

    n = len(plan)
    s, held = scores(0), None
    for i in range(n):
        later = scores(i + 1) if i + 1 < n else None
        done = soft(i, *s)
        if held is not None:
            mix(i - 1, *held)
        s, held = later, done
    mix(n - 1, *held)
    dqkv[:, pl.ds(LANES, LANES)] = ak[...].astype(bf16)
    dqkv[:, pl.ds(2 * LANES, LANES)] = av[...].astype(bf16)

    @pl.when(step == 0)
    def _():
        wait_load(whole, sem)

    mine = whole[:, pl.ds(pl.multiple_of(step * 3 * LANES, 3 * LANES), 3 * LANES)]

    @pl.when(step == 0)
    def _():
        part = dot(dqkv[...], mine, NT)
        if first:
            gn[...] = part
        else:
            copies[0].wait()
            gn[...] = part + gn_vm[...].astype(f32)

    @pl.when((step > 0) & (step < steps - 1))
    def _():
        gn[...] += dot(dqkv[...], mine, NT)

    @pl.when(step == steps - 1)
    def _():
        for copy in copies[-2:] if last else []:
            copy.wait()
        for i in range(0, length, BM):
            at = pl.ds(i, BM)
            grad = gn[at, :] + dot(dqkv[at, :], mine, NT)
            if last:
                back = norm_back(x_vm[at, :].astype(f32), row_of(v_ref, GAIN1, out_ref.shape[1]), grad)
                grad = gm_vm[at, :].astype(f32) + back
            out_ref[at, :] = grad.astype(bf16)


def attend_back(group, qkv, probs, prefix_kv, do, so_far, w, rest=None, ties=()):
    length, model = do.shape
    steps = GROUP_STEPS
    total = spans(length)[1]
    first, last = so_far is None, rest is not None
    hbm = pl.BlockSpec(memory_space=pl.ANY)
    args = [qkv, probs, prefix_kv, prefix_kv, do]
    specs = [
        pl.BlockSpec((length, 3 * LANES), lambda i: (0, i)),
        pl.BlockSpec((1, total, HEADS * BQ), lambda i: (i, 0, 0)),
        *prefix_specs(GROUPS * steps, group * steps),
        pl.BlockSpec((length, LANES), lambda i: (0, group * steps + i)),
    ]
    if not first:
        args, specs = args + [so_far], specs + [hbm]
    if last:
        args, specs = args + list(rest), specs + [hbm, hbm, whole_spec(rest[2].shape)]
    scratch = [pltpu.VMEM((length, model), f32)] + [pltpu.VMEM((length, LANES), f32)] * 2
    scratch = scratch + [pltpu.VMEM((length, 3 * LANES), bf16)] + w.scratch() + [pltpu.SemaphoreType.DMA((3,))]
    if not first:
        scratch = scratch + [pltpu.VMEM((length, model), bf16)]
    if last:
        scratch = scratch + [pltpu.VMEM((length, model), bf16)] * 2
    return pl.pallas_call(
        tied(functools.partial(attend_back_kernel, length, w, first, last), len(ties)),
        grid=(steps,),
        in_specs=tie_specs(ties) + specs + w.specs(),
        out_specs=whole_spec((length, model)),
        out_shape=jax.ShapeDtypeStruct((length, model), bf16),
        scratch_shapes=scratch,
        compiler_params=params(LIMIT),
        cost_estimate=cost(17),
        name="attend_back",
    )(*ties, *args, *w.arrays)


def prefix_kernel(e_ref, w1_ref, b1_ref, w2_ref, b2_ref, h_ref, low_ref, kv_ref):
    rows, model = e_ref.shape
    emb = jnp.concatenate([e_ref[...].astype(f32), jnp.zeros((PW - rows, model), f32)], 0).astype(bf16)
    mid, cols = b1_ref.shape[0], b2_ref.shape[0]
    hidden = jnp.tanh(dot(emb, w1_ref[...], NT) + b1_ref[...].astype(f32).reshape(1, mid))
    low = hidden.astype(bf16)
    h_ref[...] = hidden
    low_ref[...] = low
    kv_ref[:, pl.ds(0, cols)] = (dot(low, w2_ref[...]) + b2_ref[...].astype(f32).reshape(1, cols)).astype(bf16)
    if cols < kv_ref.shape[1]:
        kv_ref[:, pl.ds(cols, kv_ref.shape[1] - cols)] = jnp.zeros((PW, kv_ref.shape[1] - cols), bf16)


def prefix_forward(emb, weight1, bias1, weight2, bias2, room):
    mid, cols = weight2.shape
    args = (emb, weight1, bias1, weight2, bias2)
    outs = [((PW, mid), f32), ((PW, mid), bf16), ((PW, max(cols, room)), bf16)]
    return pl.pallas_call(
        prefix_kernel,
        grid=(1,),
        in_specs=[whole_spec(a.shape) for a in args],
        out_specs=[whole_spec(shape) for shape, _ in outs],
        out_shape=[jax.ShapeDtypeStruct(*a) for a in outs],
        compiler_params=params(16),
        cost_estimate=cost(0),
        name="prefix_forward",
    )(*args)


def add_pairs(refs):
    if len(refs) == 1:
        return refs[0][...]
    return (refs[0][...] + refs[1][...]) + (refs[2][...] + refs[3][...])


def real_rows(values, rows):
    return jnp.where(lax.broadcasted_iota(jnp.int32, values.shape, 0) < rows, values, 0.0)


def add_terms(terms):
    def kernel(a_ref, b_ref, c_ref, d_ref, o_ref):
        o_ref[...] = (a_ref[...] + b_ref[...]) + (c_ref[...] + d_ref[...])

    spec = whole_spec(terms[0].shape)
    return pl.pallas_call(
        kernel,
        grid=(1,),
        in_specs=[spec] * 4,
        out_specs=spec,
        out_shape=jax.ShapeDtypeStruct(terms[0].shape, f32),
        compiler_params=params(8),
        cost_estimate=cost(1),
        name="add_terms",
    )(*terms)


def second_layer_kernel(n, rows, *refs):
    parts, (low_ref, w_ref, wg_ref, bg_ref, hg_ref) = refs[:n], refs[n:]
    kv = real_rows(add_pairs(parts), rows).astype(bf16)
    bg_ref[...] = jnp.sum(kv.astype(f32), axis=0)
    wg_ref[...] = dot(low_ref[...], kv, TN)
    hg_ref[...] = dot(kv, w_ref[...], NT)


def second_layer_back(parts, rows, hidden_low, weight):
    mid, cols = weight.shape
    args = (*parts, hidden_low, weight)
    shapes = [(mid, cols), (cols,), (PW, mid)]
    return pl.pallas_call(
        functools.partial(second_layer_kernel, len(parts), rows),
        grid=(1,),
        in_specs=[whole_spec(a.shape) for a in args],
        out_specs=[whole_spec(a) for a in shapes],
        out_shape=[jax.ShapeDtypeStruct(a, f32) for a in shapes],
        compiler_params=params(20),
        cost_estimate=cost(3),
        name="second_layer_back",
    )(*args)


def first_layer_kernel(n, *refs):
    parts, (hidden_ref, e_ref, w_ref, wg_ref, bg_ref, eg_ref) = refs[:n], refs[n:]
    hidden = hidden_ref[...]
    low = real_rows(add_pairs(parts) * (1.0 - hidden * hidden), e_ref.shape[0]).astype(bf16)
    bg_ref[...] = jnp.sum(low.astype(f32), axis=0)
    rows, model = e_ref.shape
    emb = jnp.concatenate([e_ref[...].astype(f32), jnp.zeros((PW - rows, model), f32)], 0).astype(bf16)
    wg_ref[...] = dot(low, emb, TN)
    eg_ref[...] = dot(low, w_ref[...])[:rows]


def first_layer_back(parts, hidden, emb, weight):
    mid, model = weight.shape
    shapes = [(mid, model), (mid,), emb.shape]
    args = (*parts, hidden, emb, weight)
    return pl.pallas_call(
        functools.partial(first_layer_kernel, len(parts)),
        grid=(1,),
        in_specs=[whole_spec(a.shape) for a in args],
        out_specs=[whole_spec(a) for a in shapes],
        out_shape=[jax.ShapeDtypeStruct(a, f32) for a in shapes],
        compiler_params=params(24),
        cost_estimate=cost(4),
        name="first_layer_back",
    )(*args)


def after(value, *others):
    return lax.optimization_barrier((value, *others))[0]


def gather_lines(net, parts, planes, rows_out, rows_in, ties):
    cols = planes[0].shape[1]
    size = rows_out + net.planes * rows_in

    def kernel(*refs):
        ins, outs, sems = refs[: net.planes], refs[net.planes : -1], refs[-1]
        here = net.position()[0]
        for n, part in enumerate(parts):
            for k in range(net.planes):
                plane = here ^ k
                at = pl.multiple_of(rows_out + rows_in * plane, rows_in)
                pltpu.make_async_copy(
                    ins[k].at[pl.ds(rows_out + rows_in * part, rows_in)], outs[n].at[pl.ds(at, rows_in)], sems.at[n]
                ).start()

                @pl.when(plane == part)
                def _():
                    pltpu.make_async_copy(
                        ins[k].at[pl.ds(0, rows_out)], outs[n].at[pl.ds(0, rows_out)], sems.at[n]
                    ).start()

        for n in range(len(parts)):
            pltpu.make_async_copy(outs[n], outs[n], sems.at[n]).wait()

    shape = jax.ShapeDtypeStruct((size, cols), bf16)
    return pl.pallas_call(
        tied(kernel, len(ties)),
        grid=(1,),
        in_specs=tie_specs(ties) + [pl.BlockSpec(memory_space=pl.ANY)] * net.planes,
        out_specs=[whole_spec((size, cols))] * len(parts),
        out_shape=[shape] * len(parts),
        scratch_shapes=[pltpu.SemaphoreType.DMA((len(parts),))],
        compiler_params=params(ROOM),
        cost_estimate=cost(2),
        name="gather_lines",
    )(*ties, *planes)


class Plain:
    def position(self):
        return ()

    def gather(self, shard):
        whole = lax.all_gather(shard, ALL, axis=0, tiled=True)
        rows, cols = whole.shape
        return Weight(self, [whole], rows, [(0, 0, lambda: 0)], rows, cols)

    def sum_columns(self, both):
        part = jnp.concatenate([both[0], both[1]], 1)
        return [lax.psum_scatter(lax.psum(part, "rows"), "pre", scatter_dimension=1, tiled=True)]

    def over_pre(self, part):
        return [lax.psum(part, "pre")]


class Grid:
    planes = 4

    def __init__(self):
        self.places = [(z, x, y, c) for z in range(4) for x in range(2) for y in range(2) for c in range(2)]

    def position(self):
        rows, pre = lax.axis_index("rows"), lax.axis_index("pre")
        return rows // 2, rows % 2, pre // 2, pre % 2

    @staticmethod
    def number(z, x, y, c):
        return z * 8 + x * 4 + y * 2 + c

    @staticmethod
    def side(x, y, c, second):
        along_x = (c + second + 1) % 2
        return (x + along_x) % 2, (y + 1 - along_x) % 2

    def send(self, value, where):
        return lax.ppermute(value, ALL, [(self.number(*p), self.number(*where(*p))) for p in self.places])

    def plane(self, block, k):
        return self.send(block, lambda z, x, y, c: (z ^ k, x, y, c))

    def planes_of(self, block):
        return [self.plane(block, k) for k in range(1, self.planes)]

    def planes_by_relay(self, block):
        two = self.plane(block, 2)
        return [block, self.plane(block, 1), two, self.plane(two, 1)]

    def beside(self, value, second):
        return self.send(value, lambda z, x, y, c: (z, *self.side(x, y, c, second), c))

    def across(self, value):
        return self.send(value, lambda z, x, y, c: (z, 1 - x, 1 - y, c))

    def core(self, value):
        return self.send(value, lambda z, x, y, c: (z, x, y, 1 - c))

    def source(self, array, x, y, c):
        if array >= 4:
            c = 1 - c
        if array % 4 >= 2:
            x, y = self.side(x, y, c, 1)
        if array % 2:
            x, y = self.side(x, y, c, 0)
        return x, y, c

    def arrays_of(self, line, near, far, end):
        own = [line, near, far, end]
        return own + [self.core(a) for a in own]

    def weight(self, arrays, rows, cols, at=0):
        def place(array, k):
            return lambda z, x, y, c: rows * self.number(z ^ k, *self.source(array, x, y, c))

        pieces = [(a, k * rows, place(a, k)) for a in range(8) for k in range(4)]
        return Weight(self, arrays, rows, pieces, rows * len(self.places), cols, at)

    def hidden_weights(self, arrays, rows_in, rows_out):
        devices, cols = len(self.places), arrays[0].shape[1]

        def inner(array, k):
            return lambda z, x, y, c: rows_in * self.number(k, *self.source(array, x, y, c))

        def outer(array):
            return lambda z, x, y, c: rows_out * self.number(0, *self.source(array, x, y, c))

        return (
            Weight(
                self,
                arrays,
                rows_in,
                [(a, rows_out + rows_in * k, inner(a, k)) for a in range(8) for k in range(4)],
                rows_in * devices,
                cols,
            ),
            Weight(self, arrays, rows_out, [(a, 0, outer(a)) for a in range(8)], rows_out * devices // 4, cols),
        )

    def sum_cores(self, both):
        _, _, y, c = self.position()
        both = both + self.core(both)
        cols = both.shape[2] // 2
        both = jnp.where(c == 0, both[:, :, :cols], both[:, :, cols:])
        return jnp.where(y == 0, both[0], both[1]), jnp.where(y == 0, both[1], both[0])

    def send_across(self, mine, other):
        along_x = self.send(mine, lambda z, x, y, c: (z, 1 - x, y, c))
        along_y = self.send(other, lambda z, x, y, c: (z, x, 1 - y, c))
        across = self.send(other, lambda z, x, y, c: (z, 1 - x, 1 - y, c))
        return [mine, along_x, along_y, across]

    def over_pre(self, part):
        along = self.send(part, lambda z, x, y, c: (z, x, 1 - y, c))
        across = self.send(part, lambda z, x, y, c: (z, x, 1 - y, 1 - c))
        return [part, self.core(part), along, across]


def per_device(
    tokens,
    seg_ids,
    valid,
    out_grad,
    ln1_gain,
    ln1_bias,
    qkv_weight,
    qkv_bias,
    proj_weight,
    proj_bias,
    ln2_gain,
    ln2_bias,
    fc_weight,
    fc_bias,
    out_weight,
    out_bias,
    prefix_emb,
    rep_weight1,
    rep_bias1,
    rep_weight2,
    rep_bias2,
):
    x, og = tokens[0], out_grad[0]
    model = x.shape[1]
    hidden_units = fc_weight.shape[1]
    prefix_len = prefix_emb.shape[0]
    own_q, own_o = qkv_weight.shape[0], out_weight.shape[0]
    width = hidden_units // CHUNKS
    part = model // GROUPS
    on_grid = (lax.axis_size("rows"), lax.axis_size("pre")) == (8, 4)
    net = Grid() if on_grid else Plain()

    def step_starts(g):
        return [i * model + g * part + k * LANES for k in range(GROUP_STEPS) for i in range(3)]

    def by_step(g):
        return [(0, k * LANES, 0, 0, at, own_q, LANES) for k, at in enumerate(step_starts(g))]

    second = by_step(1) + [(0, 3 * part, 1, 0, 0, own_q, model)]
    (shard,) = arrange(
        [((own_q, 6 * part + model), by_step(0) + [(0, 3 * part + at, *rest) for _, at, *rest in second])],
        qkv_weight,
        proj_weight,
    )
    if on_grid:
        others = net.planes_of(shard)
    starts = [at for g in range(GROUPS) for at in step_starts(g)]
    one = [(0, 0, model)]
    vecs = pack(
        [(GAIN1, one), (SHIFT1, one), (GAIN2, one), (SHIFT2, one), (PROJ_SHIFT, one), (OUT_SHIFT, one)]
        + [(QKV_SHIFT, [(k * LANES, at, LANES) for k, at in enumerate(starts)]), (FC_SHIFT, [(0, 0, hidden_units)])],
        hidden_units,
        ln1_gain,
        ln1_bias,
        ln2_gain,
        ln2_bias,
        proj_bias,
        out_bias,
        qkv_bias,
        fc_bias,
    )
    hidden, hidden_low, kv_local = prefix_forward(
        prefix_emb, rep_weight1.T, rep_bias1, rep_weight2, rep_bias2, 3 * part if on_grid else 0
    )

    def run_hidden(j, so_far, normed2, w_in, w_out, ties=()):
        back = (mixes, pprobs, qkvs, prefix_kv)
        w_last = w_proj if j == CHUNKS - 1 else None
        return hidden_part(j, normed2, og, vecs, mid, so_far, w_in, w_out, w_last, back, ties)

    so_far = None
    if not on_grid:
        prefix_kv = lax.all_gather(kv_local, "pre", axis=1, tiled=True)
        w_qkv = [net.gather(shard[:, g * 3 * part : (g + 1) * 3 * part]) for g in range(GROUPS)]
        w_proj = net.gather(proj_weight)
        out_all = lax.all_gather(out_weight, ALL, axis=0, tiled=True)
        normed1, bias = first_norm(x, vecs), mask_bias(seg_ids, valid, prefix_len)
        qkvs, mixes, probs, pprobs = zip(
            *[attend(g, normed1, w_qkv[g], vecs, prefix_kv, bias) for g in range(GROUPS)], strict=True
        )
        mid, normed2 = middle_block(mixes, x, w_proj, vecs)
        for j in range(CHUNKS):
            w_in = net.gather(fc_weight[:, j * width : (j + 1) * width])
            w_out = Weight(net, [out_all], width, [(0, j * width, lambda: 0)], width, model)
            so_far = run_hidden(j, so_far, normed2, w_in, w_out)
    else:
        def send_lines(parts, ties):
            return gather_lines(net, parts, planes_h, own_o, own_q, ties)

        rows, wide = net.planes * own_q, 3 * part + model
        normed1, bias = first_norm(x, vecs), mask_bias(seg_ids, valid, prefix_len)
        (line_a,) = arrange(
            [
                (
                    (rows + PW, 3 * part),
                    [(k * own_q, 0, k, 0, 0, own_q, 3 * part) for k in range(net.planes)]
                    + [(rows, 0, net.planes, 0, 0, PW, 3 * part)],
                ),
            ],
            shard,
            *others,
            kv_local,
            ties=(normed1, bias),
        )
        (shard_h,) = arrange(
            [
                (
                    (own_o + CHUNKS * own_q, model),
                    [(0, 0, 0, 0, 0, own_o, model)]
                    + [(own_o + j * own_q, 0, 1, 0, j * width, own_q, width) for j in range(CHUNKS)],
                )
            ],
            out_weight,
            fc_weight,
            ties=(line_a,),
        )
        planes_h = net.planes_by_relay(shard_h)
        near_a, far_a = net.beside(line_a, False), net.beside(line_a, True)
        end_a = net.across(line_a)
        (line_b,) = arrange(
            [((rows, wide), [(k * own_q, 0, k, 0, 3 * part, own_q, wide) for k in range(net.planes)])],
            shard,
            *others,
            ties=(shard_h,),
        )
        near_b, far_b = net.beside(line_b, False), net.beside(line_b, True)
        end_b = net.beside(near_b, True)
        w_a = net.weight(net.arrays_of(line_a, near_a, far_a, end_a), own_q, 3 * part)
        qkv_a, mix_a, probs_a, pprobs_a, prefix_kv = attend(0, normed1, w_a, vecs, None, bias, (near_b, planes_h[1], planes_h[2]))
        far_b, end_b = gate((far_b, end_b), (mix_a,))
        lines = list(send_lines((0, 1), (far_b, end_b)))
        arrays_b = net.arrays_of(line_b, near_b, far_b, end_b)
        w_b, w_proj = net.weight(arrays_b, own_q, 3 * part), net.weight(arrays_b, own_q, model, 3 * part)
        nears = [net.beside(a, False) for a in lines]
        fars = [net.beside(a, True) for a in lines]
        qkv_b, mix_b, probs_b, pprobs_b = attend(1, normed1, w_b, vecs, prefix_kv, bias, tuple(lines))
        ends = [net.beside(after(a, mix_b), True) for a in nears]
        mid, normed2 = middle_block([mix_a, mix_b], x, w_proj, vecs, tuple(nears))
        lines += send_lines((2, 3), (mid, ends[0]))
        nears += [net.beside(a, False) for a in lines[2:]]
        fars += [net.beside(a, True) for a in lines[2:]]
        w_qkv, qkvs, probs = [w_a, w_b], [qkv_a, qkv_b], [probs_a, probs_b]
        mixes, pprobs = [mix_a, mix_b], [pprobs_a, pprobs_b]
        latest = mid
        for j in range(CHUNKS):
            arrays = net.arrays_of(lines[j], nears[j], after(fars[j], latest), after(ends[j], latest))
            w_in, w_out = net.hidden_weights(arrays, own_q, own_o)
            ties = tuple(lines[2:]) if j == 0 else ()
            if 0 < j < CHUNKS - 1:
                ends.append(net.beside(after(nears[j + 1], latest), True))
                ties = (nears[j + 1],)
            so_far = run_hidden(j, so_far, normed2, w_in, w_out, ties)
            latest = so_far[0]
    output, grad_mid, grad_attn, prefix_grad = so_far
    rest = (x, grad_mid, vecs)
    if on_grid:
        mine, other = net.sum_cores(prefix_grad)
        terms = net.send_across(mine, other)
        so_far = attend_back(0, qkvs[0], probs[0], prefix_kv, grad_attn, None, w_qkv[0], ties=(mine, other))
        plane = add_terms(terms)
        sums = [plane, *net.planes_of(plane)]
        in_grad = attend_back(1, qkvs[1], probs[1], prefix_kv, grad_attn, so_far, w_qkv[1], rest, ties=(plane,))
    else:
        sums = net.sum_columns(prefix_grad)
        so_far = attend_back(0, qkvs[0], probs[0], prefix_kv, grad_attn, None, w_qkv[0])
        in_grad = attend_back(1, qkvs[1], probs[1], prefix_kv, grad_attn, so_far, w_qkv[1], rest)
    weight2_grad, bias2_grad, hid_grad = second_layer_back(sums, prefix_len, hidden_low, rep_weight2)
    hid_grads = net.over_pre(hid_grad)
    weight1_grad, bias1_grad, emb_grad = first_layer_back(hid_grads, hidden, prefix_emb, rep_weight1.T)
    return output[None], in_grad[None], emb_grad, weight1_grad.T, bias1_grad, weight2_grad, bias2_grad


def solution(mesh):
    split_all = P(ALL, None)
    whole = P()
    return jax.shard_map(
        per_device,
        mesh=mesh,
        in_specs=(
            P(ALL, None, None),
            split_all,
            split_all,
            P(ALL, None, None),
            whole,
            whole,
            split_all,
            whole,
            split_all,
            whole,
            whole,
            whole,
            split_all,
            whole,
            split_all,
            whole,
            whole,
            whole,
            whole,
            P(None, "pre"),
            P("pre"),
        ),
        out_specs=(
            P(ALL, None, None),
            P(ALL, None, None),
            whole,
            whole,
            whole,
            P(None, "pre"),
            P("pre"),
        ),
        check_vma=False,
    )
```

```python
import functools

import jax
import jax.numpy as jnp
from jax import lax
from jax.experimental import pallas as pl
from jax.experimental.pallas import tpu as pltpu
from jax.sharding import PartitionSpec as P

f32 = jnp.float32
bf16 = jnp.bfloat16
ALL = ("rows", "pre")
NEG = -1e30
EPS = 1e-05
HD = 64
SPAN = 256
BQ = 128
PW = 16
LANES = 256
HEADS = LANES // HD
GROUPS = 2
GROUP_STEPS = 2
CHUNKS = 4
BM = 256
BIG = 512
LIMIT = 58
ROOM = 52
SUB = 256

NN = (((1,), (0,)), ((), ()))
NT = (((1,), (1,)), ((), ()))
TN = (((0,), (0,)), ((), ()))


def dot(a, b, dims=NN):
    return lax.dot_general(a, b, dims, preferred_element_type=f32)


def params(mebibytes):
    return pltpu.CompilerParams(vmem_limit_bytes=mebibytes << 20)


def cost(microseconds):
    return pl.CostEstimate(flops=int(microseconds * 1.65e+08), bytes_accessed=1, transcendentals=0)


class Weight:
    def __init__(self, net, arrays, block, pieces, rows, cols, at=0):
        self.net, self.arrays, self.block, self.pieces = net, arrays, block, pieces
        self.rows, self.cols, self.at = rows, cols, at

    def specs(self):
        return [pl.BlockSpec(memory_space=pl.ANY) for _ in self.arrays]

    def count(self):
        return len(self.arrays)

    def scratch(self):
        return [pltpu.VMEM((self.rows, self.cols), bf16), pltpu.SemaphoreType.DMA]


def start_load(w, refs, whole, sem, at=0, cols=None):
    cols = cols or w.cols
    here = w.net.position()
    for array, row, place in w.pieces:
        first = pl.multiple_of(place(*here), w.block)
        pltpu.make_async_copy(
            refs[array].at[pl.ds(row, w.block), pl.ds(w.at + at, cols)],
            whole.at[pl.ds(first, w.block), pl.ds(at, cols)],
            sem,
        ).start()


def wait_load(whole, sem):
    pltpu.make_async_copy(whole, whole, sem).wait()


def tied(kernel, count):
    return lambda *refs: kernel(*refs[count:])


def tie_specs(ties):
    return [pl.BlockSpec(memory_space=pl.ANY)] * len(ties)


def arrange(plan, *arrays, ties=()):
    def kernel(*refs):
        ins, outs, sems = refs[: len(arrays)], refs[len(arrays) + len(ties) : -1], refs[-1]
        for k, (_, parts) in enumerate(plan):
            for row, col, array, from_row, from_col, rows, cols in parts:
                pltpu.make_async_copy(
                    ins[array].at[pl.ds(from_row, rows), pl.ds(from_col, cols)],
                    outs[k].at[pl.ds(row, rows), pl.ds(col, cols)],
                    sems.at[k],
                ).start()
        for k in range(len(plan)):
            pltpu.make_async_copy(outs[k], outs[k], sems.at[k]).wait()

    return pl.pallas_call(
        kernel,
        grid=(1,),
        in_specs=[pl.BlockSpec(memory_space=pl.ANY)] * (len(arrays) + len(ties)),
        out_specs=[whole_spec(shape) for shape, _ in plan],
        out_shape=[jax.ShapeDtypeStruct(shape, bf16) for shape, _ in plan],
        scratch_shapes=[pltpu.SemaphoreType.DMA((len(plan),))],
        compiler_params=params(12),
        cost_estimate=cost(0),
        name="arrange",
    )(*arrays, *ties)


def gate(arrays, ties):
    n = len(arrays)
    spec = pl.BlockSpec(memory_space=pl.ANY)
    return pl.pallas_call(
        lambda *refs: None,
        grid=(1,),
        in_specs=[spec] * (n + len(ties)),
        out_specs=[spec] * n,
        out_shape=[jax.ShapeDtypeStruct(a.shape, a.dtype) for a in arrays],
        input_output_aliases={i: i for i in range(n)},
        compiler_params=params(LIMIT),
        cost_estimate=cost(1),
        name="gate",
    )(*arrays, *ties)


def join(*arrays, ties=()):
    parts, at = [], 0
    for k, a in enumerate(arrays):
        parts.append((at, 0, k, 0, 0, *a.shape))
        at += a.shape[0]
    return arrange([((at, arrays[0].shape[1]), parts)], *arrays, ties=ties)[0]


GAIN1, SHIFT1, GAIN2, SHIFT2, PROJ_SHIFT, OUT_SHIFT, QKV_SHIFT, FC_SHIFT = range(8)


def pack_kernel(plan, *refs):
    out = refs[-1]
    out[...] = jnp.zeros_like(out)
    for ref, row in zip(refs[:-1], plan, strict=True):
        for at, start, size in row[1]:
            out[pl.ds(row[0], 1), pl.ds(at, size)] = ref[pl.ds(start, size)].astype(f32).reshape(1, size)


def pack(plan, width, *vectors):
    return pl.pallas_call(
        functools.partial(pack_kernel, plan),
        grid=(1,),
        in_specs=[whole_spec(v.shape) for v in vectors],
        out_specs=whole_spec((8, width)),
        out_shape=jax.ShapeDtypeStruct((8, width), f32),
        compiler_params=params(LIMIT),
        cost_estimate=cost(0),
        name="pack",
    )(*vectors)


def row_of(ref, row, size, at=0):
    return ref[pl.ds(row, 1), pl.ds(at, size)]


def norm(values):
    center = values - jnp.mean(values, axis=-1, keepdims=True)
    rate = lax.rsqrt(jnp.mean(center * center, axis=-1, keepdims=True) + EPS)
    return center * rate, rate


def norm_back(values, gain, grad):
    n, rate = norm(values)
    w = grad * gain
    return rate * (
        w - jnp.mean(w, axis=-1, keepdims=True) - n * jnp.mean(w * n, axis=-1, keepdims=True)
    )


def rows_spec(cols, at=0, rows=None):
    return pl.BlockSpec((rows or BM, cols), lambda i: (i, at))


def whole_spec(shape):
    return pl.BlockSpec(shape, lambda i: (0,) * len(shape))


def middle_kernel(w, *refs):
    parts, (x_ref, v_ref), refs = refs[:GROUPS], refs[GROUPS : GROUPS + 2], refs[GROUPS + 2 :]
    wr = refs[: w.count()]
    mid_ref, n_ref, whole, sem = refs[w.count() :]
    model = w.cols

    @pl.when(pl.program_id(0) == 0)
    def _():
        start_load(w, wr, whole, sem)
        wait_load(whole, sem)

    for i in range(0, x_ref.shape[0], BM):
        at = pl.ds(i, BM)
        attn = jnp.concatenate([p[at, :] for p in parts], 1)
        mid = x_ref[at, :].astype(f32) + (dot(attn, whole[...]) + row_of(v_ref, PROJ_SHIFT, model))
        mid_ref[at, :] = mid.astype(bf16)
        n_ref[at, :] = (norm(mid)[0] * row_of(v_ref, GAIN2, model) + row_of(v_ref, SHIFT2, model)).astype(bf16)


def middle_block(parts, x, w, vecs, ties=()):
    length, model = x.shape
    return pl.pallas_call(
        tied(functools.partial(middle_kernel, w), len(ties)),
        grid=(length // BIG,),
        in_specs=tie_specs(ties) + [rows_spec(p.shape[1], rows=BIG) for p in parts] + [rows_spec(model, rows=BIG), whole_spec(vecs.shape)] + w.specs(),
        out_specs=[rows_spec(model, rows=BIG)] * 2,
        out_shape=[
            jax.ShapeDtypeStruct((length, model), bf16),
            jax.ShapeDtypeStruct((length, model), bf16),
        ],
        scratch_shapes=w.scratch(),
        compiler_params=params(ROOM),
        cost_estimate=cost(8.5),
        name="middle_block",
    )(*ties, *parts, x, vecs, *w.arrays)


def gelu_both(v):
    c, a = 0.7978845608, 0.044715
    sq = v * v
    t = jnp.tanh(v * (c + (c * a) * sq))
    half = 0.5 + 0.5 * t
    act = v * half
    slope = half + (0.5 * v) * (1.0 - t * t) * (c + (3.0 * c * a) * sq)
    return act, slope


def hidden_kernel(w_in, w_out, w_proj, chunk, *refs):
    refs = list(refs)
    first, last = chunk == 0, w_proj is not None
    model, width = w_in.rows, w_in.cols
    (n_ref, og_ref, v_ref), refs = refs[:3], refs[3:]
    if first or last:
        mid_ref = refs.pop(0)
    if not first:
        (out_in, gn_in), refs = refs[:2], refs[2:]
    if last:
        back, refs = refs[: BACK_REFS], refs[BACK_REFS:]
    wi, refs = refs[: w_in.count()], refs[w_in.count() :]
    wo, refs = refs[: w_out.count()], refs[w_out.count() :]
    if last:
        wp, refs = refs[: w_proj.count()], refs[w_proj.count() :]
        (out_ref, gm_ref, ga_ref, dp_ref), refs = refs[:4], refs[4:]
    else:
        (out_ref, gn_ref), refs = refs[:2], refs[2:]
    fc, fc_sem, ow, ow_sem = refs[:4]

    step = pl.program_id(0)

    @pl.when(step == 0)
    def _():
        start_load(w_out, wo, ow, ow_sem)
        start_load(w_in, wi, fc, fc_sem)
        if last:
            start_load(w_proj, wp, refs[4], refs[5])
            start_back(back, refs[6:11])
        wait_load(ow, ow_sem)
        wait_load(fc, fc_sem)
        if last:
            wait_load(refs[4], refs[5])

    normed, og = n_ref[...], og_ref[...]
    acts, grads = [], []
    for j in range(0, width, SUB):
        at = pl.ds(j, SUB)
        act, slope = gelu_both(dot(normed, fc[:, at]) + row_of(v_ref, FC_SHIFT, SUB, chunk * width + j))
        acts.append(act.astype(bf16))
        grads.append((dot(og, ow[at, :], NT) * slope).astype(bf16))
    gn = dot(jnp.concatenate(grads, 1), fc[...], NT)
    if not first:
        gn = gn + gn_in[...].astype(f32)
    if last:
        gm = og.astype(f32) + norm_back(mid_ref[...].astype(f32), row_of(v_ref, GAIN2, model), gn)
        low = gm.astype(bf16)
    out = dot(jnp.concatenate(acts, 1), ow[...])
    if first:
        out = out + (mid_ref[...].astype(f32) + row_of(v_ref, OUT_SHIFT, model))
    else:
        out = out + out_in[...].astype(f32)
    out_ref[...] = out.astype(bf16)
    if last:
        gm_ref[...] = low
        ga = dot(low, refs[4][...], NT).astype(bf16)
        ga_ref[...] = ga
        refs[9][pl.ds(pl.multiple_of(step * BM, BM), BM), :] = ga

        @pl.when(step == pl.num_programs(0) - 1)
        def _():
            finish_back(back[-1], dp_ref, refs[6:11])
    else:
        gn_ref[...] = gn.astype(bf16)


BACK_REFS = 2 * GROUPS + GROUPS + 1


def start_back(refs, scratch):
    mixes, probs, qkvs = refs[:GROUPS], refs[GROUPS : 2 * GROUPS], refs[2 * GROUPS : 3 * GROUPS]
    q_all, mix_all, p_all, _, sems = scratch[:5]
    wide = GROUP_STEPS * LANES
    for g in range(GROUPS):
        rows = probs[g].shape[0]
        pltpu.make_async_copy(probs[g], p_all.at[pl.ds(g * rows, rows)], sems.at[0]).start()
        pltpu.make_async_copy(mixes[g], mix_all.at[:, pl.ds(g * wide, wide)], sems.at[1]).start()
        for k in range(GROUP_STEPS):
            pltpu.make_async_copy(
                qkvs[g].at[:, pl.ds(3 * LANES * k, LANES)], q_all.at[:, pl.ds(g * wide + k * LANES, LANES)], sems.at[2]
            ).start()


def own_head(rows, each, model):
    head = lax.broadcasted_iota(jnp.int32, (rows, model), 0) // each
    return head == lax.broadcasted_iota(jnp.int32, (rows, model), 1) // HD


def finish_back(pv_ref, dp_ref, scratch):
    q_all, mix_all, p_all, do_all, sems = scratch
    for k, ref in enumerate((p_all, mix_all, q_all)):
        pltpu.make_async_copy(ref, ref, sems.at[k]).wait()
    model = do_all.shape[1]
    heads = model // HD
    do = do_all[...]
    own = own_head(heads * PW, PW, model)
    pv = jnp.concatenate([pv_ref[...]] * heads, 0)
    dp = dot(jnp.where(own, pv, jnp.zeros_like(pv)), do, NT)
    ones = jnp.where(own_head(heads, 1, model), 1.0, 0.0).astype(bf16)
    delta = dot(ones, (do.astype(f32) * mix_all[...].astype(f32)).astype(bf16), NT)
    delta = jnp.concatenate([jnp.broadcast_to(delta[h : h + 1], (PW, delta.shape[1])) for h in range(heads)], 0)
    p = p_all[...]
    ds = (p.astype(f32) * (dp - delta)).astype(bf16)
    for k, (total, scale) in enumerate(((dot(ds, q_all[...]), HD**-0.5), (dot(p, do), 1.0))):
        kept = jnp.where(own, total, 0.0)
        dp_ref[k] = sum(kept[h * PW : (h + 1) * PW] for h in range(heads)) * scale


def hidden_part(chunk, normed, og, vecs, mid, so_far, w_in, w_out, w_proj, back, ties=()):
    length, model = og.shape
    first, last = chunk == 0, w_proj is not None
    full = rows_spec(model)
    specs, args = [full, full, whole_spec(vecs.shape)], [normed, og, vecs]
    if first or last:
        specs, args = specs + [full], args + [mid]
    if not first:
        specs, args = specs + [full, full], args + list(so_far)
    if last:
        mixes, probs, qkvs, prefix_kv = back
        specs = specs + tie_specs([*mixes, *probs, *qkvs]) + [pl.BlockSpec((PW, model), lambda i: (0, 1))]
        args = args + [*mixes, *probs, *qkvs, prefix_kv]
    specs, args = specs + w_in.specs() + w_out.specs(), args + list(w_in.arrays) + list(w_out.arrays)
    scratch = w_in.scratch() + w_out.scratch()
    outs = [bf16, bf16]
    if last:
        specs, args = specs + w_proj.specs(), args + list(w_proj.arrays)
        scratch = scratch + w_proj.scratch()
        scratch = scratch + [
            pltpu.VMEM((length, model), bf16),
            pltpu.VMEM((length, model), bf16),
            pltpu.VMEM((model // HD * PW, length), bf16),
            pltpu.VMEM((length, model), bf16),
            pltpu.SemaphoreType.DMA((3,)),
        ]
        outs = [bf16, bf16, bf16]
    out_specs = [full] * len(outs)
    out_shape = [jax.ShapeDtypeStruct((length, model), t) for t in outs]
    if last:
        out_specs = out_specs + [whole_spec((2, PW, model))]
        out_shape = out_shape + [jax.ShapeDtypeStruct((2, PW, model), f32)]
    return pl.pallas_call(
        tied(functools.partial(hidden_kernel, w_in, w_out, w_proj, chunk), len(ties)),
        grid=(length // BM,),
        in_specs=tie_specs(ties) + specs,
        out_specs=out_specs,
        out_shape=out_shape,
        scratch_shapes=scratch,
        compiler_params=params(ROOM),
        cost_estimate=cost(25 if last else 15),
        name="hidden_part",
    )(*ties, *args)


def spans(length):
    out, at = [], 0
    for first in range(0, length, BQ):
        key = max(0, first - SPAN)
        keys = PW + first + BQ - key
        out.append((first, key, keys, at))
        at += keys
    return out, at


def mask_kernel(length, prefix, seg_ref, valid_ref, o_ref):
    keyed = jnp.where(valid_ref[...] > 0, seg_ref[...], -1).astype(f32)
    columns = [jnp.broadcast_to(keyed[:, i : i + BQ], (BQ, BQ)).T for i in range(0, length, BQ)]
    column = jnp.concatenate(columns, 0)
    for first, key, keys, at in spans(length)[0]:
        n = keys - PW
        pad = lax.broadcasted_iota(jnp.int32, (PW, BQ), 0) < prefix
        o_ref[pl.ds(at, PW), :] = jnp.where(pad, 0.0, NEG)
        key_at = key + lax.broadcasted_iota(jnp.int32, (n, BQ), 0)
        query_at = first + lax.broadcasted_iota(jnp.int32, (n, BQ), 1)
        seen = (column[key : key + n] == seg_ref[:, pl.ds(first, BQ)].astype(f32)) & (key_at <= query_at)
        o_ref[pl.ds(at + PW, n), :] = jnp.where(seen, 0.0, NEG)


def mask_bias(seg, valid, prefix, ties=()):
    length = seg.shape[1]
    total = spans(length)[1]
    return pl.pallas_call(
        tied(functools.partial(mask_kernel, length, prefix), len(ties)),
        grid=(1,),
        in_specs=tie_specs(ties) + [whole_spec((1, length))] * 2,
        out_specs=whole_spec((total, BQ)),
        out_shape=jax.ShapeDtypeStruct((total, BQ), f32),
        compiler_params=params(16),
        cost_estimate=cost(0),
        name="mask_bias",
    )(*ties, seg, valid)


def first_norm_kernel(x_ref, v_ref, o_ref):
    model = x_ref.shape[1]
    normed = norm(x_ref[...].astype(f32))[0]
    o_ref[...] = (normed * row_of(v_ref, GAIN1, model) + row_of(v_ref, SHIFT1, model)).astype(bf16)


def first_norm(x, vecs, ties=()):
    length, model = x.shape
    return pl.pallas_call(
        tied(first_norm_kernel, len(ties)),
        grid=(length // BM,),
        in_specs=tie_specs(ties) + [rows_spec(model), whole_spec(vecs.shape)],
        out_specs=rows_spec(model),
        out_shape=jax.ShapeDtypeStruct((length, model), bf16),
        compiler_params=params(16),
        cost_estimate=cost(0),
        name="first_norm",
    )(*ties, x, vecs)


def of_head(shape, head):
    lane = lax.broadcasted_iota(jnp.int32, shape, 1)
    return (lane >= HD * head) & (lane < HD * (head + 1))


def stack_heads(q):
    return jnp.concatenate([jnp.where(of_head(q.shape, h), q, jnp.zeros_like(q)) for h in range(HEADS)], 0)


def pick_heads(o):
    out = o[:BQ]
    for h in range(1, HEADS):
        out = jnp.where(of_head(out.shape, h), o[h * BQ : (h + 1) * BQ], out)
    return out


def attend_kernel(length, group, w, collect, *refs):
    (x_ref, v_ref, bias_ref), refs = refs[:3], refs[3:]
    if not collect:
        kv_ref, refs = refs[0], refs[1:]
    wr, refs = refs[: w.count()], refs[w.count() :]
    (qkv_hbm, o_ref, p_hbm, pp_ref), refs = refs[:4], refs[4:]
    if collect:
        kv_ref, refs = refs[0], refs[1:]
    (whole, sem, qkv_all, p_all, out_sem), refs = refs[:5], refs[5:]
    plan = spans(length)[0]
    step = pl.program_id(0)
    width = 3 * LANES
    qkv_ref, p_ref = qkv_all.at[step], p_all.at[step]

    def qkv_copy(k):
        return pltpu.make_async_copy(
            qkv_all.at[k], qkv_hbm.at[:, pl.ds(pl.multiple_of(k * width, width), width)], out_sem.at[0, k]
        )

    @pl.when(step == 0)
    def _():
        if collect:
            start_collect(w, wr, kv_ref.shape[1], *refs)
        for k in range(GROUP_STEPS):
            start_load(w, wr, whole, sem.at[k], k * width, width)
        if collect:
            wait_load(*refs)
            kv_ref[...] = refs[0][0]

    for k in range(GROUP_STEPS):

        @pl.when(step == k)
        def _():
            wait_load(whole.at[:, pl.ds(k * width, width)], sem.at[k])

    lane = pl.multiple_of((group * GROUP_STEPS + step) * LANES, LANES)
    pk = kv_ref[:, pl.ds(lane, LANES)]
    pv = kv_ref[:, pl.ds(kv_ref.shape[1] // 2 + lane, LANES)]

    at = pl.multiple_of(step * 3 * LANES, 3 * LANES)
    shift = row_of(v_ref, QKV_SHIFT, 3 * LANES, group * GROUP_STEPS * 3 * LANES + at)
    qkv_ref[...] = (dot(x_ref[...], whole[:, pl.ds(at, 3 * LANES)]) + shift).astype(bf16)
    qkv_copy(step).start()

    def score(i):
        first, key, keys, _ = plan[i]
        q = qkv_ref[pl.ds(first, BQ), pl.ds(0, LANES)] * jnp.asarray(HD**-0.5, bf16)
        ks = jnp.concatenate([pk, qkv_ref[pl.ds(key, keys - PW), pl.ds(LANES, LANES)]], 0)
        return dot(ks, stack_heads(q), NT)

    def soft(i, s):
        first, _, keys, at = plan[i]
        s = s + jnp.concatenate([bias_ref[pl.ds(at, keys), :]] * HEADS, 1)
        e = jnp.exp(s - jnp.max(s, axis=0, keepdims=True))
        probs = (e * (1.0 / jnp.sum(e, axis=0, keepdims=True))).astype(bf16)
        rows = pl.ds(at, keys)
        p_ref[rows, :] = probs
        pltpu.make_async_copy(p_ref.at[rows], p_hbm.at[step, rows], out_sem.at[1, step]).start()
        for h in range(HEADS):
            pp_ref[pl.ds(h * PW, PW), pl.ds(first, BQ)] = probs[:PW, h * BQ : (h + 1) * BQ]
        return probs

    def mix(i, probs):
        first, key, keys, _ = plan[i]
        vs = jnp.concatenate([pv, qkv_ref[pl.ds(key, keys - PW), pl.ds(2 * LANES, LANES)]], 0)
        o_ref[pl.ds(first, BQ), :] = pick_heads(dot(probs, vs, TN)).astype(bf16)

    n = len(plan)
    s, held = score(0), None
    for i in range(n):
        later = score(i + 1) if i + 1 < n else None
        probs = soft(i, s)
        if held is not None:
            mix(i - 1, held)
        s, held = later, probs
    mix(n - 1, held)

    @pl.when(step == GROUP_STEPS - 1)
    def _():
        for k in range(GROUP_STEPS):
            qkv_copy(k).wait()
            pltpu.make_async_copy(p_all.at[k], p_hbm.at[k], out_sem.at[1, k]).wait()


def start_collect(w, refs, cols, kv, sem):
    here = w.net.position()
    part = cols // 4
    for array in range(len(refs)):
        x, y, c = w.net.source(array, *here[1:])
        at = pl.multiple_of((2 * y + c) * part, part)
        pltpu.make_async_copy(
            refs[array].at[pl.ds(w.net.planes * w.block, PW), pl.ds(0, part)],
            kv.at[(x + here[1]) % 2, :, pl.ds(at, part)],
            sem,
        ).start()


def attend(group, x, w, vecs, prefix_kv, bias, ties=()):
    length, model = x.shape
    steps = w.cols // (3 * LANES)
    total = spans(length)[1]
    collect = prefix_kv is None
    kv_spec = whole_spec((PW, 2 * model))
    out_specs = [
        pl.BlockSpec(memory_space=pl.ANY),
        pl.BlockSpec((length, LANES), lambda i: (0, i)),
        pl.BlockSpec(memory_space=pl.ANY),
        pl.BlockSpec((HEADS * PW, length), lambda i: (i, 0)),
    ]
    out_shape = [
        jax.ShapeDtypeStruct((length, w.cols), bf16),
        jax.ShapeDtypeStruct((length, steps * LANES), bf16),
        jax.ShapeDtypeStruct((steps, total, HEADS * BQ), bf16),
        jax.ShapeDtypeStruct((steps * HEADS * PW, length), bf16),
    ]
    scratch = [pltpu.VMEM((w.rows, w.cols), bf16), pltpu.SemaphoreType.DMA((GROUP_STEPS,))]
    scratch = scratch + [
        pltpu.VMEM((steps, length, 3 * LANES), bf16),
        pltpu.VMEM((steps, total, HEADS * BQ), bf16),
        pltpu.SemaphoreType.DMA((2, steps)),
    ]
    if collect:
        out_specs.append(kv_spec)
        out_shape.append(jax.ShapeDtypeStruct((PW, 2 * model), bf16))
        scratch = scratch + [pltpu.VMEM((2, PW, 2 * model), bf16), pltpu.SemaphoreType.DMA]
    return pl.pallas_call(
        tied(functools.partial(attend_kernel, length, group, w, collect), len(ties)),
        grid=(steps,),
        in_specs=tie_specs(ties)
        + [whole_spec(x.shape), whole_spec(vecs.shape), whole_spec((total, BQ))]
        + ([] if collect else [kv_spec])
        + w.specs(),
        out_specs=out_specs,
        out_shape=out_shape,
        scratch_shapes=scratch,
        compiler_params=params(ROOM),
        cost_estimate=cost(8 * steps),
        name="attend",
    )(*ties, x, vecs, bias, *([] if collect else [prefix_kv]), *w.arrays)


def prefix_specs(steps, first):
    return [pl.BlockSpec((PW, LANES), lambda i, at=at: (0, at + first + i)) for at in (0, steps)]


def attend_back_kernel(length, w, first, last, *refs):
    (qkv_ref, p_ref, pk_ref, pv_ref, do_ref), refs = refs[:5], refs[5:]
    if not first:
        gn_in, refs = refs[0], refs[1:]
    if last:
        (x_hbm, gm_hbm, v_ref), refs = refs[:3], refs[3:]
    wr, refs = refs[: w.count()], refs[w.count() :]
    (out_ref, gn, ak, av, dqkv, whole, sem, io_sem), refs = refs[:8], refs[8:]
    step, steps = pl.program_id(0), pl.num_programs(0)
    if not first:
        gn_vm, refs = refs[0], refs[1:]
    copies = [] if first else [pltpu.make_async_copy(gn_in, gn_vm, io_sem.at[0])]
    if last:
        x_vm, gm_vm = refs
        copies.append(pltpu.make_async_copy(x_hbm, x_vm, io_sem.at[1]))
        copies.append(pltpu.make_async_copy(gm_hbm, gm_vm, io_sem.at[2]))

    @pl.when(step == 0)
    def _():
        start_load(w, wr, whole, sem)
        for copy in copies:
            copy.start()

    ak[...] = jnp.zeros_like(ak)
    av[...] = jnp.zeros_like(av)
    plan = spans(length)[0]

    def scores(i):
        first, key, keys, _ = plan[i]
        dos = stack_heads(do_ref[pl.ds(first, BQ), :])
        vs = jnp.concatenate([pv_ref[...], qkv_ref[pl.ds(key, keys - PW), pl.ds(2 * LANES, LANES)]], 0)
        return dos, dot(vs, dos, NT)

    def soft(i, dos, dp):
        _, _, keys, at = plan[i]
        probs = p_ref[0, pl.ds(at, keys), :]
        wide = probs.astype(f32)
        t = wide * dp
        return dos, probs, (t - wide * jnp.sum(t, axis=0, keepdims=True)).astype(bf16)

    def mix(i, dos, probs, ds):
        first, key, keys, _ = plan[i]
        n = keys - PW
        qs = stack_heads(qkv_ref[pl.ds(first, BQ), pl.ds(0, LANES)] * jnp.asarray(HD**-0.5, bf16))
        ks = jnp.concatenate([pk_ref[...], qkv_ref[pl.ds(key, n), pl.ds(LANES, LANES)]], 0)
        ak[pl.ds(key, n), :] += dot(ds[PW:], qs)
        av[pl.ds(key, n), :] += dot(probs[PW:], dos)
        dqkv[pl.ds(first, BQ), pl.ds(0, LANES)] = (pick_heads(dot(ds, ks, TN)) * HD**-0.5).astype(bf16)

    n = len(plan)
    s, held = scores(0), None
    for i in range(n):
        later = scores(i + 1) if i + 1 < n else None
        done = soft(i, *s)
        if held is not None:
            mix(i - 1, *held)
        s, held = later, done
    mix(n - 1, *held)
    dqkv[:, pl.ds(LANES, LANES)] = ak[...].astype(bf16)
    dqkv[:, pl.ds(2 * LANES, LANES)] = av[...].astype(bf16)

    @pl.when(step == 0)
    def _():
        wait_load(whole, sem)

    mine = whole[:, pl.ds(pl.multiple_of(step * 3 * LANES, 3 * LANES), 3 * LANES)]

    @pl.when(step == 0)
    def _():
        part = dot(dqkv[...], mine, NT)
        if first:
            gn[...] = part
        else:
            copies[0].wait()
            gn[...] = part + gn_vm[...].astype(f32)

    @pl.when((step > 0) & (step < steps - 1))
    def _():
        gn[...] += dot(dqkv[...], mine, NT)

    @pl.when(step == steps - 1)
    def _():
        for copy in copies[-2:] if last else []:
            copy.wait()
        for i in range(0, length, BM):
            at = pl.ds(i, BM)
            grad = gn[at, :] + dot(dqkv[at, :], mine, NT)
            if last:
                back = norm_back(x_vm[at, :].astype(f32), row_of(v_ref, GAIN1, out_ref.shape[1]), grad)
                grad = gm_vm[at, :].astype(f32) + back
            out_ref[at, :] = grad.astype(bf16)


def attend_back(group, qkv, probs, prefix_kv, do, so_far, w, rest=None, ties=()):
    length, model = do.shape
    steps = GROUP_STEPS
    total = spans(length)[1]
    first, last = so_far is None, rest is not None
    hbm = pl.BlockSpec(memory_space=pl.ANY)
    args = [qkv, probs, prefix_kv, prefix_kv, do]
    specs = [
        pl.BlockSpec((length, 3 * LANES), lambda i: (0, i)),
        pl.BlockSpec((1, total, HEADS * BQ), lambda i: (i, 0, 0)),
        *prefix_specs(GROUPS * steps, group * steps),
        pl.BlockSpec((length, LANES), lambda i: (0, group * steps + i)),
    ]
    if not first:
        args, specs = args + [so_far], specs + [hbm]
    if last:
        args, specs = args + list(rest), specs + [hbm, hbm, whole_spec(rest[2].shape)]
    scratch = [pltpu.VMEM((length, model), f32)] + [pltpu.VMEM((length, LANES), f32)] * 2
    scratch = scratch + [pltpu.VMEM((length, 3 * LANES), bf16)] + w.scratch() + [pltpu.SemaphoreType.DMA((3,))]
    if not first:
        scratch = scratch + [pltpu.VMEM((length, model), bf16)]
    if last:
        scratch = scratch + [pltpu.VMEM((length, model), bf16)] * 2
    return pl.pallas_call(
        tied(functools.partial(attend_back_kernel, length, w, first, last), len(ties)),
        grid=(steps,),
        in_specs=tie_specs(ties) + specs + w.specs(),
        out_specs=whole_spec((length, model)),
        out_shape=jax.ShapeDtypeStruct((length, model), bf16),
        scratch_shapes=scratch,
        compiler_params=params(LIMIT),
        cost_estimate=cost(17),
        name="attend_back",
    )(*ties, *args, *w.arrays)


def prefix_kernel(e_ref, w1_ref, b1_ref, w2_ref, b2_ref, h_ref, low_ref, kv_ref):
    rows, model = e_ref.shape
    emb = jnp.concatenate([e_ref[...].astype(f32), jnp.zeros((PW - rows, model), f32)], 0).astype(bf16)
    mid, cols = b1_ref.shape[0], b2_ref.shape[0]
    hidden = jnp.tanh(dot(emb, w1_ref[...], NT) + b1_ref[...].astype(f32).reshape(1, mid))
    low = hidden.astype(bf16)
    h_ref[...] = hidden
    low_ref[...] = low
    kv_ref[:, pl.ds(0, cols)] = (dot(low, w2_ref[...]) + b2_ref[...].astype(f32).reshape(1, cols)).astype(bf16)
    if cols < kv_ref.shape[1]:
        kv_ref[:, pl.ds(cols, kv_ref.shape[1] - cols)] = jnp.zeros((PW, kv_ref.shape[1] - cols), bf16)


def prefix_forward(emb, weight1, bias1, weight2, bias2, room):
    mid, cols = weight2.shape
    args = (emb, weight1, bias1, weight2, bias2)
    outs = [((PW, mid), f32), ((PW, mid), bf16), ((PW, max(cols, room)), bf16)]
    return pl.pallas_call(
        prefix_kernel,
        grid=(1,),
        in_specs=[whole_spec(a.shape) for a in args],
        out_specs=[whole_spec(shape) for shape, _ in outs],
        out_shape=[jax.ShapeDtypeStruct(*a) for a in outs],
        compiler_params=params(16),
        cost_estimate=cost(0),
        name="prefix_forward",
    )(*args)


def add_pairs(refs):
    if len(refs) == 1:
        return refs[0][...]
    return (refs[0][...] + refs[1][...]) + (refs[2][...] + refs[3][...])


def real_rows(values, rows):
    return jnp.where(lax.broadcasted_iota(jnp.int32, values.shape, 0) < rows, values, 0.0)


def add_terms(terms):
    return (terms[0] + terms[1]) + (terms[2] + terms[3])


def second_layer_kernel(n, rows, *refs):
    parts, (low_ref, w_ref, wg_ref, bg_ref, hg_ref) = refs[:n], refs[n:]
    kv = real_rows(add_pairs(parts), rows).astype(bf16)
    bg_ref[...] = jnp.sum(kv.astype(f32), axis=0)
    wg_ref[...] = dot(low_ref[...], kv, TN)
    hg_ref[...] = dot(kv, w_ref[...], NT)


def second_layer_back(parts, rows, hidden_low, weight):
    mid, cols = weight.shape
    args = (*parts, hidden_low, weight)
    shapes = [(mid, cols), (cols,), (PW, mid)]
    return pl.pallas_call(
        functools.partial(second_layer_kernel, len(parts), rows),
        grid=(1,),
        in_specs=[whole_spec(a.shape) for a in args],
        out_specs=[whole_spec(a) for a in shapes],
        out_shape=[jax.ShapeDtypeStruct(a, f32) for a in shapes],
        compiler_params=params(20),
        cost_estimate=cost(3),
        name="second_layer_back",
    )(*args)


def first_layer_kernel(n, *refs):
    parts, (hidden_ref, e_ref, w_ref, wg_ref, bg_ref, eg_ref) = refs[:n], refs[n:]
    hidden = hidden_ref[...]
    low = real_rows(add_pairs(parts) * (1.0 - hidden * hidden), e_ref.shape[0]).astype(bf16)
    bg_ref[...] = jnp.sum(low.astype(f32), axis=0)
    rows, model = e_ref.shape
    emb = jnp.concatenate([e_ref[...].astype(f32), jnp.zeros((PW - rows, model), f32)], 0).astype(bf16)
    wg_ref[...] = dot(low, emb, TN)
    eg_ref[...] = dot(low, w_ref[...])[:rows]


def first_layer_back(parts, hidden, emb, weight):
    mid, model = weight.shape
    shapes = [(mid, model), (mid,), emb.shape]
    args = (*parts, hidden, emb, weight)
    return pl.pallas_call(
        functools.partial(first_layer_kernel, len(parts)),
        grid=(1,),
        in_specs=[whole_spec(a.shape) for a in args],
        out_specs=[whole_spec(a) for a in shapes],
        out_shape=[jax.ShapeDtypeStruct(a, f32) for a in shapes],
        compiler_params=params(24),
        cost_estimate=cost(4),
        name="first_layer_back",
    )(*args)


def after(value, *others):
    return lax.optimization_barrier((value, *others))[0]


def gather_lines(net, parts, planes, rows_out, rows_in, ties):
    cols = planes[0].shape[1]
    size = rows_out + net.planes * rows_in

    def kernel(*refs):
        ins, outs, sems = refs[: net.planes], refs[net.planes : -1], refs[-1]
        here = net.position()[0]
        for n, part in enumerate(parts):
            for k in range(net.planes):
                plane = here ^ k
                at = pl.multiple_of(rows_out + rows_in * plane, rows_in)
                pltpu.make_async_copy(
                    ins[k].at[pl.ds(rows_out + rows_in * part, rows_in)], outs[n].at[pl.ds(at, rows_in)], sems.at[n]
                ).start()

                @pl.when(plane == part)
                def _():
                    pltpu.make_async_copy(
                        ins[k].at[pl.ds(0, rows_out)], outs[n].at[pl.ds(0, rows_out)], sems.at[n]
                    ).start()

        for n in range(len(parts)):
            pltpu.make_async_copy(outs[n], outs[n], sems.at[n]).wait()

    shape = jax.ShapeDtypeStruct((size, cols), bf16)
    return pl.pallas_call(
        tied(kernel, len(ties)),
        grid=(1,),
        in_specs=tie_specs(ties) + [pl.BlockSpec(memory_space=pl.ANY)] * net.planes,
        out_specs=[whole_spec((size, cols))] * len(parts),
        out_shape=[shape] * len(parts),
        scratch_shapes=[pltpu.SemaphoreType.DMA((len(parts),))],
        compiler_params=params(ROOM),
        cost_estimate=cost(2),
        name="gather_lines",
    )(*ties, *planes)


class Plain:
    def position(self):
        return ()

    def gather(self, shard):
        whole = lax.all_gather(shard, ALL, axis=0, tiled=True)
        rows, cols = whole.shape
        return Weight(self, [whole], rows, [(0, 0, lambda: 0)], rows, cols)

    def sum_columns(self, both):
        part = jnp.concatenate([both[0], both[1]], 1)
        return [lax.psum_scatter(lax.psum(part, "rows"), "pre", scatter_dimension=1, tiled=True)]

    def over_pre(self, part):
        return [lax.psum(part, "pre")]


class Grid:
    planes = 4

    def __init__(self):
        self.places = [(z, x, y, c) for z in range(4) for x in range(2) for y in range(2) for c in range(2)]

    def position(self):
        rows, pre = lax.axis_index("rows"), lax.axis_index("pre")
        return rows // 2, rows % 2, pre // 2, pre % 2

    @staticmethod
    def number(z, x, y, c):
        return z * 8 + x * 4 + y * 2 + c

    @staticmethod
    def side(x, y, c, second):
        along_x = (c + second + 1) % 2
        return (x + along_x) % 2, (y + 1 - along_x) % 2

    def send(self, value, where):
        return lax.ppermute(value, ALL, [(self.number(*p), self.number(*where(*p))) for p in self.places])

    def plane(self, block, k):
        return self.send(block, lambda z, x, y, c: (z ^ k, x, y, c))

    def planes_of(self, block):
        return [self.plane(block, k) for k in range(1, self.planes)]

    def planes_by_relay(self, block):
        two = self.plane(block, 2)
        return [block, self.plane(block, 1), two, self.plane(two, 1)]

    def beside(self, value, second):
        return self.send(value, lambda z, x, y, c: (z, *self.side(x, y, c, second), c))

    def across(self, value):
        return self.send(value, lambda z, x, y, c: (z, 1 - x, 1 - y, c))

    def core(self, value):
        return self.send(value, lambda z, x, y, c: (z, x, y, 1 - c))

    def source(self, array, x, y, c):
        if array >= 4:
            c = 1 - c
        if array % 4 >= 2:
            x, y = self.side(x, y, c, 1)
        if array % 2:
            x, y = self.side(x, y, c, 0)
        return x, y, c

    def arrays_of(self, line, near, far, end):
        own = [line, near, far, end]
        return own + [self.core(a) for a in own]

    def weight(self, arrays, rows, cols, at=0):
        def place(array, k):
            return lambda z, x, y, c: rows * self.number(z ^ k, *self.source(array, x, y, c))

        pieces = [(a, k * rows, place(a, k)) for a in range(8) for k in range(4)]
        return Weight(self, arrays, rows, pieces, rows * len(self.places), cols, at)

    def hidden_weights(self, arrays, rows_in, rows_out):
        devices, cols = len(self.places), arrays[0].shape[1]

        def inner(array, k):
            return lambda z, x, y, c: rows_in * self.number(k, *self.source(array, x, y, c))

        def outer(array):
            return lambda z, x, y, c: rows_out * self.number(0, *self.source(array, x, y, c))

        return (
            Weight(
                self,
                arrays,
                rows_in,
                [(a, rows_out + rows_in * k, inner(a, k)) for a in range(8) for k in range(4)],
                rows_in * devices,
                cols,
            ),
            Weight(self, arrays, rows_out, [(a, 0, outer(a)) for a in range(8)], rows_out * devices // 4, cols),
        )

    def sum_cores(self, both):
        _, _, y, c = self.position()
        both = both + self.core(both)
        cols = both.shape[2] // 2
        both = jnp.where(c == 0, both[:, :, :cols], both[:, :, cols:])
        return jnp.where(y == 0, both[0], both[1]), jnp.where(y == 0, both[1], both[0])

    def send_across(self, mine, other):
        along_x = self.send(mine, lambda z, x, y, c: (z, 1 - x, y, c))
        along_y = self.send(other, lambda z, x, y, c: (z, x, 1 - y, c))
        across = self.send(other, lambda z, x, y, c: (z, 1 - x, 1 - y, c))
        return [mine, along_x, along_y, across]

    def over_pre(self, part):
        along = self.send(part, lambda z, x, y, c: (z, x, 1 - y, c))
        across = self.send(part, lambda z, x, y, c: (z, x, 1 - y, 1 - c))
        return [part, self.core(part), along, across]


def per_device(
    tokens,
    seg_ids,
    valid,
    out_grad,
    ln1_gain,
    ln1_bias,
    qkv_weight,
    qkv_bias,
    proj_weight,
    proj_bias,
    ln2_gain,
    ln2_bias,
    fc_weight,
    fc_bias,
    out_weight,
    out_bias,
    prefix_emb,
    rep_weight1,
    rep_bias1,
    rep_weight2,
    rep_bias2,
):
    x, og = tokens[0], out_grad[0]
    model = x.shape[1]
    hidden_units = fc_weight.shape[1]
    prefix_len = prefix_emb.shape[0]
    own_q, own_o = qkv_weight.shape[0], out_weight.shape[0]
    width = hidden_units // CHUNKS
    part = model // GROUPS
    on_grid = (lax.axis_size("rows"), lax.axis_size("pre")) == (8, 4)
    net = Grid() if on_grid else Plain()

    def step_starts(g):
        return [i * model + g * part + k * LANES for k in range(GROUP_STEPS) for i in range(3)]

    def by_step(g):
        return [(0, k * LANES, 0, 0, at, own_q, LANES) for k, at in enumerate(step_starts(g))]

    second = by_step(1) + [(0, 3 * part, 1, 0, 0, own_q, model)]
    (shard,) = arrange(
        [((own_q, 6 * part + model), by_step(0) + [(0, 3 * part + at, *rest) for _, at, *rest in second])],
        qkv_weight,
        proj_weight,
    )
    if on_grid:
        others = net.planes_of(shard)
    starts = [at for g in range(GROUPS) for at in step_starts(g)]
    one = [(0, 0, model)]
    vecs = pack(
        [(GAIN1, one), (SHIFT1, one), (GAIN2, one), (SHIFT2, one), (PROJ_SHIFT, one), (OUT_SHIFT, one)]
        + [(QKV_SHIFT, [(k * LANES, at, LANES) for k, at in enumerate(starts)]), (FC_SHIFT, [(0, 0, hidden_units)])],
        hidden_units,
        ln1_gain,
        ln1_bias,
        ln2_gain,
        ln2_bias,
        proj_bias,
        out_bias,
        qkv_bias,
        fc_bias,
    )
    hidden, hidden_low, kv_local = prefix_forward(
        prefix_emb, rep_weight1.T, rep_bias1, rep_weight2, rep_bias2, 3 * part if on_grid else 0
    )

    def run_hidden(j, so_far, normed2, w_in, w_out, ties=()):
        back = (mixes, pprobs, qkvs, prefix_kv)
        w_last = w_proj if j == CHUNKS - 1 else None
        return hidden_part(j, normed2, og, vecs, mid, so_far, w_in, w_out, w_last, back, ties)

    so_far = None
    if not on_grid:
        prefix_kv = lax.all_gather(kv_local, "pre", axis=1, tiled=True)
        w_qkv = [net.gather(shard[:, g * 3 * part : (g + 1) * 3 * part]) for g in range(GROUPS)]
        w_proj = net.gather(proj_weight)
        out_all = lax.all_gather(out_weight, ALL, axis=0, tiled=True)
        normed1, bias = first_norm(x, vecs), mask_bias(seg_ids, valid, prefix_len)
        qkvs, mixes, probs, pprobs = zip(
            *[attend(g, normed1, w_qkv[g], vecs, prefix_kv, bias) for g in range(GROUPS)], strict=True
        )
        mid, normed2 = middle_block(mixes, x, w_proj, vecs)
        for j in range(CHUNKS):
            w_in = net.gather(fc_weight[:, j * width : (j + 1) * width])
            w_out = Weight(net, [out_all], width, [(0, j * width, lambda: 0)], width, model)
            so_far = run_hidden(j, so_far, normed2, w_in, w_out)
    else:
        def send_lines(parts, ties):
            return gather_lines(net, parts, planes_h, own_o, own_q, ties)

        rows, wide = net.planes * own_q, 3 * part + model
        normed1, bias = first_norm(x, vecs), mask_bias(seg_ids, valid, prefix_len)
        (line_a,) = arrange(
            [
                (
                    (rows + PW, 3 * part),
                    [(k * own_q, 0, k, 0, 0, own_q, 3 * part) for k in range(net.planes)]
                    + [(rows, 0, net.planes, 0, 0, PW, 3 * part)],
                ),
            ],
            shard,
            *others,
            kv_local,
            ties=(normed1, bias),
        )
        (shard_h,) = arrange(
            [
                (
                    (own_o + CHUNKS * own_q, model),
                    [(0, 0, 0, 0, 0, own_o, model)]
                    + [(own_o + j * own_q, 0, 1, 0, j * width, own_q, width) for j in range(CHUNKS)],
                )
            ],
            out_weight,
            fc_weight,
            ties=(line_a,),
        )
        planes_h = net.planes_by_relay(shard_h)
        near_a, far_a = net.beside(line_a, False), net.beside(line_a, True)
        end_a = net.across(line_a)
        (line_b,) = arrange(
            [((rows, wide), [(k * own_q, 0, k, 0, 3 * part, own_q, wide) for k in range(net.planes)])],
            shard,
            *others,
            ties=(shard_h,),
        )
        near_b, far_b = net.beside(line_b, False), net.beside(line_b, True)
        end_b = net.beside(near_b, True)
        w_a = net.weight(net.arrays_of(line_a, near_a, far_a, end_a), own_q, 3 * part)
        qkv_a, mix_a, probs_a, pprobs_a, prefix_kv = attend(0, normed1, w_a, vecs, None, bias, (near_b, planes_h[1], planes_h[2]))
        far_b, end_b = gate((far_b, end_b), (mix_a,))
        lines = list(send_lines((0, 1), (far_b, end_b)))
        arrays_b = net.arrays_of(line_b, near_b, far_b, end_b)
        w_b, w_proj = net.weight(arrays_b, own_q, 3 * part), net.weight(arrays_b, own_q, model, 3 * part)
        nears = [net.beside(a, False) for a in lines]
        fars = [net.beside(a, True) for a in lines]
        qkv_b, mix_b, probs_b, pprobs_b = attend(1, normed1, w_b, vecs, prefix_kv, bias, tuple(lines))
        ends = [net.beside(after(a, mix_b), True) for a in nears]
        mid, normed2 = middle_block([mix_a, mix_b], x, w_proj, vecs, tuple(nears))
        lines += send_lines((2, 3), (mid, ends[0]))
        nears += [net.beside(a, False) for a in lines[2:]]
        fars += [net.beside(a, True) for a in lines[2:]]
        w_qkv, qkvs, probs = [w_a, w_b], [qkv_a, qkv_b], [probs_a, probs_b]
        mixes, pprobs = [mix_a, mix_b], [pprobs_a, pprobs_b]
        latest = mid
        for j in range(CHUNKS):
            arrays = net.arrays_of(lines[j], nears[j], after(fars[j], latest), after(ends[j], latest))
            w_in, w_out = net.hidden_weights(arrays, own_q, own_o)
            ties = tuple(lines[2:]) if j == 0 else ()
            if 0 < j < CHUNKS - 1:
                ends.append(net.beside(after(nears[j + 1], latest), True))
                ties = (nears[j + 1],)
            so_far = run_hidden(j, so_far, normed2, w_in, w_out, ties)
            latest = so_far[0]
    output, grad_mid, grad_attn, prefix_grad = so_far
    rest = (x, grad_mid, vecs)
    if on_grid:
        mine, other = net.sum_cores(prefix_grad)
        terms = net.send_across(mine, other)
        so_far = attend_back(0, qkvs[0], probs[0], prefix_kv, grad_attn, None, w_qkv[0], ties=(mine, other))
        plane = add_terms(terms)
        sums = [plane, *net.planes_of(plane)]
        in_grad = attend_back(1, qkvs[1], probs[1], prefix_kv, grad_attn, so_far, w_qkv[1], rest, ties=(plane,))
    else:
        sums = net.sum_columns(prefix_grad)
        so_far = attend_back(0, qkvs[0], probs[0], prefix_kv, grad_attn, None, w_qkv[0])
        in_grad = attend_back(1, qkvs[1], probs[1], prefix_kv, grad_attn, so_far, w_qkv[1], rest)
    weight2_grad, bias2_grad, hid_grad = second_layer_back(sums, prefix_len, hidden_low, rep_weight2)
    hid_grads = net.over_pre(hid_grad)
    weight1_grad, bias1_grad, emb_grad = first_layer_back(hid_grads, hidden, prefix_emb, rep_weight1.T)
    return output[None], in_grad[None], emb_grad, weight1_grad.T, bias1_grad, weight2_grad, bias2_grad


def solution(mesh):
    split_all = P(ALL, None)
    whole = P()
    return jax.shard_map(
        per_device,
        mesh=mesh,
        in_specs=(
            P(ALL, None, None),
            split_all,
            split_all,
            P(ALL, None, None),
            whole,
            whole,
            split_all,
            whole,
            split_all,
            whole,
            whole,
            whole,
            split_all,
            whole,
            split_all,
            whole,
            whole,
            whole,
            whole,
            P(None, "pre"),
            P("pre"),
        ),
        out_specs=(
            P(ALL, None, None),
            P(ALL, None, None),
            whole,
            whole,
            whole,
            P(None, "pre"),
            P("pre"),
        ),
        check_vma=False,
    )
```
